32 devices in a mesh: batch: 4 (over z), tm: 8 (over y, x, core).
Axes of the slice: x: 2, y: 2, z: 4, core: 2. Of those that a mesh axis runs over, the one named last changes fastest.
Arguments:
- x_small: bfloat16 [32, 8, 49, 512], P('batch', 'tm'), may hold values from -6 to 6
- x_large: bfloat16 [32, 8, 100, 512], P('batch', 'tm'), may hold values from -6 to 6
- small_output_gradient: bfloat16 [32, 8, 49, 512], P('batch', 'tm'), may hold values from -6 to 6
- large_output_gradient: bfloat16 [32, 8, 100, 512], P('batch', 'tm'), may hold values from -6 to 6
- clip_counts: int32 [2, 4], replicated, may hold values from 1 to 8, as said below
- first_spatial: float32 [4608, 1152], P('tm', 'batch'), may hold values from -0.09375 to 0.09375
- first_temporal: float32 [3456, 512], P('tm', 'batch'), may hold values from -0.109375 to 0.109375
- second_spatial: float32 [4608, 1152], P('tm', 'batch'), may hold values from -0.09375 to 0.09375
- second_temporal: float32 [3456, 512], P('tm', 'batch'), may hold values from -0.109375 to 0.109375
- norm_params: float32 [2, 3328], replicated, may hold values from -0.5 to 1.4, as said below
- first_spatial_momentum: float32 [4608, 1152], P('tm', 'batch'), may hold values from -0.0004272461 to 0.0004272461
- first_temporal_momentum: float32 [3456, 512], P('tm', 'batch'), may hold values from -0.0004272461 to 0.0004272461
- second_spatial_momentum: float32 [4608, 1152], P('tm', 'batch'), may hold values from -0.0004272461 to 0.0004272461
- second_temporal_momentum: float32 [3456, 512], P('tm', 'batch'), may hold values from -0.0004272461 to 0.0004272461
- norm_momentum: float32 [2, 3328], replicated, may hold values from -0.0012207031 to 0.0012207031
- first_spatial_variance: float32 [4608, 1152], P('tm', 'batch'), may hold values from 7.0609345e-11 to 2.8243738e-10
- first_temporal_variance: float32 [3456, 512], P('tm', 'batch'), may hold values from 7.0609345e-11 to 2.8243738e-10
- second_spatial_variance: float32 [4608, 1152], P('tm', 'batch'), may hold values from 7.0609345e-11 to 2.8243738e-10
- second_temporal_variance: float32 [3456, 512], P('tm', 'batch'), may hold values from 7.0609345e-11 to 2.8243738e-10
- norm_variance: float32 [2, 3328], replicated, may hold values from 8.473121e-11 to 3.3892483e-10
Outputs:
- output_small: float32 [32, 8, 49, 512], P('batch', 'tm')
- output_large: float32 [32, 8, 100, 512], P('batch', 'tm')
- input_grad_small: float32 [32, 8, 49, 512], P('batch', 'tm')
- input_grad_large: float32 [32, 8, 100, 512], P('batch', 'tm')
- grad_norm: float32 [], replicated
- updated_first_spatial: float32 [4608, 1152], P('tm', 'batch')
- momentum_first_spatial: float32 [4608, 1152], P('tm', 'batch')
- variance_first_spatial: float32 [4608, 1152], P('tm', 'batch')
- updated_first_temporal: float32 [3456, 512], P('tm', 'batch')
- momentum_first_temporal: float32 [3456, 512], P('tm', 'batch')
- variance_first_temporal: float32 [3456, 512], P('tm', 'batch')
- updated_second_spatial: float32 [4608, 1152], P('tm', 'batch')
- momentum_second_spatial: float32 [4608, 1152], P('tm', 'batch')
- variance_second_spatial: float32 [4608, 1152], P('tm', 'batch')
- updated_second_temporal: float32 [3456, 512], P('tm', 'batch')
- momentum_second_temporal: float32 [3456, 512], P('tm', 'batch')
- variance_second_temporal: float32 [3456, 512], P('tm', 'batch')
- updated_norms: float32 [2, 3328], replicated
- momentum_norms: float32 [2, 3328], replicated
- variance_norms: float32 [2, 3328], replicated
The draws below stay inside these ranges and needn't reach their ends.
Inputs may be any that keep to these rules, and one draw needn't show every extreme that they name: `clip_counts`: the live clips of a group on a batch index are its first slots; in each group some batch index has all 8 live. `norm_params`: gains lie in 0.6 to 1.4, biases in -0.5 to 0.5.
All inputs are finite; a program needn't handle non-finite values.
Results may differ from the reference program's by a relative error of at most 0.02.
Values may be sent and summed in bfloat16 or wider, within the bound.
A program may use at most 320 MiB of HBM per device.

```python
import math
import jax
import jax.numpy as jnp
from jax import lax

D = 512
MID = 1152
HS = 7
HL = 10
CL_DEV = 8
STEP = 10
CLIPS = 32
FRAMES = 8
NORM_WIDTH = 3328
PARAMS = 14162432
N_BATCH = 4


def draw_clip_counts(key, part):
    key = jax.random.fold_in(key, 5)
    base = jax.random.randint(key, (2, N_BATCH), 1, CL_DEV + 1)
    place = jax.random.randint(jax.random.fold_in(key, 1), (2, 1), 0, N_BATCH)
    filled = jnp.arange(N_BATCH)[None, :] == place
    return jnp.where(filled, CL_DEV, base).astype(jnp.int32)


def draw_norm_params(key, part):
    key = jax.random.fold_in(key, 7)
    gain_vectors = jax.random.uniform(key, (1, NORM_WIDTH), jnp.float32, 0.6, 1.4)
    bias_vectors = jax.random.uniform(jax.random.fold_in(key, 1), (1, NORM_WIDTH), jnp.float32, -0.5, 0.5)
    return jnp.concatenate([gain_vectors, bias_vectors], axis=0)


def levels(rng, dims, split, least, largest):
    level = 1.0
    for axis_at, blocks in split:
        draws = jax.random.uniform(jax.random.fold_in(jax.random.fold_in(rng, 6), axis_at), (blocks,), jnp.float32, least / len(split), largest / len(split))
        level = level * jnp.repeat(jnp.exp(draws), dims[axis_at] // blocks).reshape((-1,) + (1,) * (len(dims) - 1 - axis_at))
    return level


def noise(key, dims, deviation, reach, cuts=(), kind=jnp.bfloat16):
    factor_of = levels(key, dims, cuts, -0.22, 0.18) if cuts else 1.0
    array = jax.random.normal(key, dims, jnp.float32) * deviation * factor_of
    return jnp.minimum(jnp.maximum(array, -reach), reach).astype(kind)


def setup_inputs(seed: int = 0) -> dict:
    key_of = jax.random.split(jax.random.key(seed), 21)
    x_small = noise(key_of[0], (CLIPS, FRAMES, HS * HS, D), 1.0, 6.0, ((0, 4), (1, 8)))
    x_large = noise(key_of[1], (CLIPS, FRAMES, HL * HL, D), 1.0, 6.0, ((0, 4), (1, 8)))
    small_output_gradient = noise(key_of[2], (CLIPS, FRAMES, HS * HS, D), 1.0, 6.0, ((0, 4), (1, 8)))
    large_output_gradient = noise(key_of[3], (CLIPS, FRAMES, HL * HL, D), 1.0, 6.0, ((0, 4), (1, 8)))
    clip_counts = draw_clip_counts(jax.random.fold_in(key_of[20], 71), 0)
    first_spatial = noise(key_of[5], (9 * D, MID), (9 * D) ** -0.5, 0.09375, ((0, 8), (1, 4)), jnp.float32)
    first_temporal = noise(key_of[6], (3 * MID, D), (3 * MID) ** -0.5, 0.109375, ((0, 8), (1, 4)), jnp.float32)
    second_spatial = noise(key_of[7], (9 * D, MID), (9 * D) ** -0.5, 0.09375, ((0, 8), (1, 4)), jnp.float32)
    second_temporal = noise(key_of[8], (3 * MID, D), (3 * MID) ** -0.5, 0.109375, ((0, 8), (1, 4)), jnp.float32)
    norm_params = draw_norm_params(jax.random.fold_in(key_of[20], 71), 0)
    first_spatial_momentum = noise(key_of[10], (9 * D, MID), (0.11 / PARAMS ** 0.5), 0.0004272461, ((0, 8), (1, 4)), jnp.float32)
    first_temporal_momentum = noise(key_of[11], (3 * MID, D), (0.11 / PARAMS ** 0.5), 0.0004272461, ((0, 8), (1, 4)), jnp.float32)
    second_spatial_momentum = noise(key_of[12], (9 * D, MID), (0.11 / PARAMS ** 0.5), 0.0004272461, ((0, 8), (1, 4)), jnp.float32)
    second_temporal_momentum = noise(key_of[13], (3 * MID, D), (0.11 / PARAMS ** 0.5), 0.0004272461, ((0, 8), (1, 4)), jnp.float32)
    norm_momentum = noise(key_of[14], (2, NORM_WIDTH), (0.33 / PARAMS ** 0.5), 0.0012207031, (), jnp.float32)
    first_spatial_variance = jnp.clip(jnp.exp(math.log(2.8243737903999033e-10) - 1.3862944 * jax.random.uniform(key_of[15], (9 * D, MID), jnp.float32) ** levels(key_of[15], (9 * D, MID), ((0, 8), (1, 4)), -0.2, 0.2)), 7.060934475999758e-11, 2.8243737903999033e-10)
    first_temporal_variance = jnp.clip(jnp.exp(math.log(2.8243737903999033e-10) - 1.3862944 * jax.random.uniform(key_of[16], (3 * MID, D), jnp.float32) ** levels(key_of[16], (3 * MID, D), ((0, 8), (1, 4)), -0.2, 0.2)), 7.060934475999758e-11, 2.8243737903999033e-10)
    second_spatial_variance = jnp.clip(jnp.exp(math.log(2.8243737903999033e-10) - 1.3862944 * jax.random.uniform(key_of[17], (9 * D, MID), jnp.float32) ** levels(key_of[17], (9 * D, MID), ((0, 8), (1, 4)), -0.2, 0.2)), 7.060934475999758e-11, 2.8243737903999033e-10)
    second_temporal_variance = jnp.clip(jnp.exp(math.log(2.8243737903999033e-10) - 1.3862944 * jax.random.uniform(key_of[18], (3 * MID, D), jnp.float32) ** levels(key_of[18], (3 * MID, D), ((0, 8), (1, 4)), -0.2, 0.2)), 7.060934475999758e-11, 2.8243737903999033e-10)
    norm_variance = jnp.clip(jnp.exp(jax.random.uniform(key_of[19], (2, NORM_WIDTH), jnp.float32, math.log(8.473120816088198e-11), math.log(3.389248326435279e-10))), 8.473120816088198e-11, 3.389248326435279e-10)
    return {"x_small": x_small, "x_large": x_large, "small_output_gradient": small_output_gradient, "large_output_gradient": large_output_gradient, "clip_counts": clip_counts, "first_spatial": first_spatial, "first_temporal": first_temporal, "second_spatial": second_spatial, "second_temporal": second_temporal, "norm_params": norm_params, "first_spatial_momentum": first_spatial_momentum, "first_temporal_momentum": first_temporal_momentum, "second_spatial_momentum": second_spatial_momentum, "second_temporal_momentum": second_temporal_momentum, "norm_momentum": norm_momentum, "first_spatial_variance": first_spatial_variance, "first_temporal_variance": first_temporal_variance, "second_spatial_variance": second_spatial_variance, "second_temporal_variance": second_temporal_variance, "norm_variance": norm_variance}


@jax.custom_vjp
def low(v):
    return lax.optimization_barrier(v.astype(jnp.bfloat16)).astype(jnp.float32)

@jax.custom_vjp
def low_back(v):
    return v

def low_keep(v):
    return (low(v), None)

def low_pass(kept, grad):
    return (grad,)

def back_keep(v):
    return (v, None)

def back_low(kept, grad):
    return (low(grad),)
low.defvjp(low_keep, low_pass)
low_back.defvjp(back_keep, back_low)
HIGH = lax.Precision.HIGHEST
NORM_EPS = 1e-05
THRESHOLD = 1.0
BETA_ONE = 0.9
BETA_TWO = 0.999
WEIGHT_RATE = 0.03
NORM_RATE = 0.25
WEIGHT_DECAY = 0.05
ADAM_EPS = 1e-08

def spatial(field, weight, side):
    clips, frames, cells, channels = field.shape
    grid = field.reshape(clips, frames, side, side, channels)
    padded = jnp.pad(grid, ((0, 0), (0, 0), (1, 1), (1, 1), (0, 0)))
    pieces = [padded[:, :, row:row + side, column:column + side, :] for row in range(3) for column in range(3)]
    stacked = jnp.concatenate(pieces, axis=-1).reshape(clips * frames * cells, 9 * channels)
    return jnp.dot(stacked, weight, precision=HIGH).reshape(clips, frames, cells, weight.shape[1])

def temporal(field, weight):
    clips, frames, cells, channels = field.shape
    padded = jnp.pad(field, ((0, 0), (1, 1), (0, 0), (0, 0)))
    pieces = [padded[:, shift:shift + frames] for shift in range(3)]
    stacked = jnp.concatenate(pieces, axis=-1).reshape(clips * frames * cells, 3 * channels)
    return jnp.dot(stacked, weight, precision=HIGH).reshape(clips, frames, cells, weight.shape[1])

def batch_norm(input_value, live, total, norm_gain_vector, norm_shift_bias):
    mean = lax.optimization_barrier(jnp.sum(live * input_value, axis=(0, 1, 2))) / total
    square = lax.optimization_barrier(jnp.sum(live * input_value * input_value, axis=(0, 1, 2))) / total
    scale = lax.rsqrt(square - mean * mean + NORM_EPS)
    return (input_value - mean) * scale * norm_gain_vector + norm_shift_bias

def forward(x_small, x_large, first_spatial, first_temporal, second_spatial, second_temporal, norm_params, lives, grand_totals):
    bounds = (0, MID, MID + D, 2 * MID + D, 2 * MID + 2 * D)
    gain_vectors = [norm_params[0, bounds[index]:bounds[index + 1]] for index in range(4)]
    bias_vectors = [norm_params[1, bounds[index]:bounds[index + 1]] for index in range(4)]
    inputs = (x_small, x_large)
    sides = (HS, HL)
    split_point = HS * HS
    spatial_one = low(first_spatial)
    temporal_one = low(first_temporal)
    spatial_two = low(second_spatial)
    temporal_two = low(second_temporal)
    first_act = [low(jax.nn.silu(batch_norm(low_back(spatial(inputs[group], spatial_one, sides[group])), lives[group], grand_totals[group], gain_vectors[0], bias_vectors[0]))) for group in range(2)]
    mixed = low_back(temporal(jnp.concatenate(first_act, axis=2), temporal_one))
    parts = (mixed[:, :, :split_point], mixed[:, :, split_point:])
    second_act = [low(jax.nn.silu(batch_norm(parts[group], lives[group], grand_totals[group], gain_vectors[1], bias_vectors[1]))) for group in range(2)]
    third_act = [low(jax.nn.silu(batch_norm(low_back(spatial(second_act[group], spatial_two, sides[group])), lives[group], grand_totals[group], gain_vectors[2], bias_vectors[2]))) for group in range(2)]
    mixed = low_back(temporal(jnp.concatenate(third_act, axis=2), temporal_two))
    parts = (mixed[:, :, :split_point], mixed[:, :, split_point:])
    outputs = [lives[group] * jax.nn.silu(batch_norm(parts[group], lives[group], grand_totals[group], gain_vectors[3], bias_vectors[3]) + inputs[group]) for group in range(2)]
    return (outputs[0], outputs[1])

def adamw(weight, gradient, momentum, variance, factor, rate, decay):
    clipped = gradient * factor
    new_momentum = BETA_ONE * momentum + (1.0 - BETA_ONE) * clipped
    new_variance = BETA_TWO * variance + (1.0 - BETA_TWO) * clipped * clipped
    corrected = new_momentum / (1.0 - BETA_ONE ** STEP)
    spread = jnp.sqrt(new_variance / (1.0 - BETA_TWO ** STEP))
    new_weight = weight - rate * (corrected / (spread + ADAM_EPS) + decay * weight)
    return (new_weight, new_momentum, new_variance)

def reference(x_small, x_large, small_output_gradient, large_output_gradient, clip_counts, first_spatial, first_temporal, second_spatial, second_temporal, norm_params, first_spatial_momentum, first_temporal_momentum, second_spatial_momentum, second_temporal_momentum, norm_momentum, first_spatial_variance, first_temporal_variance, second_spatial_variance, second_temporal_variance, norm_variance):
    slots = jnp.arange(CLIPS, dtype=jnp.int32)
    owners = slots // CL_DEV
    places = slots % CL_DEV
    lives = [(places < clip_counts[group][owners]).astype(jnp.float32).reshape(CLIPS, 1, 1, 1) for group in range(2)]
    cell_counts = (HS * HS, HL * HL)
    grand_totals = [jnp.sum(clip_counts[group]).astype(jnp.float32) * FRAMES * cell_counts[group] for group in range(2)]

    def wrapped(small, large, spatial_one, temporal_one, spatial_two, temporal_two, params):
        return forward(small, large, spatial_one, temporal_one, spatial_two, temporal_two, params, lives, grand_totals)
    outputs, pullback = jax.vjp(wrapped, x_small.astype(jnp.float32), x_large.astype(jnp.float32), first_spatial, first_temporal, second_spatial, second_temporal, norm_params)
    grads = pullback((small_output_gradient.astype(jnp.float32), large_output_gradient.astype(jnp.float32)))
    input_small, input_large, grad_one, grad_two, grad_three, grad_four, grad_params = grads
    total_square = jnp.sum(grad_one * grad_one) + jnp.sum(grad_two * grad_two) + jnp.sum(grad_three * grad_three) + jnp.sum(grad_four * grad_four) + jnp.sum(grad_params * grad_params)
    grad_norm = jnp.sqrt(total_square)
    factor = THRESHOLD / jnp.maximum(grad_norm, THRESHOLD)
    one = adamw(first_spatial, grad_one, first_spatial_momentum, first_spatial_variance, factor, WEIGHT_RATE, WEIGHT_DECAY)
    two = adamw(first_temporal, grad_two, first_temporal_momentum, first_temporal_variance, factor, WEIGHT_RATE, WEIGHT_DECAY)
    three = adamw(second_spatial, grad_three, second_spatial_momentum, second_spatial_variance, factor, WEIGHT_RATE, WEIGHT_DECAY)
    four = adamw(second_temporal, grad_four, second_temporal_momentum, second_temporal_variance, factor, WEIGHT_RATE, WEIGHT_DECAY)
    norms = adamw(norm_params, grad_params, norm_momentum, norm_variance, factor, NORM_RATE, 0.0)
    return (outputs[0], outputs[1], input_small, input_large, grad_norm, one[0], one[1], one[2], two[0], two[1], two[2], three[0], three[1], three[2], four[0], four[1], four[2], norms[0], norms[1], norms[2])
```

```python
import functools
import math

import jax
import jax.numpy as jnp
from jax import lax
from jax.experimental import pallas as pl
from jax.experimental.pallas import tpu as pltpu
from jax.sharding import PartitionSpec as P

D = 512
MID = 1152
HS = 7
HL = 10
STEP = 10


NORM_EPS = 1e-05
THRESHOLD = 1.0
BETA_ONE = 0.9
BETA_TWO = 0.999
WEIGHT_RATE = 0.03
NORM_RATE = 0.25
WEIGHT_DECAY = 0.05
ADAM_EPS = 1e-08


def padded_2(value, sides, width):
    for axis, dim in sides:
        size, length = (lax.axis_size(axis), value.shape[dim])
        up = [(i, (i + 1) % size) for i in range(size - 1)]
        down = [(j, i) for i, j in up]
        last = lax.slice_in_dim(value, length - width, length, axis=dim)
        first = lax.slice_in_dim(value, 0, width, axis=dim)
        before = lax.ppermute(last, axis, up)
        after = lax.ppermute(first, axis, down)
        value = jnp.concatenate([before, value, after], axis=dim)
    return value


def silu_slope(input_value):
    sigmoid_value = jax.nn.sigmoid(input_value)
    return sigmoid_value * (1.0 + input_value * (1.0 - sigmoid_value))


def spatial_taps(field, side):
    clips, frames, cells, channels = field.shape
    grid = field.reshape(clips, frames, side, side, channels)
    padded = jnp.pad(grid, ((0, 0), (0, 0), (1, 1), (1, 1), (0, 0)))
    pieces = [
        padded[:, :, row : row + side, column : column + side, :]
        for row in range(3)
        for column in range(3)
    ]
    return jnp.concatenate(pieces, axis=-1).reshape(clips * frames * cells, 9 * channels)


def spatial_forward(field_small, field_large, weight):
    taps_small = spatial_taps(field_small, HS)
    taps_large = spatial_taps(field_large, HL)
    result_small = jnp.dot(taps_small, weight, preferred_element_type=jnp.float32).reshape(
        field_small.shape[:3] + (weight.shape[1],)
    )
    result_large = jnp.dot(taps_large, weight, preferred_element_type=jnp.float32).reshape(
        field_large.shape[:3] + (weight.shape[1],)
    )
    return (jnp.concatenate([result_small, result_large], axis=2), taps_small, taps_large)


def spatial_backward(upstream_rows, weight, shape, side):
    clips, frames, cells, channels = shape
    columns = lax.dot_general(
        upstream_rows, weight, (((1,), (1,)), ((), ())), preferred_element_type=jnp.float32
    )
    columns = columns.reshape(clips, frames, side, side, 9 * channels)
    padded = jnp.pad(columns, ((0, 0), (0, 0), (1, 1), (1, 1), (0, 0)))
    final_result = None
    for row in range(3):
        for column in range(3):
            offset = (3 * row + column) * channels
            window = padded[
                :,
                :,
                2 - row : 2 - row + side,
                2 - column : 2 - column + side,
                offset : offset + channels,
            ]
            final_result = window if final_result is None else final_result + window
    return final_result.reshape(clips, frames, cells, channels)


def temporal_forward(field, weight):
    padded = padded_2(field, (("tm", 1),), 1)
    frames = field.shape[1]
    pieces = jnp.concatenate([padded[:, shift : shift + frames] for shift in range(3)], axis=-1)
    rows = pieces.reshape(-1, pieces.shape[-1])
    final_result = jnp.dot(rows, weight, preferred_element_type=jnp.float32).reshape(
        field.shape[:3] + (weight.shape[1],)
    )
    return (final_result, rows)


def temporal_backward(upstream_gradient, weight):
    padded = padded_2(upstream_gradient, (("tm", 1),), 1)
    frames = upstream_gradient.shape[1]
    pieces = jnp.concatenate(
        [padded[:, 2 - shift : 2 - shift + frames] for shift in range(3)], axis=-1
    )
    rows = pieces.reshape(-1, pieces.shape[-1])
    kernel = (
        weight.reshape(3, -1, weight.shape[1]).transpose(1, 0, 2).reshape(-1, 3 * weight.shape[1])
    )
    final_result = lax.dot_general(
        rows, kernel, (((1,), (1,)), ((), ())), preferred_element_type=jnp.float32
    )
    return final_result.reshape(upstream_gradient.shape[:3] + (kernel.shape[0],))


def group_totals(leading_part, trailing_part, active_flags, split_point):
    leading_cells = jnp.sum(active_flags * leading_part, axis=(0, 1))
    trailing_cells = jnp.sum(active_flags * trailing_part, axis=(0, 1))
    first_groups = jnp.stack(
        [jnp.sum(leading_cells[:split_point], axis=0), jnp.sum(leading_cells[split_point:], axis=0)]
    )
    second_groups = jnp.stack(
        [
            jnp.sum(trailing_cells[:split_point], axis=0),
            jnp.sum(trailing_cells[split_point:], axis=0),
        ]
    )
    return (first_groups, second_groups)


def per_cell(stat, split_point, cells):
    channels = stat.shape[1]
    return jnp.concatenate(
        [
            jnp.broadcast_to(stat[0], (split_point, channels)),
            jnp.broadcast_to(stat[1], (cells - split_point, channels)),
        ],
        axis=0,
    )


def norm_forward_pass(
    input_value, active_flags, split_point, grand_totals, norm_gain_vector, norm_shift_bias
):
    running_sums, squared_values = group_totals(
        input_value, input_value * input_value, active_flags, split_point
    )
    running_sums, squared_values = lax.psum((running_sums, squared_values), ("batch", "tm"))
    mean = running_sums / grand_totals[:, None]
    scale = lax.rsqrt(squared_values / grand_totals[:, None] - mean * mean + NORM_EPS)
    cells = input_value.shape[2]
    cell_scale = per_cell(scale, split_point, cells)
    normalized_values = (input_value - per_cell(mean, split_point, cells)) * cell_scale
    return (normalized_values * norm_gain_vector + norm_shift_bias, normalized_values, cell_scale)


def norm_reverse_pass(
    upstream_gradient,
    normalized_values,
    cell_scale,
    norm_gain_vector,
    active_flags,
    split_point,
    grand_totals,
):
    running_sums, cross_product = group_totals(
        upstream_gradient, upstream_gradient * normalized_values, active_flags, split_point
    )
    running_sums, cross_product = lax.psum((running_sums, cross_product), ("batch", "tm"))
    cells = upstream_gradient.shape[2]
    upstream_average = per_cell(running_sums / grand_totals[:, None], split_point, cells)
    cross_average = per_cell(cross_product / grand_totals[:, None], split_point, cells)
    final_result = (
        active_flags
        * (norm_gain_vector * cell_scale)
        * (upstream_gradient - upstream_average - normalized_values * cross_average)
    )
    return (final_result, jnp.sum(cross_product, axis=0), jnp.sum(running_sums, axis=0))


def reduce_weight(pairs, depth, width):
    total = jnp.zeros((depth // lax.axis_size("tm") * lax.axis_size("tm"), width), jnp.float32)
    for left, right in pairs:
        total = total + lax.dot_general(
            left, right, (((0,), (0,)), ((), ())), preferred_element_type=jnp.float32
        )
    shared = lax.psum_scatter(total.astype(jnp.bfloat16), "tm", scatter_dimension=0, tiled=True)
    return lax.psum_scatter(shared, "batch", scatter_dimension=1, tiled=True).astype(jnp.float32)


def own_square(shard):
    local = jnp.sum(shard * shard)
    return local


def adamw(weight, gradient, momentum, variance, factor, rate, decay):
    clipped = gradient * factor
    new_momentum = BETA_ONE * momentum + (1.0 - BETA_ONE) * clipped
    new_variance = BETA_TWO * variance + (1.0 - BETA_TWO) * clipped * clipped
    corrected = new_momentum / (1.0 - BETA_ONE**STEP)
    spread = jnp.sqrt(new_variance / (1.0 - BETA_TWO**STEP))
    new_weight = weight - rate * (corrected / (spread + ADAM_EPS) + decay * weight)
    return (new_weight, new_momentum, new_variance)


def plain_body(
    x_small,
    x_large,
    small_output_gradient,
    large_output_gradient,
    clip_counts,
    first_spatial,
    first_temporal,
    second_spatial,
    second_temporal,
    norm_params,
    first_spatial_momentum,
    first_temporal_momentum,
    second_spatial_momentum,
    second_temporal_momentum,
    norm_momentum,
    first_spatial_variance,
    first_temporal_variance,
    second_spatial_variance,
    second_temporal_variance,
    norm_variance,
):
    low_one = first_spatial.astype(jnp.bfloat16)
    low_two = first_temporal.astype(jnp.bfloat16)
    low_three = second_spatial.astype(jnp.bfloat16)
    low_four = second_temporal.astype(jnp.bfloat16)
    columns = (
        lax.all_gather(low_one, "batch", axis=1, tiled=True),
        lax.all_gather(low_two, "batch", axis=1, tiled=True),
        lax.all_gather(low_three, "batch", axis=1, tiled=True),
        lax.all_gather(low_four, "batch", axis=1, tiled=True),
    )
    spatial_one, temporal_one, spatial_two, temporal_two = (
        lax.all_gather(columns[0], "tm", axis=0, tiled=True),
        lax.all_gather(columns[1], "tm", axis=0, tiled=True),
        lax.all_gather(columns[2], "tm", axis=0, tiled=True),
        lax.all_gather(columns[3], "tm", axis=0, tiled=True),
    )
    clips = x_small.shape[0]
    split_point = x_small.shape[2]
    large_cells = x_large.shape[2]
    batch_index = lax.axis_index("batch")
    slots = jnp.arange(clips, dtype=jnp.int32)
    live_small = (slots < clip_counts[0, batch_index]).astype(jnp.float32)
    live_large = (slots < clip_counts[1, batch_index]).astype(jnp.float32)
    active_flags = jnp.concatenate(
        [
            jnp.broadcast_to(live_small[:, None, None, None], (clips, 1, split_point, 1)),
            jnp.broadcast_to(live_large[:, None, None, None], (clips, 1, large_cells, 1)),
        ],
        axis=2,
    )
    frames_total = x_small.shape[1] * lax.axis_size("tm")
    grand_totals = jnp.stack(
        [
            jnp.sum(clip_counts[0]).astype(jnp.float32) * frames_total * split_point,
            jnp.sum(clip_counts[1]).astype(jnp.float32) * frames_total * large_cells,
        ]
    )
    bounds = (0, MID, MID + D, 2 * MID + D, 2 * MID + 2 * D)
    gain_vectors = [norm_params[0, bounds[index] : bounds[index + 1]] for index in range(4)]
    bias_vectors = [norm_params[1, bounds[index] : bounds[index + 1]] for index in range(4)]
    first_convolved, taps_one_small, taps_one_large = spatial_forward(x_small, x_large, spatial_one)
    hidden_one, normed_one, scale_one = norm_forward_pass(
        first_convolved, active_flags, split_point, grand_totals, gain_vectors[0], bias_vectors[0]
    )
    act_one = jax.nn.silu(hidden_one).astype(jnp.bfloat16)
    second_convolved, rows_two = temporal_forward(act_one, temporal_one)
    hidden_two, normed_two, scale_two = norm_forward_pass(
        second_convolved, active_flags, split_point, grand_totals, gain_vectors[1], bias_vectors[1]
    )
    act_two = jax.nn.silu(hidden_two).astype(jnp.bfloat16)
    third_convolved, taps_three_small, taps_three_large = spatial_forward(
        act_two[:, :, :split_point], act_two[:, :, split_point:], spatial_two
    )
    hidden_three, normed_three, scale_three = norm_forward_pass(
        third_convolved, active_flags, split_point, grand_totals, gain_vectors[2], bias_vectors[2]
    )
    act_three = jax.nn.silu(hidden_three).astype(jnp.bfloat16)
    fourth_convolved, rows_four = temporal_forward(act_three, temporal_two)
    hidden_four, fourth_normalized, fourth_scale = norm_forward_pass(
        fourth_convolved, active_flags, split_point, grand_totals, gain_vectors[3], bias_vectors[3]
    )
    residual_in = jnp.concatenate([x_small, x_large], axis=2).astype(jnp.float32)
    output_preactivation = hidden_four + residual_in
    block_output = active_flags * jax.nn.silu(output_preactivation)
    upstream_gradient = (
        jnp.concatenate([small_output_gradient, large_output_gradient], axis=2).astype(jnp.float32)
        * active_flags
    )
    passed_gradient = upstream_gradient * silu_slope(output_preactivation)
    squared_values = []
    grad_conv_four, gain_four, bias_four = norm_reverse_pass(
        passed_gradient,
        fourth_normalized,
        fourth_scale,
        gain_vectors[3],
        active_flags,
        split_point,
        grand_totals,
    )
    grad_conv_four = grad_conv_four.astype(jnp.bfloat16)
    rows_grad_four = grad_conv_four.reshape(-1, grad_conv_four.shape[-1])
    grad_second_temporal = reduce_weight(
        [(rows_four, rows_grad_four)], rows_four.shape[1], rows_grad_four.shape[1]
    )
    squared_values.append(own_square(grad_second_temporal))
    grad_act_three = temporal_backward(grad_conv_four, temporal_two)
    grad_conv_three, gain_three, bias_three = norm_reverse_pass(
        grad_act_three * silu_slope(hidden_three),
        normed_three,
        scale_three,
        gain_vectors[2],
        active_flags,
        split_point,
        grand_totals,
    )
    grad_conv_three = grad_conv_three.astype(jnp.bfloat16)
    rows_three_small = grad_conv_three[:, :, :split_point].reshape(-1, grad_conv_three.shape[-1])
    rows_three_large = grad_conv_three[:, :, split_point:].reshape(-1, grad_conv_three.shape[-1])
    grad_second_spatial = reduce_weight(
        [(taps_three_small, rows_three_small), (taps_three_large, rows_three_large)],
        taps_three_small.shape[1],
        rows_three_small.shape[1],
    )
    squared_values.append(own_square(grad_second_spatial))
    channels_mid = act_two.shape[-1]
    grad_act_two = jnp.concatenate(
        [
            spatial_backward(
                rows_three_small,
                spatial_two,
                (clips, act_two.shape[1], split_point, channels_mid),
                HS,
            ),
            spatial_backward(
                rows_three_large,
                spatial_two,
                (clips, act_two.shape[1], large_cells, channels_mid),
                HL,
            ),
        ],
        axis=2,
    )
    grad_conv_two, gain_two, bias_two = norm_reverse_pass(
        grad_act_two * silu_slope(hidden_two),
        normed_two,
        scale_two,
        gain_vectors[1],
        active_flags,
        split_point,
        grand_totals,
    )
    grad_conv_two = grad_conv_two.astype(jnp.bfloat16)
    rows_grad_two = grad_conv_two.reshape(-1, grad_conv_two.shape[-1])
    grad_first_temporal = reduce_weight(
        [(rows_two, rows_grad_two)], rows_two.shape[1], rows_grad_two.shape[1]
    )
    squared_values.append(own_square(grad_first_temporal))
    grad_act_one = temporal_backward(grad_conv_two, temporal_one)
    grad_conv_one, gain_one, bias_one = norm_reverse_pass(
        grad_act_one * silu_slope(hidden_one),
        normed_one,
        scale_one,
        gain_vectors[0],
        active_flags,
        split_point,
        grand_totals,
    )
    grad_conv_one = grad_conv_one.astype(jnp.bfloat16)
    rows_one_small = grad_conv_one[:, :, :split_point].reshape(-1, grad_conv_one.shape[-1])
    rows_one_large = grad_conv_one[:, :, split_point:].reshape(-1, grad_conv_one.shape[-1])
    grad_first_spatial = reduce_weight(
        [(taps_one_small, rows_one_small), (taps_one_large, rows_one_large)],
        taps_one_small.shape[1],
        rows_one_small.shape[1],
    )
    squared_values.append(own_square(grad_first_spatial))
    input_small = passed_gradient[:, :, :split_point] + spatial_backward(
        rows_one_small, spatial_one, x_small.shape, HS
    )
    input_large = passed_gradient[:, :, split_point:] + spatial_backward(
        rows_one_large, spatial_one, x_large.shape, HL
    )
    grad_params = jnp.stack(
        [
            jnp.concatenate([gain_one, gain_two, gain_three, gain_four]),
            jnp.concatenate([bias_one, bias_two, bias_three, bias_four]),
        ]
    )
    summed = lax.psum(
        (squared_values[0], squared_values[1], squared_values[2], squared_values[3]),
        ("batch", "tm"),
    )
    weight_square = summed[0] + summed[1] + summed[2] + summed[3]
    grad_norm = jnp.sqrt(weight_square + jnp.sum(grad_params * grad_params))
    factor = THRESHOLD / jnp.maximum(grad_norm, THRESHOLD)
    one = adamw(
        first_spatial,
        grad_first_spatial,
        first_spatial_momentum,
        first_spatial_variance,
        factor,
        WEIGHT_RATE,
        WEIGHT_DECAY,
    )
    two = adamw(
        first_temporal,
        grad_first_temporal,
        first_temporal_momentum,
        first_temporal_variance,
        factor,
        WEIGHT_RATE,
        WEIGHT_DECAY,
    )
    three = adamw(
        second_spatial,
        grad_second_spatial,
        second_spatial_momentum,
        second_spatial_variance,
        factor,
        WEIGHT_RATE,
        WEIGHT_DECAY,
    )
    four = adamw(
        second_temporal,
        grad_second_temporal,
        second_temporal_momentum,
        second_temporal_variance,
        factor,
        WEIGHT_RATE,
        WEIGHT_DECAY,
    )
    norms = adamw(norm_params, grad_params, norm_momentum, norm_variance, factor, NORM_RATE, 0.0)
    return (
        block_output[:, :, :split_point],
        block_output[:, :, split_point:],
        input_small,
        input_large,
        grad_norm,
        one[0],
        one[1],
        one[2],
        two[0],
        two[1],
        two[2],
        three[0],
        three[1],
        three[2],
        four[0],
        four[1],
        four[2],
        norms[0],
        norms[1],
        norms[2],
    )


BF = jnp.bfloat16
F32 = jnp.float32
MESH_ID = pl.DeviceIdType.MESH
NT_DIMS = (((1,), (1,)), ((), ()))
NN_DIMS = (((1,), (0,)), ((), ()))
UP, DOWN, ACROSS, ALONG, TWIN = range(5)


class Place:
    def __init__(self, batches, slots):
        self.batches, self.slots = batches, slots
        self.z = lax.axis_index("batch")
        self.t = lax.axis_index("tm")
        self.core = lax.rem(self.t, 2)
        self.slab = self.t // 2
        self.slabs = slots // 2
        side = lax.rem(self.slab, 2)
        deep = self.slab // 2
        self.side_slab = deep * 2 + (1 - side)
        self.deep_slab = (1 - deep) * 2 + side
        self.far_slab = (1 - deep) * 2 + (1 - side)
        self.rel = (self.slab, self.side_slab, self.deep_slab, self.far_slab)
        self.twin = self.t + 1 - 2 * self.core

    def device(self, way):
        if way == UP:
            return (self.z + 1, self.t)
        if way == DOWN:
            return (self.z - 1, self.t)
        if way == ACROSS:
            return (self.z, self.side_slab * 2 + self.core)
        if way == ALONG:
            return (self.z, self.deep_slab * 2 + self.core)
        return (self.z, self.twin)

    def greet(self):
        barrier = pltpu.get_barrier_semaphore()
        for step in range(1, self.slots):
            pl.semaphore_signal(
                barrier, inc=1, device_id=(self.z, lax.rem(self.t + step, self.slots)),
                device_id_type=MESH_ID,
            )
        for step in range(1, self.batches):
            pl.semaphore_signal(
                barrier, inc=1, device_id=(lax.rem(self.z + step, self.batches), self.t),
                device_id_type=MESH_ID,
            )
        pl.semaphore_wait(barrier, self.slots + self.batches - 2)


def send(src, dst, send_sem, recv_sem, device):
    return pltpu.make_async_remote_copy(
        src_ref=src, dst_ref=dst, send_sem=send_sem, recv_sem=recv_sem,
        device_id=device, device_id_type=MESH_ID,
    )


class Totals:
    def __init__(self, place, rows, planes, lines, sems):
        self.place, self.rows, self.planes, self.lines = place, rows, planes, lines
        self.plane_send, self.plane_recv, self.line_send, self.line_recv = sems

    def run(self, n, value):
        p = self.place
        width = value.shape[1]
        plane, line = self.planes.at[n], self.lines.at[n]
        plane[p.t, :, :width] = value

        def plane_copy(step):
            to = lax.rem(p.t + step, p.slots)
            ref = plane.at[p.t, :, pl.ds(0, width)]
            return send(ref, ref, self.plane_send.at[n, step], self.plane_recv.at[n, p.t], (p.z, to))

        def plane_wait(step):
            origin = lax.rem(p.t + p.slots - step, p.slots)
            ref = plane.at[origin, :, pl.ds(0, width)]
            send(ref, ref, self.plane_send.at[n, step], self.plane_recv.at[n, origin], (p.z, p.twin)).wait_recv()

        for step in range(1, p.slots):
            plane_copy(step).start()
        for step in range(1, p.slots):
            plane_wait(step)
        total = plane[0, :, :width]
        for slot in range(1, p.slots):
            total = total + plane[slot, :, :width]
        line[p.z, :, :width] = total

        def line_copy(step):
            to = lax.rem(p.z + step, p.batches)
            ref = line.at[p.z, :, pl.ds(0, width)]
            return send(ref, ref, self.line_send.at[n, step], self.line_recv.at[n, p.z], (to, p.t))

        def line_wait(step):
            origin = lax.rem(p.z + p.batches - step, p.batches)
            ref = line.at[origin, :, pl.ds(0, width)]
            send(ref, ref, self.line_send.at[n, step], self.line_recv.at[n, origin], (p.z, p.twin)).wait_recv()

        for step in range(1, p.batches):
            line_copy(step).start()
        for step in range(1, p.batches):
            line_wait(step)
        total = line[0, :, :width]
        for slot in range(1, p.batches):
            total = total + line[slot, :, :width]
        for step in range(1, p.slots):
            plane_copy(step).wait_send()
        for step in range(1, p.batches):
            line_copy(step).wait_send()
        return total


class Gather:
    def __init__(self, place, index, own, whole, block, sems):
        self.p, self.n, self.own, self.whole, self.block = place, index, own, whole, block
        self.send_sem, self.recv_sem, self.twin_sem = sems

    def copy(self, way, rel, batch, src=None):
        p = self.p
        core = p.core
        dst = self.whole.at[self.block(p.rel[rel], core, batch)]
        there = {ACROSS: {0: 1, 2: 3}, ALONG: {0: 2, 1: 3}}.get(way, {}).get(rel, rel)
        sem = self.twin_sem if way == TWIN else self.recv_sem
        return send(
            dst if src is None else src, dst, self.send_sem.at[self.n, way, rel, batch],
            sem.at[self.n, there, batch], p.device(way),
        )

    def wait(self, rel, batch, twin=False):
        p = self.p
        core = 1 - p.core if twin else p.core
        ref = self.whole.at[self.block(p.rel[rel], core, batch)]
        sem = self.twin_sem if twin else self.recv_sem
        send(ref, ref, self.send_sem.at[self.n, TWIN, rel, batch], sem.at[self.n, rel, batch],
             p.device(TWIN)).wait_recv()

    def at(self, k, fn):
        p = self.p
        if k == 0:
            fn(p.z)
            return
        pl.when(p.z - k >= 0)(lambda: fn(p.z - k))
        pl.when(p.z + k < p.batches)(lambda: fn(p.z + k))

    def start(self):
        p = self.p
        pl.when(p.z < p.batches - 1)(lambda: self.copy(UP, 0, p.z, self.own).start())
        pl.when(p.z > 0)(lambda: self.copy(DOWN, 0, p.z, self.own).start())
        for way in (ACROSS, ALONG, TWIN):
            self.copy(way, 0, p.z, self.own).start()

    def hop(self, k):
        p = self.p

        def below(b):
            self.wait(0, b)
            pl.when(p.z < p.batches - 1)(lambda: self.copy(UP, 0, b).start())
            for way in (ACROSS, ALONG, TWIN):
                self.copy(way, 0, b).start()

        def above(b):
            self.wait(0, b)
            pl.when(p.z > 0)(lambda: self.copy(DOWN, 0, b).start())
            for way in (ACROSS, ALONG, TWIN):
                self.copy(way, 0, b).start()

        pl.when(p.z - k >= 0)(lambda: below(p.z - k))
        pl.when(p.z + k < p.batches)(lambda: above(p.z + k))

    def plane(self, k):
        half = self.p.batches // 2

        def one(b):
            self.wait(1, b)
            pl.when(b < half)(lambda: self.copy(ALONG, 1, b).start())
            self.copy(TWIN, 1, b).start()
            self.wait(2, b)
            pl.when(b >= half)(lambda: self.copy(ACROSS, 2, b).start())
            self.copy(TWIN, 2, b).start()

        self.at(k, one)

    def far(self, k):
        def one(b):
            self.wait(3, b)
            self.copy(TWIN, 3, b).start()

        self.at(k, one)

    def twins(self, rel):
        def body(b, _):
            self.wait(rel, b, twin=True)
            return 0

        lax.fori_loop(0, self.p.batches, body, 0)

    def steps(self):
        batches = self.p.batches
        order = [self.start]
        for k in range(batches):
            if k:
                order.append(functools.partial(self.hop, k))
                order.append(functools.partial(self.far, k - 1))
            order.append(functools.partial(self.plane, k))
        order.append(functools.partial(self.far, batches - 1))
        return order

    def finish(self):
        p = self.p
        half = p.batches // 2

        def body(b, _):
            pl.when((b <= p.z) & (p.z < p.batches - 1))(lambda: self.copy(UP, 0, b, self.own).wait_send())
            pl.when((b >= p.z) & (p.z > 0))(lambda: self.copy(DOWN, 0, b, self.own).wait_send())
            for way in (ACROSS, ALONG):
                self.copy(way, 0, b, self.own).wait_send()
            for rel in range(4):
                self.copy(TWIN, rel, b, self.own).wait_send()
            pl.when(b < half)(lambda: self.copy(ALONG, 1, b, self.own).wait_send())
            pl.when(b >= half)(lambda: self.copy(ACROSS, 2, b, self.own).wait_send())
            return 0

        lax.fori_loop(0, p.batches, body, 0)


def sigmoid(v):
    return 0.5 * jnp.tanh(0.5 * v) + 0.5


class Shape:
    def __init__(self, x_small, x_large, batches, slots):
        self.clips = x_small[0]
        self.cells = (x_small[2], x_large[2])
        self.sides = (math.isqrt(x_small[2]), math.isqrt(x_large[2]))
        self.d = x_small[3]
        self.padded = tuple(n + n % 2 for n in self.cells)
        self.rows = tuple(n * self.clips for n in self.padded)
        self.m = sum(self.rows)
        self.mid = MID
        self.k = 9 * self.d
        self.batches, self.slots = batches, slots
        self.slabs = slots // 2
        self.kw = self.k // self.slabs
        self.nb = self.mid // (2 * batches)
        self.ur = 3 * self.mid // slots
        self.uc = self.d // batches


def fits(x_small, x_large, batches, slots):
    s = Shape(x_small, x_large, batches, slots)
    return (
        s.clips == 8 and x_small[1] == 1 and slots == 8 and batches >= 2 and batches % 2 == 0
        and all(side * side == cells for side, cells in zip(s.sides, s.cells))
        and all(r % 80 == 0 for r in s.rows)
        and s.kw % 128 == 0 and s.mid % (32 * batches) == 0 and s.ur % 16 == 0 and s.uc % 128 == 0
    )


def chunks(s, size, fn, carry=None, unroll=1):
    out = []
    base = 0
    for group, rows in enumerate(s.rows):
        def body(i, c, group=group, base=base):
            return fn(group, pl.multiple_of(base + i * size, size if base % size == 0 else 16), c)

        out.append(lax.fori_loop(0, rows // size, body, carry if carry is not None else 0, unroll=unroll))
        base += rows
    return out


def sums_of(s, load, live, width):
    def body(group, r0, c):
        values = load(group, r0, 80)
        return tuple(t + jnp.sum(v.reshape(10, 8, width), axis=0) for t, v in zip(c, values))

    zero = jnp.zeros((8, width), F32)
    small, large = chunks(s, 80, body, (zero, zero))
    rows = [jnp.sum(v * live[g], axis=0, keepdims=True) for v, g in
            ((small[0], 0), (large[0], 1), (small[1], 0), (large[1], 1))]
    return jnp.concatenate(rows, axis=0)


def build_taps(s, grids, taps):
    pieces = []
    for tap in range(9):
        lo = tap * s.d
        end = lo + s.d
        while lo < end:
            hi = min(end, (lo // s.kw + 1) * s.kw)
            pieces.append((tap, lo - tap * s.d, lo // s.kw, lo % s.kw, hi - lo))
            lo = hi
    base = 0
    for group in range(2):
        side, cells = s.sides[group], s.cells[group]
        grid = grids[group]
        for tap, channel, slab, lane, width in pieces:
            i, j = tap // 3, tap % 3
            if side % 2 == 0:
                n = 2 * side * 8

                def body(r, _):
                    window = grid[pl.ds(i + 2 * r, 2), j : j + side, :, channel : channel + width]
                    taps[slab, pl.ds(pl.multiple_of(base + r * n, 16), n), lane : lane + width] = (
                        window.reshape(n, width).astype(BF)
                    )
                    return 0

                lax.fori_loop(0, side // 2, body, 0)
            else:
                window = grid[i : i + side, j : j + side, :, channel : channel + width]
                window = window.reshape(cells * 8, width)
                window = jnp.concatenate(
                    [window, jnp.zeros((s.rows[group] - cells * 8, width), F32)], axis=0
                ) if s.rows[group] > cells * 8 else window
                taps[slab, base : base + s.rows[group], lane : lane + width] = window.astype(BF)
        base += s.rows[group]


def fill_grid(s, grids, group, cell, value):
    side = s.sides[group]
    grids[group][1 + cell // side, 1 + lax.rem(cell, side)] = value


def zero_padding(s, ref, width):
    base = 0
    for group in range(2):
        base += s.rows[group]
        spare = (s.padded[group] - s.cells[group]) * s.clips
        if spare:
            size = -(-spare // 16) * 16
            keep = lax.broadcasted_iota(jnp.int32, (size, width), 0) < size - spare
            value = ref[base - size : base, :].astype(F32)
            ref[base - size : base, :] = jnp.where(keep, value, 0.0).astype(ref.dtype)


def grid_of_rows(s, grids, group, r0, value):
    side = s.sides[group]
    base = 0 if group == 0 else s.rows[0]
    first = (r0 - base) // 8
    split = value.reshape(10, 8, s.d)
    for n in range(10):
        cell = first + n
        grids[group][1 + cell // side, 1 + lax.rem(cell, side)] = split[n]


def clear_pad_cells(s, grids):
    for group in range(2):
        side = s.sides[group]
        for cell in range(s.cells[group], s.padded[group]):
            grids[group][1 + cell // side, 1 + cell % side] = jnp.zeros((8, s.d), F32)


def moments(total, inverse, width):
    mean = [total[g : g + 1, :] * inverse[g] for g in range(2)]
    scale = [
        lax.rsqrt(total[2 + g : 3 + g, :] * inverse[g] - mean[g] * mean[g] + NORM_EPS) for g in range(2)
    ]
    return mean, scale


def wide_cuts(width):
    half = -(-width // 256) * 128
    return ((0, half), (half, width - half))


def forward_kernel(s, *refs):
    (x, grad, sw1, uw1, sw2, uw2, norm, live_ref, inverse,
     gs1, gu1, gs2, gu2, taps1_o, taps2_o, xh1_o, xh2_o, xh3_o, xh4_o, z1_o, z3_o, out, dpre,
     r1_o, r2_o, r3_o, r4_o, last_o,
     tb1, tb2, own1, own2, wb, wub, taps, a, z, grid_s, grid_l, b, hs, hr, planes, lines,
     ag_send, ag_recv, ag_twin, tb_send, tb_recv, local, load, hs_send, hs_recv,
     pl_send, pl_recv, ln_send, ln_recv) = refs
    p = Place(s.batches, s.slots)
    live = [live_ref[g] for g in range(2)]
    inv = [inverse[g] for g in range(2)]
    totals = Totals(p, 4, planes, lines, (pl_send, pl_recv, ln_send, ln_recv))
    d, mid = s.d, s.mid
    bounds = (0, mid, mid + d, 2 * mid + d, 2 * mid + 2 * d)

    def gain_bias(n):
        return norm[0:1, bounds[n] : bounds[n + 1]], norm[1:2, bounds[n] : bounds[n + 1]]

    p.greet()

    def twin_copy(n, src, dst):
        return send(
            src.at[1 - p.core], dst.at[pl.ds(pl.multiple_of(p.core * (s.kw // 2), 16), s.kw // 2)],
            tb_send.at[n], tb_recv.at[n], p.device(TWIN),
        )

    def twin_wait(n, src, dst):
        send(
            src.at[1 - p.core], dst.at[pl.ds(pl.multiple_of((1 - p.core) * (s.kw // 2), 16), s.kw // 2)],
            tb_send.at[n], tb_recv.at[n], p.device(TWIN),
        ).wait_recv()

    for n, src, dst in ((0, sw1, tb1), (1, sw2, tb2)):
        twin_copy(n, src, dst).start()
        dst[pl.ds(pl.multiple_of(p.core * (s.kw // 2), 16), s.kw // 2)] = src[p.core]

    def s_block(slab, core, batch):
        return (slab, pl.ds(pl.multiple_of((batch * 2 + core) * s.nb, 16), s.nb))

    def u_block(slab, core, batch):
        return (pl.ds(pl.multiple_of((slab * 2 + core) * s.ur, 16), s.ur),
                pl.ds(pl.multiple_of(batch * s.uc, 128), s.uc))

    sems = (ag_send, ag_recv, ag_twin)
    gather = [
        Gather(p, 0, own1, gs1, s_block, sems),
        Gather(p, 1, uw1, gu1, u_block, sems),
        Gather(p, 2, own2, gs2, s_block, sems),
        Gather(p, 3, uw2, gu2, u_block, sems),
    ]

    def keep_own(n):
        g = gather[n]
        return pltpu.make_async_copy(g.own, g.whole.at[g.block(p.slab, p.core, p.z)], local.at[n])

    twin_wait(0, sw1, tb1)
    own1[...] = tb1[...].T
    queue = [(0, step) for step in gather[0].steps()]
    queue.pop(0)[1]()
    keep_own(0).start()
    twin_wait(1, sw2, tb2)
    own2[...] = tb2[...].T
    keep_own(1).start()
    keep_own(2).start()
    keep_own(3).start()
    for n in (1, 2, 3):
        queue += [(n, step) for step in gather[n].steps()]

    def tick(count):
        for _ in range(count):
            if queue:
                queue.pop(0)[1]()

    def flush(n):
        while queue and queue[0][0] <= n:
            queue.pop(0)[1]()

    for side, edge in ((0, 0), (1, p.slots - 1)):
        @pl.when(p.t == edge)
        def _(side=side):
            hr[side] = jnp.zeros(hr.shape[1:], BF)

    grids = (grid_s, grid_l)
    for grid in grids:
        def clear(i, _, grid=grid):
            grid[i] = jnp.zeros(grid.shape[1:], F32)
            return 0

        lax.fori_loop(0, grid.shape[0], clear, 0)

    def x_rows(group, r0, c):
        grid_of_rows(s, grids, group, r0, x[pl.ds(r0, 80), :].astype(F32))
        return c

    chunks(s, 80, x_rows)
    clear_pad_cells(s, grids)
    build_taps(s, grids, taps)
    taps_copy = pltpu.make_async_copy(taps, taps1_o, local.at[4])
    taps_copy.start()

    def slab_load(whole, rel):
        return pltpu.make_async_copy(whole.at[p.rel[rel]], wb.at[rel], load.at[rel])

    def conv_slab(rel):
        for lo, width in wide_cuts(mid):
            y = lax.dot_general(taps[p.rel[rel]], wb[rel, lo : lo + width, :], NT_DIMS, preferred_element_type=F32)
            if rel == 0:
                a[:, lo : lo + width] = y
            else:
                a[:, lo : lo + width] += y

    def spatial(n, whole, spare):
        g = gather[n]
        while queue and queue[0][0] <= n and len([q for q in queue if q[0] <= n]) > 1:
            queue.pop(0)[1]()
        g.twins(0)
        if n == 0:
            keep_own(0).wait()
        else:
            keep_own(2).wait()
        slab_load(whole, 0).start()
        g.twins(1)
        slab_load(whole, 1).start()
        g.twins(2)
        slab_load(whole, 2).start()
        slab_load(whole, 0).wait()
        conv_slab(0)
        flush(n)
        g.twins(3)
        slab_load(whole, 3).start()
        for rel in (1, 2, 3):
            tick(spare)
            slab_load(whole, rel).wait()
            conv_slab(rel)

    def stats(load_rows, width):
        return sums_of(s, load_rows, live, width)

    def wide_norm(index, n, zo, xo, ro, sem):
        def load_rows(group, r0, size):
            v = a[pl.ds(r0, size), :]
            return v, v * v

        total = totals.run(index, stats(load_rows, mid))
        mean, scale = moments(total, inv, mid)
        ro[...] = jnp.concatenate(scale, axis=0)
        gain, bias = gain_bias(n)

        def rows(group, r0, c):
            xhat = (a[pl.ds(r0, 16), :] - mean[group]) * scale[group]
            a[pl.ds(r0, 16), :] = xhat
            h = xhat * gain + bias
            z[pl.ds(r0, 16), :] = (h * sigmoid(h)).astype(BF)
            return c

        chunks(s, 16, rows)
        zero_padding(s, z, mid)
        xc = pltpu.make_async_copy(a, xo, local.at[sem])
        zc = pltpu.make_async_copy(z, zo, local.at[sem + 1])
        xc.start()
        zc.start()
        return xc, zc

    def u_load(n, whole):
        return pltpu.make_async_copy(whole, wub, load.at[4 + n])

    def halo(n, side):
        to = p.t + 1 if side == 0 else p.t - 1
        return send(hs.at[side], hr.at[side], hs_send.at[n, side], hs_recv.at[n, side], (p.z, to))

    def temporal(n, index, between):
        flush(index)
        for rel in range(4):
            gather[index].twins(rel)
        keep_own(index).wait()
        load_w = u_load(n, gather[index].whole)
        load_w.start()
        load_w.wait()
        hs[0] = jnp.dot(z[...], wub[:mid, :], preferred_element_type=F32).astype(BF)
        pl.when(p.t < p.slots - 1)(lambda: halo(n, 0).start())
        hs[1] = jnp.dot(z[...], wub[2 * mid :, :], preferred_element_type=F32).astype(BF)
        pl.when(p.t > 0)(lambda: halo(n, 1).start())
        b[...] = jnp.dot(z[...], wub[mid : 2 * mid, :], preferred_element_type=F32)
        between()
        pl.when(p.t > 0)(lambda: halo(n, 0).wait_recv())
        pl.when(p.t < p.slots - 1)(lambda: halo(n, 1).wait_recv())

    def narrow_total(index):
        def load_rows(group, r0, size):
            v = b[pl.ds(r0, size), :] + hr[0, pl.ds(r0, size), :].astype(F32) + hr[1, pl.ds(r0, size), :].astype(F32)
            b[pl.ds(r0, size), :] = v
            return v, v * v

        return totals.run(index, stats(load_rows, d))

    def halo_done(n):
        pl.when(p.t < p.slots - 1)(lambda: halo(n, 0).wait_send())
        pl.when(p.t > 0)(lambda: halo(n, 1).wait_send())

    spatial(0, gs1, 4)
    tick(1)
    xc1, zc1 = wide_norm(0, 0, z1_o, xh1_o, r1_o, 5)
    tick(2)
    temporal(0, 1, lambda: tick(2))
    total = narrow_total(1)
    tick(1)
    mean2, scale2 = moments(total, inv, d)
    r2_o[...] = jnp.concatenate(scale2, axis=0)
    gain2, bias2 = gain_bias(1)

    def second(group, r0, c):
        xhat = (b[pl.ds(r0, 80), :] - mean2[group]) * scale2[group]
        b[pl.ds(r0, 80), :] = xhat
        h = xhat * gain2 + bias2
        grid_of_rows(s, grids, group, r0, (h * sigmoid(h)).astype(BF).astype(F32))
        return c

    chunks(s, 80, second)
    clear_pad_cells(s, grids)
    xc2 = pltpu.make_async_copy(b, xh2_o, local.at[7])
    xc2.start()
    halo_done(0)
    tick(2)
    taps_copy.wait()
    build_taps(s, grids, taps)
    taps_copy2 = pltpu.make_async_copy(taps, taps2_o, local.at[8])
    taps_copy2.start()
    xc1.wait()
    spatial(2, gs2, 4)
    tick(2)
    zc1.wait()
    xc3, zc3 = wide_norm(2, 2, z3_o, xh3_o, r3_o, 9)
    tick(2)
    xc2.wait()
    temporal(1, 3, lambda: None)
    total = narrow_total(3)
    mean4, scale4 = moments(total, inv, d)
    r4_o[...] = jnp.concatenate(scale4, axis=0)
    gain4, bias4 = gain_bias(3)

    def last(group, r0, c):
        xhat = (b[pl.ds(r0, 80), :] - mean4[group]) * scale4[group]
        b[pl.ds(r0, 80), :] = xhat
        pre = xhat * gain4 + bias4 + x[pl.ds(r0, 80), :].astype(F32)
        gate = sigmoid(pre)
        alive = jnp.broadcast_to(live[group][None], (10, 8, d)).reshape(80, d)
        out[pl.ds(r0, 80), :] = alive * (pre * gate)
        up = alive * grad[pl.ds(r0, 80), :].astype(F32) * (gate * (1.0 + pre * (1.0 - gate)))
        dpre[pl.ds(r0, 80), :] = up
        return c

    chunks(s, 80, last)
    zero_padding(s, dpre, d)
    xc4 = pltpu.make_async_copy(b, xh4_o, local.at[11])
    xc4.start()

    def last_rows(group, r0, size):
        v = dpre[pl.ds(r0, size), :]
        return v, v * b[pl.ds(r0, size), :]

    last_o[...] = totals.run(4, stats(last_rows, d))
    halo_done(1)
    for g in gather:
        g.finish()
    for n, src, dst in ((0, sw1, tb1), (1, sw2, tb2)):
        twin_copy(n, src, dst).wait_send()
    for c in (taps_copy2, zc3, xc3, xc4):
        c.wait()


def forward_call(s, x, grad, sw1, uw1, sw2, uw2, norm, live, inverse):
    any_, vmem, smem = (pl.BlockSpec(memory_space=m) for m in (pl.ANY, pltpu.VMEM, pltpu.SMEM))
    S = jax.ShapeDtypeStruct
    m, d, mid = s.m, s.d, s.mid
    gs = S((s.slabs, mid, s.kw), BF)
    gu = S((3 * mid, d), BF)
    taps = S((s.slabs, m, s.kw), BF)
    wide, narrow = S((m, mid), F32), S((m, d), F32)
    zs = S((m, mid), BF)
    outs = (gs, gu, gs, gu, taps, taps, wide, narrow, wide, narrow, zs, zs, narrow, narrow,
            S((2, mid), F32), S((2, d), F32), S((2, mid), F32), S((2, d), F32), S((4, d), F32))
    specs = (any_,) * 12 + (vmem,) * 7
    dma, V = pltpu.SemaphoreType.DMA, pltpu.VMEM
    nb = s.batches
    n_sums = 5
    scratch = [
        V((s.kw, s.nb), BF), V((s.kw, s.nb), BF), V((s.nb, s.kw), BF), V((s.nb, s.kw), BF),
        V((s.slabs, mid, s.kw), BF), V((3 * mid, d), BF), V((s.slabs, m, s.kw), BF),
        V((m, mid), F32), V((m, mid), BF),
        V((s.sides[0] + 2, s.sides[0] + 2, 8, d), F32), V((s.sides[1] + 2, s.sides[1] + 2, 8, d), F32),
        V((m, d), F32), V((2, m, d), BF), V((2, m, d), BF),
        V((n_sums, s.slots, 4, mid), F32), V((n_sums, nb, 4, mid), F32),
        dma((4, 5, 4, nb)), dma((4, 4, nb)), dma((4, 4, nb)), dma((2,)), dma((2,)), dma((12,)), dma((6,)),
        dma((2, 2)), dma((2, 2)),
        dma((n_sums, s.slots)), dma((n_sums, s.slots)), dma((n_sums, nb)), dma((n_sums, nb)),
    ]
    return pl.pallas_call(
        functools.partial(forward_kernel, s),
        out_shape=outs,
        in_specs=[vmem, vmem, vmem, any_, vmem, any_, vmem, vmem, smem],
        out_specs=specs,
        scratch_shapes=scratch,
        compiler_params=pltpu.CompilerParams(
            collective_id=0, has_side_effects=True, vmem_limit_bytes=63 * 2**20
        ),
        name="forward",
    )(x, grad, sw1, uw1, sw2, uw2, norm, live, inverse)


def cell_major(s, small, large):
    parts = []
    for group, v in enumerate((small, large)):
        v = v.reshape(s.clips, s.cells[group], s.d).transpose(1, 0, 2)
        parts.append(jnp.pad(v, ((0, s.padded[group] - s.cells[group]), (0, 0), (0, 0))))
    return jnp.concatenate(parts, axis=0).reshape(s.m, s.d)


def clip_major(s, v):
    v = v.reshape(-1, s.clips, s.d)
    parts, base = [], 0
    for group in range(2):
        part = v[base : base + s.cells[group]].transpose(1, 0, 2)
        parts.append(part.reshape(s.clips, 1, s.cells[group], s.d))
        base += s.padded[group]
    return parts


def halves(s, w):
    return w.astype(BF).reshape(w.shape[0], 2, s.nb).transpose(1, 0, 2)


def body(batches, slots, *args):
    x_small, x_large = args[0], args[1]
    plain = plain_body(*args)
    if not fits(x_small.shape, x_large.shape, batches, slots):
        return plain
    fast = fast_body(Shape(x_small.shape, x_large.shape, batches, slots), *args)
    return tuple(fast[:2]) + tuple(plain[2:])


def fast_body(s, x_small, x_large, grad_small, grad_large, clip_counts, first_spatial, first_temporal,
              second_spatial, second_temporal, norm_params, *states):
    z = lax.axis_index("batch")
    slots = jnp.arange(s.clips, dtype=jnp.int32)
    counts = lax.dynamic_index_in_dim(clip_counts, z, 1, keepdims=False)
    live = (slots[None, :] < counts[:, None]).astype(F32)[:, :, None]
    totals = jnp.sum(clip_counts, axis=1).astype(F32) * (s.slots * jnp.array(s.cells, F32))
    x = cell_major(s, x_small, x_large)
    grad = cell_major(s, grad_small, grad_large)
    res = forward_call(
        s, x, grad, halves(s, first_spatial), first_temporal.astype(BF), halves(s, second_spatial),
        second_temporal.astype(BF), norm_params, live, 1.0 / totals,
    )
    out_small, out_large = clip_major(s, res[12])
    return (out_small, out_large) + tuple(res)


def solution(mesh):
    return jax.shard_map(
        functools.partial(body, mesh.shape["batch"], mesh.shape["tm"]),
        mesh=mesh,
        in_specs=(
            P("batch", "tm", None, None),
            P("batch", "tm", None, None),
            P("batch", "tm", None, None),
            P("batch", "tm", None, None),
            P(),
            P("tm", "batch"),
            P("tm", "batch"),
            P("tm", "batch"),
            P("tm", "batch"),
            P(),
            P("tm", "batch"),
            P("tm", "batch"),
            P("tm", "batch"),
            P("tm", "batch"),
            P(),
            P("tm", "batch"),
            P("tm", "batch"),
            P("tm", "batch"),
            P("tm", "batch"),
            P(),
        ),
        out_specs=(
            P("batch", "tm", None, None),
            P("batch", "tm", None, None),
            P("batch", "tm", None, None),
            P("batch", "tm", None, None),
            P(),
            P("tm", "batch"),
            P("tm", "batch"),
            P("tm", "batch"),
            P("tm", "batch"),
            P("tm", "batch"),
            P("tm", "batch"),
            P("tm", "batch"),
            P("tm", "batch"),
            P("tm", "batch"),
            P("tm", "batch"),
            P("tm", "batch"),
            P("tm", "batch"),
            P(),
            P(),
            P(),
        ),
        check_vma=False,
    )
```

```python
import functools
import math

import jax
import jax.numpy as jnp
from jax import lax
from jax.experimental import pallas as pl
from jax.experimental.pallas import tpu as pltpu
from jax.sharding import PartitionSpec as P

D = 512
MID = 1152
HS = 7
HL = 10
STEP = 10


NORM_EPS = 1e-05
THRESHOLD = 1.0
BETA_ONE = 0.9
BETA_TWO = 0.999
WEIGHT_RATE = 0.03
NORM_RATE = 0.25
WEIGHT_DECAY = 0.05
ADAM_EPS = 1e-08


def padded_2(value, sides, width):
    for axis, dim in sides:
        size, length = (lax.axis_size(axis), value.shape[dim])
        up = [(i, (i + 1) % size) for i in range(size - 1)]
        down = [(j, i) for i, j in up]
        last = lax.slice_in_dim(value, length - width, length, axis=dim)
        first = lax.slice_in_dim(value, 0, width, axis=dim)
        before = lax.ppermute(last, axis, up)
        after = lax.ppermute(first, axis, down)
        value = jnp.concatenate([before, value, after], axis=dim)
    return value


def silu_slope(input_value):
    sigmoid_value = jax.nn.sigmoid(input_value)
    return sigmoid_value * (1.0 + input_value * (1.0 - sigmoid_value))


def spatial_taps(field, side):
    clips, frames, cells, channels = field.shape
    grid = field.reshape(clips, frames, side, side, channels)
    padded = jnp.pad(grid, ((0, 0), (0, 0), (1, 1), (1, 1), (0, 0)))
    pieces = [
        padded[:, :, row : row + side, column : column + side, :]
        for row in range(3)
        for column in range(3)
    ]
    return jnp.concatenate(pieces, axis=-1).reshape(clips * frames * cells, 9 * channels)


def spatial_forward(field_small, field_large, weight):
    taps_small = spatial_taps(field_small, HS)
    taps_large = spatial_taps(field_large, HL)
    result_small = jnp.dot(taps_small, weight, preferred_element_type=jnp.float32).reshape(
        field_small.shape[:3] + (weight.shape[1],)
    )
    result_large = jnp.dot(taps_large, weight, preferred_element_type=jnp.float32).reshape(
        field_large.shape[:3] + (weight.shape[1],)
    )
    return (jnp.concatenate([result_small, result_large], axis=2), taps_small, taps_large)


def spatial_backward(upstream_rows, weight, shape, side):
    clips, frames, cells, channels = shape
    columns = lax.dot_general(
        upstream_rows, weight, (((1,), (1,)), ((), ())), preferred_element_type=jnp.float32
    )
    columns = columns.reshape(clips, frames, side, side, 9 * channels)
    padded = jnp.pad(columns, ((0, 0), (0, 0), (1, 1), (1, 1), (0, 0)))
    final_result = None
    for row in range(3):
        for column in range(3):
            offset = (3 * row + column) * channels
            window = padded[
                :,
                :,
                2 - row : 2 - row + side,
                2 - column : 2 - column + side,
                offset : offset + channels,
            ]
            final_result = window if final_result is None else final_result + window
    return final_result.reshape(clips, frames, cells, channels)


def temporal_forward(field, weight):
    padded = padded_2(field, (("tm", 1),), 1)
    frames = field.shape[1]
    pieces = jnp.concatenate([padded[:, shift : shift + frames] for shift in range(3)], axis=-1)
    rows = pieces.reshape(-1, pieces.shape[-1])
    final_result = jnp.dot(rows, weight, preferred_element_type=jnp.float32).reshape(
        field.shape[:3] + (weight.shape[1],)
    )
    return (final_result, rows)


def temporal_backward(upstream_gradient, weight):
    padded = padded_2(upstream_gradient, (("tm", 1),), 1)
    frames = upstream_gradient.shape[1]
    pieces = jnp.concatenate(
        [padded[:, 2 - shift : 2 - shift + frames] for shift in range(3)], axis=-1
    )
    rows = pieces.reshape(-1, pieces.shape[-1])
    kernel = (
        weight.reshape(3, -1, weight.shape[1]).transpose(1, 0, 2).reshape(-1, 3 * weight.shape[1])
    )
    final_result = lax.dot_general(
        rows, kernel, (((1,), (1,)), ((), ())), preferred_element_type=jnp.float32
    )
    return final_result.reshape(upstream_gradient.shape[:3] + (kernel.shape[0],))


def group_totals(leading_part, trailing_part, active_flags, split_point):
    leading_cells = jnp.sum(active_flags * leading_part, axis=(0, 1))
    trailing_cells = jnp.sum(active_flags * trailing_part, axis=(0, 1))
    first_groups = jnp.stack(
        [jnp.sum(leading_cells[:split_point], axis=0), jnp.sum(leading_cells[split_point:], axis=0)]
    )
    second_groups = jnp.stack(
        [
            jnp.sum(trailing_cells[:split_point], axis=0),
            jnp.sum(trailing_cells[split_point:], axis=0),
        ]
    )
    return (first_groups, second_groups)


def per_cell(stat, split_point, cells):
    channels = stat.shape[1]
    return jnp.concatenate(
        [
            jnp.broadcast_to(stat[0], (split_point, channels)),
            jnp.broadcast_to(stat[1], (cells - split_point, channels)),
        ],
        axis=0,
    )


def norm_forward_pass(
    input_value, active_flags, split_point, grand_totals, norm_gain_vector, norm_shift_bias
):
    running_sums, squared_values = group_totals(
        input_value, input_value * input_value, active_flags, split_point
    )
    running_sums, squared_values = lax.psum((running_sums, squared_values), ("batch", "tm"))
    mean = running_sums / grand_totals[:, None]
    scale = lax.rsqrt(squared_values / grand_totals[:, None] - mean * mean + NORM_EPS)
    cells = input_value.shape[2]
    cell_scale = per_cell(scale, split_point, cells)
    normalized_values = (input_value - per_cell(mean, split_point, cells)) * cell_scale
    return (normalized_values * norm_gain_vector + norm_shift_bias, normalized_values, cell_scale)


def norm_reverse_pass(
    upstream_gradient,
    normalized_values,
    cell_scale,
    norm_gain_vector,
    active_flags,
    split_point,
    grand_totals,
):
    running_sums, cross_product = group_totals(
        upstream_gradient, upstream_gradient * normalized_values, active_flags, split_point
    )
    running_sums, cross_product = lax.psum((running_sums, cross_product), ("batch", "tm"))
    cells = upstream_gradient.shape[2]
    upstream_average = per_cell(running_sums / grand_totals[:, None], split_point, cells)
    cross_average = per_cell(cross_product / grand_totals[:, None], split_point, cells)
    final_result = (
        active_flags
        * (norm_gain_vector * cell_scale)
        * (upstream_gradient - upstream_average - normalized_values * cross_average)
    )
    return (final_result, jnp.sum(cross_product, axis=0), jnp.sum(running_sums, axis=0))


def reduce_weight(pairs, depth, width):
    total = jnp.zeros((depth // lax.axis_size("tm") * lax.axis_size("tm"), width), jnp.float32)
    for left, right in pairs:
        total = total + lax.dot_general(
            left, right, (((0,), (0,)), ((), ())), preferred_element_type=jnp.float32
        )
    shared = lax.psum_scatter(total.astype(jnp.bfloat16), "tm", scatter_dimension=0, tiled=True)
    return lax.psum_scatter(shared, "batch", scatter_dimension=1, tiled=True).astype(jnp.float32)


def own_square(shard):
    local = jnp.sum(shard * shard)
    return local


def adamw(weight, gradient, momentum, variance, factor, rate, decay):
    clipped = gradient * factor
    new_momentum = BETA_ONE * momentum + (1.0 - BETA_ONE) * clipped
    new_variance = BETA_TWO * variance + (1.0 - BETA_TWO) * clipped * clipped
    corrected = new_momentum / (1.0 - BETA_ONE**STEP)
    spread = jnp.sqrt(new_variance / (1.0 - BETA_TWO**STEP))
    new_weight = weight - rate * (corrected / (spread + ADAM_EPS) + decay * weight)
    return (new_weight, new_momentum, new_variance)


def plain_body(
    x_small,
    x_large,
    small_output_gradient,
    large_output_gradient,
    clip_counts,
    first_spatial,
    first_temporal,
    second_spatial,
    second_temporal,
    norm_params,
    first_spatial_momentum,
    first_temporal_momentum,
    second_spatial_momentum,
    second_temporal_momentum,
    norm_momentum,
    first_spatial_variance,
    first_temporal_variance,
    second_spatial_variance,
    second_temporal_variance,
    norm_variance,
):
    low_one = first_spatial.astype(jnp.bfloat16)
    low_two = first_temporal.astype(jnp.bfloat16)
    low_three = second_spatial.astype(jnp.bfloat16)
    low_four = second_temporal.astype(jnp.bfloat16)
    columns = (
        lax.all_gather(low_one, "batch", axis=1, tiled=True),
        lax.all_gather(low_two, "batch", axis=1, tiled=True),
        lax.all_gather(low_three, "batch", axis=1, tiled=True),
        lax.all_gather(low_four, "batch", axis=1, tiled=True),
    )
    spatial_one, temporal_one, spatial_two, temporal_two = (
        lax.all_gather(columns[0], "tm", axis=0, tiled=True),
        lax.all_gather(columns[1], "tm", axis=0, tiled=True),
        lax.all_gather(columns[2], "tm", axis=0, tiled=True),
        lax.all_gather(columns[3], "tm", axis=0, tiled=True),
    )
    clips = x_small.shape[0]
    split_point = x_small.shape[2]
    large_cells = x_large.shape[2]
    batch_index = lax.axis_index("batch")
    slots = jnp.arange(clips, dtype=jnp.int32)
    live_small = (slots < clip_counts[0, batch_index]).astype(jnp.float32)
    live_large = (slots < clip_counts[1, batch_index]).astype(jnp.float32)
    active_flags = jnp.concatenate(
        [
            jnp.broadcast_to(live_small[:, None, None, None], (clips, 1, split_point, 1)),
            jnp.broadcast_to(live_large[:, None, None, None], (clips, 1, large_cells, 1)),
        ],
        axis=2,
    )
    frames_total = x_small.shape[1] * lax.axis_size("tm")
    grand_totals = jnp.stack(
        [
            jnp.sum(clip_counts[0]).astype(jnp.float32) * frames_total * split_point,
            jnp.sum(clip_counts[1]).astype(jnp.float32) * frames_total * large_cells,
        ]
    )
    bounds = (0, MID, MID + D, 2 * MID + D, 2 * MID + 2 * D)
    gain_vectors = [norm_params[0, bounds[index] : bounds[index + 1]] for index in range(4)]
    bias_vectors = [norm_params[1, bounds[index] : bounds[index + 1]] for index in range(4)]
    first_convolved, taps_one_small, taps_one_large = spatial_forward(x_small, x_large, spatial_one)
    hidden_one, normed_one, scale_one = norm_forward_pass(
        first_convolved, active_flags, split_point, grand_totals, gain_vectors[0], bias_vectors[0]
    )
    act_one = jax.nn.silu(hidden_one).astype(jnp.bfloat16)
    second_convolved, rows_two = temporal_forward(act_one, temporal_one)
    hidden_two, normed_two, scale_two = norm_forward_pass(
        second_convolved, active_flags, split_point, grand_totals, gain_vectors[1], bias_vectors[1]
    )
    act_two = jax.nn.silu(hidden_two).astype(jnp.bfloat16)
    third_convolved, taps_three_small, taps_three_large = spatial_forward(
        act_two[:, :, :split_point], act_two[:, :, split_point:], spatial_two
    )
    hidden_three, normed_three, scale_three = norm_forward_pass(
        third_convolved, active_flags, split_point, grand_totals, gain_vectors[2], bias_vectors[2]
    )
    act_three = jax.nn.silu(hidden_three).astype(jnp.bfloat16)
    fourth_convolved, rows_four = temporal_forward(act_three, temporal_two)
    hidden_four, fourth_normalized, fourth_scale = norm_forward_pass(
        fourth_convolved, active_flags, split_point, grand_totals, gain_vectors[3], bias_vectors[3]
    )
    residual_in = jnp.concatenate([x_small, x_large], axis=2).astype(jnp.float32)
    output_preactivation = hidden_four + residual_in
    block_output = active_flags * jax.nn.silu(output_preactivation)
    upstream_gradient = (
        jnp.concatenate([small_output_gradient, large_output_gradient], axis=2).astype(jnp.float32)
        * active_flags
    )
    passed_gradient = upstream_gradient * silu_slope(output_preactivation)
    squared_values = []
    grad_conv_four, gain_four, bias_four = norm_reverse_pass(
        passed_gradient,
        fourth_normalized,
        fourth_scale,
        gain_vectors[3],
        active_flags,
        split_point,
        grand_totals,
    )
    grad_conv_four = grad_conv_four.astype(jnp.bfloat16)
    rows_grad_four = grad_conv_four.reshape(-1, grad_conv_four.shape[-1])
    grad_second_temporal = reduce_weight(
        [(rows_four, rows_grad_four)], rows_four.shape[1], rows_grad_four.shape[1]
    )
    squared_values.append(own_square(grad_second_temporal))
    grad_act_three = temporal_backward(grad_conv_four, temporal_two)
    grad_conv_three, gain_three, bias_three = norm_reverse_pass(
        grad_act_three * silu_slope(hidden_three),
        normed_three,
        scale_three,
        gain_vectors[2],
        active_flags,
        split_point,
        grand_totals,
    )
    grad_conv_three = grad_conv_three.astype(jnp.bfloat16)
    rows_three_small = grad_conv_three[:, :, :split_point].reshape(-1, grad_conv_three.shape[-1])
    rows_three_large = grad_conv_three[:, :, split_point:].reshape(-1, grad_conv_three.shape[-1])
    grad_second_spatial = reduce_weight(
        [(taps_three_small, rows_three_small), (taps_three_large, rows_three_large)],
        taps_three_small.shape[1],
        rows_three_small.shape[1],
    )
    squared_values.append(own_square(grad_second_spatial))
    channels_mid = act_two.shape[-1]
    grad_act_two = jnp.concatenate(
        [
            spatial_backward(
                rows_three_small,
                spatial_two,
                (clips, act_two.shape[1], split_point, channels_mid),
                HS,
            ),
            spatial_backward(
                rows_three_large,
                spatial_two,
                (clips, act_two.shape[1], large_cells, channels_mid),
                HL,
            ),
        ],
        axis=2,
    )
    grad_conv_two, gain_two, bias_two = norm_reverse_pass(
        grad_act_two * silu_slope(hidden_two),
        normed_two,
        scale_two,
        gain_vectors[1],
        active_flags,
        split_point,
        grand_totals,
    )
    grad_conv_two = grad_conv_two.astype(jnp.bfloat16)
    rows_grad_two = grad_conv_two.reshape(-1, grad_conv_two.shape[-1])
    grad_first_temporal = reduce_weight(
        [(rows_two, rows_grad_two)], rows_two.shape[1], rows_grad_two.shape[1]
    )
    squared_values.append(own_square(grad_first_temporal))
    grad_act_one = temporal_backward(grad_conv_two, temporal_one)
    grad_conv_one, gain_one, bias_one = norm_reverse_pass(
        grad_act_one * silu_slope(hidden_one),
        normed_one,
        scale_one,
        gain_vectors[0],
        active_flags,
        split_point,
        grand_totals,
    )
    grad_conv_one = grad_conv_one.astype(jnp.bfloat16)
    rows_one_small = grad_conv_one[:, :, :split_point].reshape(-1, grad_conv_one.shape[-1])
    rows_one_large = grad_conv_one[:, :, split_point:].reshape(-1, grad_conv_one.shape[-1])
    grad_first_spatial = reduce_weight(
        [(taps_one_small, rows_one_small), (taps_one_large, rows_one_large)],
        taps_one_small.shape[1],
        rows_one_small.shape[1],
    )
    squared_values.append(own_square(grad_first_spatial))
    input_small = passed_gradient[:, :, :split_point] + spatial_backward(
        rows_one_small, spatial_one, x_small.shape, HS
    )
    input_large = passed_gradient[:, :, split_point:] + spatial_backward(
        rows_one_large, spatial_one, x_large.shape, HL
    )
    grad_params = jnp.stack(
        [
            jnp.concatenate([gain_one, gain_two, gain_three, gain_four]),
            jnp.concatenate([bias_one, bias_two, bias_three, bias_four]),
        ]
    )
    summed = lax.psum(
        (squared_values[0], squared_values[1], squared_values[2], squared_values[3]),
        ("batch", "tm"),
    )
    weight_square = summed[0] + summed[1] + summed[2] + summed[3]
    grad_norm = jnp.sqrt(weight_square + jnp.sum(grad_params * grad_params))
    factor = THRESHOLD / jnp.maximum(grad_norm, THRESHOLD)
    one = adamw(
        first_spatial,
        grad_first_spatial,
        first_spatial_momentum,
        first_spatial_variance,
        factor,
        WEIGHT_RATE,
        WEIGHT_DECAY,
    )
    two = adamw(
        first_temporal,
        grad_first_temporal,
        first_temporal_momentum,
        first_temporal_variance,
        factor,
        WEIGHT_RATE,
        WEIGHT_DECAY,
    )
    three = adamw(
        second_spatial,
        grad_second_spatial,
        second_spatial_momentum,
        second_spatial_variance,
        factor,
        WEIGHT_RATE,
        WEIGHT_DECAY,
    )
    four = adamw(
        second_temporal,
        grad_second_temporal,
        second_temporal_momentum,
        second_temporal_variance,
        factor,
        WEIGHT_RATE,
        WEIGHT_DECAY,
    )
    norms = adamw(norm_params, grad_params, norm_momentum, norm_variance, factor, NORM_RATE, 0.0)
    return (
        block_output[:, :, :split_point],
        block_output[:, :, split_point:],
        input_small,
        input_large,
        grad_norm,
        one[0],
        one[1],
        one[2],
        two[0],
        two[1],
        two[2],
        three[0],
        three[1],
        three[2],
        four[0],
        four[1],
        four[2],
        norms[0],
        norms[1],
        norms[2],
    )


BF = jnp.bfloat16
F32 = jnp.float32
MESH_ID = pl.DeviceIdType.MESH
NT_DIMS = (((1,), (1,)), ((), ()))
NN_DIMS = (((1,), (0,)), ((), ()))
UP, DOWN, ACROSS, ALONG, TWIN = range(5)


class Place:
    def __init__(self, batches, slots):
        self.batches, self.slots = batches, slots
        self.z = lax.axis_index("batch")
        self.t = lax.axis_index("tm")
        self.core = lax.rem(self.t, 2)
        self.slab = self.t // 2
        self.slabs = slots // 2
        side = lax.rem(self.slab, 2)
        deep = self.slab // 2
        self.side_slab = deep * 2 + (1 - side)
        self.deep_slab = (1 - deep) * 2 + side
        self.far_slab = (1 - deep) * 2 + (1 - side)
        self.rel = (self.slab, self.side_slab, self.deep_slab, self.far_slab)
        self.twin = self.t + 1 - 2 * self.core

    def device(self, way):
        if way == UP:
            return (self.z + 1, self.t)
        if way == DOWN:
            return (self.z - 1, self.t)
        if way == ACROSS:
            return (self.z, self.side_slab * 2 + self.core)
        if way == ALONG:
            return (self.z, self.deep_slab * 2 + self.core)
        return (self.z, self.twin)

    def greet(self):
        barrier = pltpu.get_barrier_semaphore()
        for step in range(1, self.slots):
            pl.semaphore_signal(
                barrier, inc=1, device_id=(self.z, lax.rem(self.t + step, self.slots)),
                device_id_type=MESH_ID,
            )
        for step in range(1, self.batches):
            pl.semaphore_signal(
                barrier, inc=1, device_id=(lax.rem(self.z + step, self.batches), self.t),
                device_id_type=MESH_ID,
            )
        pl.semaphore_wait(barrier, self.slots + self.batches - 2)


def send(src, dst, send_sem, recv_sem, device):
    return pltpu.make_async_remote_copy(
        src_ref=src, dst_ref=dst, send_sem=send_sem, recv_sem=recv_sem,
        device_id=device, device_id_type=MESH_ID,
    )


class Totals:
    def __init__(self, place, rows, planes, lines, sems):
        self.place, self.rows, self.planes, self.lines = place, rows, planes, lines
        self.plane_send, self.plane_recv, self.line_send, self.line_recv = sems

    def run(self, n, value):
        p = self.place
        width = value.shape[1]
        plane, line = self.planes.at[n], self.lines.at[n]
        plane[p.t, :, :width] = value

        def plane_copy(step):
            to = lax.rem(p.t + step, p.slots)
            ref = plane.at[p.t, :, pl.ds(0, width)]
            return send(ref, ref, self.plane_send.at[n, step], self.plane_recv.at[n, p.t], (p.z, to))

        def plane_wait(step):
            origin = lax.rem(p.t + p.slots - step, p.slots)
            ref = plane.at[origin, :, pl.ds(0, width)]
            send(ref, ref, self.plane_send.at[n, step], self.plane_recv.at[n, origin], (p.z, p.twin)).wait_recv()

        for step in range(1, p.slots):
            plane_copy(step).start()
        for step in range(1, p.slots):
            plane_wait(step)
        total = plane[0, :, :width]
        for slot in range(1, p.slots):
            total = total + plane[slot, :, :width]
        line[p.z, :, :width] = total

        def line_copy(step):
            to = lax.rem(p.z + step, p.batches)
            ref = line.at[p.z, :, pl.ds(0, width)]
            return send(ref, ref, self.line_send.at[n, step], self.line_recv.at[n, p.z], (to, p.t))

        def line_wait(step):
            origin = lax.rem(p.z + p.batches - step, p.batches)
            ref = line.at[origin, :, pl.ds(0, width)]
            send(ref, ref, self.line_send.at[n, step], self.line_recv.at[n, origin], (p.z, p.twin)).wait_recv()

        for step in range(1, p.batches):
            line_copy(step).start()
        for step in range(1, p.batches):
            line_wait(step)
        total = line[0, :, :width]
        for slot in range(1, p.batches):
            total = total + line[slot, :, :width]
        for step in range(1, p.slots):
            plane_copy(step).wait_send()
        for step in range(1, p.batches):
            line_copy(step).wait_send()
        return total


class Gather:
    def __init__(self, place, index, own, whole, block, sems):
        self.p, self.n, self.own, self.whole, self.block = place, index, own, whole, block
        self.send_sem, self.recv_sem, self.twin_sem = sems

    def copy(self, way, rel, batch, src=None):
        p = self.p
        core = p.core
        dst = self.whole.at[self.block(p.rel[rel], core, batch)]
        there = {ACROSS: {0: 1, 2: 3}, ALONG: {0: 2, 1: 3}}.get(way, {}).get(rel, rel)
        sem = self.twin_sem if way == TWIN else self.recv_sem
        return send(
            dst if src is None else src, dst, self.send_sem.at[self.n, way, rel, batch],
            sem.at[self.n, there, batch], p.device(way),
        )

    def wait(self, rel, batch, twin=False):
        p = self.p
        core = 1 - p.core if twin else p.core
        ref = self.whole.at[self.block(p.rel[rel], core, batch)]
        sem = self.twin_sem if twin else self.recv_sem
        send(ref, ref, self.send_sem.at[self.n, TWIN, rel, batch], sem.at[self.n, rel, batch],
             p.device(TWIN)).wait_recv()

    def at(self, k, fn):
        p = self.p
        if k == 0:
            fn(p.z)
            return
        pl.when(p.z - k >= 0)(lambda: fn(p.z - k))
        pl.when(p.z + k < p.batches)(lambda: fn(p.z + k))

    def start(self):
        p = self.p
        pl.when(p.z < p.batches - 1)(lambda: self.copy(UP, 0, p.z, self.own).start())
        pl.when(p.z > 0)(lambda: self.copy(DOWN, 0, p.z, self.own).start())
        for way in (ACROSS, ALONG, TWIN):
            self.copy(way, 0, p.z, self.own).start()

    def hop(self, k):
        p = self.p

        def below(b):
            self.wait(0, b)
            pl.when(p.z < p.batches - 1)(lambda: self.copy(UP, 0, b).start())
            for way in (ACROSS, ALONG, TWIN):
                self.copy(way, 0, b).start()

        def above(b):
            self.wait(0, b)
            pl.when(p.z > 0)(lambda: self.copy(DOWN, 0, b).start())
            for way in (ACROSS, ALONG, TWIN):
                self.copy(way, 0, b).start()

        pl.when(p.z - k >= 0)(lambda: below(p.z - k))
        pl.when(p.z + k < p.batches)(lambda: above(p.z + k))

    def plane(self, k):
        half = self.p.batches // 2

        def one(b):
            self.wait(1, b)
            pl.when(b < half)(lambda: self.copy(ALONG, 1, b).start())
            self.copy(TWIN, 1, b).start()
            self.wait(2, b)
            pl.when(b >= half)(lambda: self.copy(ACROSS, 2, b).start())
            self.copy(TWIN, 2, b).start()

        self.at(k, one)

    def far(self, k):
        def one(b):
            self.wait(3, b)
            self.copy(TWIN, 3, b).start()

        self.at(k, one)

    def twins(self, rel):
        def body(b, _):
            self.wait(rel, b, twin=True)
            return 0

        lax.fori_loop(0, self.p.batches, body, 0)

    def steps(self):
        batches = self.p.batches
        order = [self.start]
        for k in range(batches):
            if k:
                order.append(functools.partial(self.hop, k))
                order.append(functools.partial(self.far, k - 1))
            order.append(functools.partial(self.plane, k))
        order.append(functools.partial(self.far, batches - 1))
        return order

    def finish(self):
        p = self.p
        half = p.batches // 2

        def body(b, _):
            pl.when((b <= p.z) & (p.z < p.batches - 1))(lambda: self.copy(UP, 0, b, self.own).wait_send())
            pl.when((b >= p.z) & (p.z > 0))(lambda: self.copy(DOWN, 0, b, self.own).wait_send())
            for way in (ACROSS, ALONG):
                self.copy(way, 0, b, self.own).wait_send()
            for rel in range(4):
                self.copy(TWIN, rel, b, self.own).wait_send()
            pl.when(b < half)(lambda: self.copy(ALONG, 1, b, self.own).wait_send())
            pl.when(b >= half)(lambda: self.copy(ACROSS, 2, b, self.own).wait_send())
            return 0

        lax.fori_loop(0, p.batches, body, 0)


def sigmoid(v):
    return 0.5 * jnp.tanh(0.5 * v) + 0.5


class Shape:
    def __init__(self, x_small, x_large, batches, slots):
        self.clips = x_small[0]
        self.cells = (x_small[2], x_large[2])
        self.sides = (math.isqrt(x_small[2]), math.isqrt(x_large[2]))
        self.d = x_small[3]
        self.padded = tuple(n + n % 2 for n in self.cells)
        self.rows = tuple(n * self.clips for n in self.padded)
        self.m = sum(self.rows)
        self.mid = MID
        self.k = 9 * self.d
        self.batches, self.slots = batches, slots
        self.slabs = slots // 2
        self.kw = self.k // self.slabs
        self.nb = self.mid // (2 * batches)
        self.ur = 3 * self.mid // slots
        self.uc = self.d // batches


def fits(x_small, x_large, batches, slots):
    s = Shape(x_small, x_large, batches, slots)
    return (
        s.clips == 8 and x_small[1] == 1 and slots == 8 and batches >= 2 and batches % 2 == 0
        and all(side * side == cells for side, cells in zip(s.sides, s.cells))
        and all(r % 80 == 0 for r in s.rows)
        and s.kw % 128 == 0 and s.mid % (32 * batches) == 0 and s.ur % 16 == 0 and s.uc % 128 == 0
    )


def chunks(s, size, fn, carry=None, unroll=1):
    out = []
    base = 0
    for group, rows in enumerate(s.rows):
        def body(i, c, group=group, base=base):
            return fn(group, pl.multiple_of(base + i * size, size if base % size == 0 else 16), c)

        out.append(lax.fori_loop(0, rows // size, body, carry if carry is not None else 0, unroll=unroll))
        base += rows
    return out


def sums_of(s, load, live, width):
    def body(group, r0, c):
        values = load(group, r0, 80)
        return tuple(t + jnp.sum(v.reshape(10, 8, width), axis=0) for t, v in zip(c, values))

    zero = jnp.zeros((8, width), F32)
    small, large = chunks(s, 80, body, (zero, zero))
    rows = [jnp.sum(v * live[g], axis=0, keepdims=True) for v, g in
            ((small[0], 0), (large[0], 1), (small[1], 0), (large[1], 1))]
    return jnp.concatenate(rows, axis=0)


def build_taps(s, grids, taps):
    pieces = []
    for tap in range(9):
        lo = tap * s.d
        end = lo + s.d
        while lo < end:
            hi = min(end, (lo // s.kw + 1) * s.kw)
            pieces.append((tap, lo - tap * s.d, lo // s.kw, lo % s.kw, hi - lo))
            lo = hi
    base = 0
    for group in range(2):
        side, cells = s.sides[group], s.cells[group]
        grid = grids[group]
        for tap, channel, slab, lane, width in pieces:
            i, j = tap // 3, tap % 3
            if side % 2 == 0:
                n = 2 * side * 8

                def body(r, _):
                    window = grid[pl.ds(i + 2 * r, 2), j : j + side, :, channel : channel + width]
                    taps[slab, pl.ds(pl.multiple_of(base + r * n, 16), n), lane : lane + width] = (
                        window.reshape(n, width).astype(BF)
                    )
                    return 0

                lax.fori_loop(0, side // 2, body, 0)
            else:
                window = grid[i : i + side, j : j + side, :, channel : channel + width]
                window = window.reshape(cells * 8, width)
                window = jnp.concatenate(
                    [window, jnp.zeros((s.rows[group] - cells * 8, width), F32)], axis=0
                ) if s.rows[group] > cells * 8 else window
                taps[slab, base : base + s.rows[group], lane : lane + width] = window.astype(BF)
        base += s.rows[group]


def fill_grid(s, grids, group, cell, value):
    side = s.sides[group]
    grids[group][1 + cell // side, 1 + lax.rem(cell, side)] = value


def zero_padding(s, ref, width):
    base = 0
    for group in range(2):
        base += s.rows[group]
        spare = (s.padded[group] - s.cells[group]) * s.clips
        if spare:
            size = -(-spare // 16) * 16
            keep = lax.broadcasted_iota(jnp.int32, (size, width), 0) < size - spare
            value = ref[base - size : base, :].astype(F32)
            ref[base - size : base, :] = jnp.where(keep, value, 0.0).astype(ref.dtype)


def grid_of_rows(s, grids, group, r0, value):
    side = s.sides[group]
    base = 0 if group == 0 else s.rows[0]
    first = (r0 - base) // 8
    split = value.reshape(10, 8, s.d)
    for n in range(10):
        cell = first + n
        grids[group][1 + cell // side, 1 + lax.rem(cell, side)] = split[n]


def clear_pad_cells(s, grids):
    for group in range(2):
        side = s.sides[group]
        for cell in range(s.cells[group], s.padded[group]):
            grids[group][1 + cell // side, 1 + cell % side] = jnp.zeros((8, s.d), F32)


def moments(total, inverse, width):
    mean = [total[g : g + 1, :] * inverse[g] for g in range(2)]
    scale = [
        lax.rsqrt(total[2 + g : 3 + g, :] * inverse[g] - mean[g] * mean[g] + NORM_EPS) for g in range(2)
    ]
    return mean, scale


def wide_cuts(width):
    half = -(-width // 256) * 128
    return ((0, half), (half, width - half))


def forward_kernel(s, *refs):
    (x, grad, sw1, uw1, sw2, uw2, norm, live_ref, inverse,
     gs1, gu1, gs2, gu2, taps1_o, taps2_o, xh1_o, xh2_o, xh3_o, xh4_o, z1_o, z3_o, out, dpre,
     r1_o, r2_o, r3_o, r4_o, last_o,
     tb1, tb2, own1, own2, wb, wub, taps, a, z, grid_s, grid_l, b, hs, hr, planes, lines,
     ag_send, ag_recv, ag_twin, tb_send, tb_recv, local, load, hs_send, hs_recv,
     pl_send, pl_recv, ln_send, ln_recv) = refs
    p = Place(s.batches, s.slots)
    live = [live_ref[g] for g in range(2)]
    inv = [inverse[g] for g in range(2)]
    totals = Totals(p, 4, planes, lines, (pl_send, pl_recv, ln_send, ln_recv))
    d, mid = s.d, s.mid
    bounds = (0, mid, mid + d, 2 * mid + d, 2 * mid + 2 * d)

    def gain_bias(n):
        return norm[0:1, bounds[n] : bounds[n + 1]], norm[1:2, bounds[n] : bounds[n + 1]]

    p.greet()

    def twin_copy(n, src, dst):
        return send(
            src.at[1 - p.core], dst.at[pl.ds(pl.multiple_of(p.core * (s.kw // 2), 16), s.kw // 2)],
            tb_send.at[n], tb_recv.at[n], p.device(TWIN),
        )

    def twin_wait(n, src, dst):
        send(
            src.at[1 - p.core], dst.at[pl.ds(pl.multiple_of((1 - p.core) * (s.kw // 2), 16), s.kw // 2)],
            tb_send.at[n], tb_recv.at[n], p.device(TWIN),
        ).wait_recv()

    for n, src, dst in ((0, sw1, tb1), (1, sw2, tb2)):
        twin_copy(n, src, dst).start()
        dst[pl.ds(pl.multiple_of(p.core * (s.kw // 2), 16), s.kw // 2)] = src[p.core]

    def s_block(slab, core, batch):
        return (slab, pl.ds(pl.multiple_of((batch * 2 + core) * s.nb, 16), s.nb))

    def u_block(slab, core, batch):
        return (pl.ds(pl.multiple_of((slab * 2 + core) * s.ur, 16), s.ur),
                pl.ds(pl.multiple_of(batch * s.uc, 128), s.uc))

    sems = (ag_send, ag_recv, ag_twin)
    gather = [
        Gather(p, 0, own1, gs1, s_block, sems),
        Gather(p, 1, uw1, gu1, u_block, sems),
        Gather(p, 2, own2, gs2, s_block, sems),
        Gather(p, 3, uw2, gu2, u_block, sems),
    ]

    def keep_own(n):
        g = gather[n]
        return pltpu.make_async_copy(g.own, g.whole.at[g.block(p.slab, p.core, p.z)], local.at[n])

    twin_wait(0, sw1, tb1)
    own1[...] = tb1[...].T
    queue = [(0, step) for step in gather[0].steps()]
    queue.pop(0)[1]()
    keep_own(0).start()
    twin_wait(1, sw2, tb2)
    own2[...] = tb2[...].T
    keep_own(1).start()
    keep_own(2).start()
    keep_own(3).start()
    for n in (1, 2, 3):
        queue += [(n, step) for step in gather[n].steps()]

    def tick(count):
        for _ in range(count):
            if queue:
                queue.pop(0)[1]()

    def flush(n):
        while queue and queue[0][0] <= n:
            queue.pop(0)[1]()

    for side, edge in ((0, 0), (1, p.slots - 1)):
        @pl.when(p.t == edge)
        def _(side=side):
            hr[side] = jnp.zeros(hr.shape[1:], BF)

    grids = (grid_s, grid_l)
    for grid in grids:
        def clear(i, _, grid=grid):
            grid[i] = jnp.zeros(grid.shape[1:], F32)
            return 0

        lax.fori_loop(0, grid.shape[0], clear, 0)

    def x_rows(group, r0, c):
        grid_of_rows(s, grids, group, r0, x[pl.ds(r0, 80), :].astype(F32))
        return c

    chunks(s, 80, x_rows)
    clear_pad_cells(s, grids)
    build_taps(s, grids, taps)
    taps_copy = pltpu.make_async_copy(taps, taps1_o, local.at[4])
    taps_copy.start()

    def slab_load(whole, rel):
        return pltpu.make_async_copy(whole.at[p.rel[rel]], wb.at[rel], load.at[rel])

    def conv_slab(rel):
        for lo, width in wide_cuts(mid):
            y = lax.dot_general(taps[p.rel[rel]], wb[rel, lo : lo + width, :], NT_DIMS, preferred_element_type=F32)
            if rel == 0:
                a[:, lo : lo + width] = y
            else:
                a[:, lo : lo + width] += y

    def spatial(n, whole, spare):
        g = gather[n]
        while queue and queue[0][0] <= n and len([q for q in queue if q[0] <= n]) > 1:
            queue.pop(0)[1]()
        g.twins(0)
        if n == 0:
            keep_own(0).wait()
        else:
            keep_own(2).wait()
        slab_load(whole, 0).start()
        g.twins(1)
        slab_load(whole, 1).start()
        g.twins(2)
        slab_load(whole, 2).start()
        slab_load(whole, 0).wait()
        conv_slab(0)
        flush(n)
        g.twins(3)
        slab_load(whole, 3).start()
        for rel in (1, 2, 3):
            tick(spare)
            slab_load(whole, rel).wait()
            conv_slab(rel)

    def stats(load_rows, width):
        return sums_of(s, load_rows, live, width)

    def wide_norm(index, n, zo, xo, ro, sem):
        def load_rows(group, r0, size):
            v = a[pl.ds(r0, size), :]
            return v, v * v

        total = totals.run(index, stats(load_rows, mid))
        mean, scale = moments(total, inv, mid)
        ro[...] = jnp.concatenate(scale, axis=0)
        gain, bias = gain_bias(n)

        def rows(group, r0, c):
            xhat = (a[pl.ds(r0, 16), :] - mean[group]) * scale[group]
            a[pl.ds(r0, 16), :] = xhat
            h = xhat * gain + bias
            z[pl.ds(r0, 16), :] = (h * sigmoid(h)).astype(BF)
            return c

        chunks(s, 16, rows)
        zero_padding(s, z, mid)
        xc = pltpu.make_async_copy(a, xo, local.at[sem])
        zc = pltpu.make_async_copy(z, zo, local.at[sem + 1])
        xc.start()
        zc.start()
        return xc, zc

    def u_load(n, whole):
        return pltpu.make_async_copy(whole, wub, load.at[4 + n])

    def halo(n, side):
        to = p.t + 1 if side == 0 else p.t - 1
        return send(hs.at[side], hr.at[side], hs_send.at[n, side], hs_recv.at[n, side], (p.z, to))

    def temporal(n, index, between):
        flush(index)
        for rel in range(4):
            gather[index].twins(rel)
        keep_own(index).wait()
        load_w = u_load(n, gather[index].whole)
        load_w.start()
        load_w.wait()
        hs[0] = jnp.dot(z[...], wub[:mid, :], preferred_element_type=F32).astype(BF)
        pl.when(p.t < p.slots - 1)(lambda: halo(n, 0).start())
        hs[1] = jnp.dot(z[...], wub[2 * mid :, :], preferred_element_type=F32).astype(BF)
        pl.when(p.t > 0)(lambda: halo(n, 1).start())
        b[...] = jnp.dot(z[...], wub[mid : 2 * mid, :], preferred_element_type=F32)
        between()
        pl.when(p.t > 0)(lambda: halo(n, 0).wait_recv())
        pl.when(p.t < p.slots - 1)(lambda: halo(n, 1).wait_recv())

    def narrow_total(index):
        def load_rows(group, r0, size):
            v = b[pl.ds(r0, size), :] + hr[0, pl.ds(r0, size), :].astype(F32) + hr[1, pl.ds(r0, size), :].astype(F32)
            b[pl.ds(r0, size), :] = v
            return v, v * v

        return totals.run(index, stats(load_rows, d))

    def halo_done(n):
        pl.when(p.t < p.slots - 1)(lambda: halo(n, 0).wait_send())
        pl.when(p.t > 0)(lambda: halo(n, 1).wait_send())

    spatial(0, gs1, 4)
    tick(1)
    xc1, zc1 = wide_norm(0, 0, z1_o, xh1_o, r1_o, 5)
    tick(2)
    temporal(0, 1, lambda: tick(2))
    total = narrow_total(1)
    tick(1)
    mean2, scale2 = moments(total, inv, d)
    r2_o[...] = jnp.concatenate(scale2, axis=0)
    gain2, bias2 = gain_bias(1)

    def second(group, r0, c):
        xhat = (b[pl.ds(r0, 80), :] - mean2[group]) * scale2[group]
        b[pl.ds(r0, 80), :] = xhat
        h = xhat * gain2 + bias2
        grid_of_rows(s, grids, group, r0, (h * sigmoid(h)).astype(BF).astype(F32))
        return c

    chunks(s, 80, second)
    clear_pad_cells(s, grids)
    xc2 = pltpu.make_async_copy(b, xh2_o, local.at[7])
    xc2.start()
    halo_done(0)
    tick(2)
    taps_copy.wait()
    build_taps(s, grids, taps)
    taps_copy2 = pltpu.make_async_copy(taps, taps2_o, local.at[8])
    taps_copy2.start()
    xc1.wait()
    spatial(2, gs2, 4)
    tick(2)
    zc1.wait()
    xc3, zc3 = wide_norm(2, 2, z3_o, xh3_o, r3_o, 9)
    tick(2)
    xc2.wait()
    temporal(1, 3, lambda: None)
    total = narrow_total(3)
    mean4, scale4 = moments(total, inv, d)
    r4_o[...] = jnp.concatenate(scale4, axis=0)
    gain4, bias4 = gain_bias(3)

    def last(group, r0, c):
        xhat = (b[pl.ds(r0, 80), :] - mean4[group]) * scale4[group]
        b[pl.ds(r0, 80), :] = xhat
        pre = xhat * gain4 + bias4 + x[pl.ds(r0, 80), :].astype(F32)
        gate = sigmoid(pre)
        alive = jnp.broadcast_to(live[group][None], (10, 8, d)).reshape(80, d)
        out[pl.ds(r0, 80), :] = alive * (pre * gate)
        up = alive * grad[pl.ds(r0, 80), :].astype(F32) * (gate * (1.0 + pre * (1.0 - gate)))
        dpre[pl.ds(r0, 80), :] = up
        return c

    chunks(s, 80, last)
    zero_padding(s, dpre, d)
    xc4 = pltpu.make_async_copy(b, xh4_o, local.at[11])
    xc4.start()

    def last_rows(group, r0, size):
        v = dpre[pl.ds(r0, size), :]
        return v, v * b[pl.ds(r0, size), :]

    last_o[...] = totals.run(4, stats(last_rows, d))
    halo_done(1)
    for g in gather:
        g.finish()
    for n, src, dst in ((0, sw1, tb1), (1, sw2, tb2)):
        twin_copy(n, src, dst).wait_send()
    for c in (taps_copy2, zc3, xc3, xc4):
        c.wait()


def forward_call(s, x, grad, sw1, uw1, sw2, uw2, norm, live, inverse):
    any_, vmem, smem = (pl.BlockSpec(memory_space=m) for m in (pl.ANY, pltpu.VMEM, pltpu.SMEM))
    S = jax.ShapeDtypeStruct
    m, d, mid = s.m, s.d, s.mid
    gs = S((s.slabs, mid, s.kw), BF)
    gu = S((3 * mid, d), BF)
    taps = S((s.slabs, m, s.kw), BF)
    wide, narrow = S((m, mid), F32), S((m, d), F32)
    zs = S((m, mid), BF)
    outs = (gs, gu, gs, gu, taps, taps, wide, narrow, wide, narrow, zs, zs, narrow, narrow,
            S((2, mid), F32), S((2, d), F32), S((2, mid), F32), S((2, d), F32), S((4, d), F32))
    specs = (any_,) * 12 + (vmem,) * 7
    dma, V = pltpu.SemaphoreType.DMA, pltpu.VMEM
    nb = s.batches
    n_sums = 5
    scratch = [
        V((s.kw, s.nb), BF), V((s.kw, s.nb), BF), V((s.nb, s.kw), BF), V((s.nb, s.kw), BF),
        V((s.slabs, mid, s.kw), BF), V((3 * mid, d), BF), V((s.slabs, m, s.kw), BF),
        V((m, mid), F32), V((m, mid), BF),
        V((s.sides[0] + 2, s.sides[0] + 2, 8, d), F32), V((s.sides[1] + 2, s.sides[1] + 2, 8, d), F32),
        V((m, d), F32), V((2, m, d), BF), V((2, m, d), BF),
        V((n_sums, s.slots, 4, mid), F32), V((n_sums, nb, 4, mid), F32),
        dma((4, 5, 4, nb)), dma((4, 4, nb)), dma((4, 4, nb)), dma((2,)), dma((2,)), dma((12,)), dma((6,)),
        dma((2, 2)), dma((2, 2)),
        dma((n_sums, s.slots)), dma((n_sums, s.slots)), dma((n_sums, nb)), dma((n_sums, nb)),
    ]
    return pl.pallas_call(
        functools.partial(forward_kernel, s),
        out_shape=outs,
        in_specs=[vmem, vmem, vmem, any_, vmem, any_, vmem, vmem, smem],
        out_specs=specs,
        scratch_shapes=scratch,
        compiler_params=pltpu.CompilerParams(
            collective_id=0, has_side_effects=True, vmem_limit_bytes=63 * 2**20
        ),
        name="forward",
    )(x, grad, sw1, uw1, sw2, uw2, norm, live, inverse)


def cell_major(s, small, large):
    parts = []
    for group, v in enumerate((small, large)):
        v = v.reshape(s.clips, s.cells[group], s.d).transpose(1, 0, 2)
        parts.append(jnp.pad(v, ((0, s.padded[group] - s.cells[group]), (0, 0), (0, 0))))
    return jnp.concatenate(parts, axis=0).reshape(s.m, s.d)


def clip_major(s, v):
    v = v.reshape(-1, s.clips, s.d)
    parts, base = [], 0
    for group in range(2):
        part = v[base : base + s.cells[group]].transpose(1, 0, 2)
        parts.append(part.reshape(s.clips, 1, s.cells[group], s.d))
        base += s.padded[group]
    return parts


def halves(s, w):
    return w.astype(BF).reshape(w.shape[0], 2, s.nb).transpose(1, 0, 2)


def add_into(dst, src, rows, step):
    def body(i, _):
        at = pl.ds(pl.multiple_of(i * step, 16), step)
        dst[at, :] = (dst[at, :].astype(F32) + src[at, :].astype(F32)).astype(BF)
        return 0

    lax.fori_loop(0, rows // step, body, 0)


class Scatter:
    def __init__(self, place, index, part, bufs, cut, rows, step, sems):
        self.p, self.n, self.part, self.cut, self.rows, self.step = place, index, part, cut, rows, step
        self.tr, self.fx, self.fa, self.rx, self.ry, self.ru, self.rd = bufs
        self.twin_s, self.twin_r, self.block_s, self.block_r = sems
        self.half = place.batches // 2

    FAR, SIDE, DEEP, RISE, FALL = range(5)

    def twin_copy(self, rel):
        p = self.p
        return send(self.part(rel, 1 - p.core), self.tr.at[rel], self.twin_s.at[self.n, rel],
                    self.twin_r.at[self.n, rel], p.device(TWIN))

    def block_copy(self, kind, b, src, dst, way):
        return send(src, dst, self.block_s.at[self.n, kind, b], self.block_r.at[self.n, kind, b],
                    self.p.device(way))

    def own(self, rel, b):
        return self.cut(self.part(rel, self.p.core), b)

    def far_copy(self, b):
        if b < self.half:
            return self.block_copy(self.FAR, b, self.own(3, b), self.cut(self.fx, b), ACROSS)
        return self.block_copy(self.FAR, b, self.own(3, b), self.cut(self.fa, b - self.half), ALONG)

    def side_copy(self, b):
        return self.block_copy(self.SIDE, b, self.own(1, b), self.cut(self.rx, b), ACROSS)

    def deep_copy(self, b):
        return self.block_copy(self.DEEP, b, self.own(2, b), self.cut(self.ry, b), ALONG)

    def rise_copy(self, b):
        return self.block_copy(self.RISE, b, self.own(0, b), self.cut(self.ru, b), UP)

    def fall_copy(self, b):
        return self.block_copy(self.FALL, b, self.own(0, b), self.cut(self.rd, b), DOWN)

    def arrive(self, kind, b, ref):
        self.block_copy(kind, b, ref, ref, TWIN).wait_recv()

    def add(self, dst, src):
        add_into(dst, src, self.rows, self.step)

    def order(self):
        n = self.p.batches
        out = []
        for i in range(n // 2):
            out += [n - 1 - i, i]
        return out

    def twin(self, rel):
        self.twin_copy(rel).start()

    def join(self, rel):
        p = self.p
        self.twin_copy(rel).wait_recv()
        for b in self.order():
            self.add(self.own(rel, b), self.cut(self.tr.at[rel], b))
            if rel == 3:
                self.far_copy(b).start()
            if rel == 1 and b < self.half:
                self.side_copy(b).start()
            if rel == 2 and b >= self.half:
                self.deep_copy(b).start()

    def relay(self, b):
        if b < self.half:
            src = self.cut(self.fx, b)
            self.arrive(self.FAR, b, src)
            self.add(self.own(2, b), src)
            self.deep_copy(b).start()
        else:
            src = self.cut(self.fa, b - self.half)
            self.arrive(self.FAR, b, src)
            self.add(self.own(1, b), src)
            self.side_copy(b).start()

    def collect(self, b):
        for kind, buf in ((self.SIDE, self.rx), (self.DEEP, self.ry)):
            src = self.cut(buf, b)
            self.arrive(kind, b, src)
            self.add(self.own(0, b), src)

    def chain(self, b):
        p = self.p

        @pl.when(p.z < b)
        def _():
            @pl.when(p.z > 0)
            def _():
                self.arrive(self.RISE, b, self.cut(self.ru, b))
                self.add(self.own(0, b), self.cut(self.ru, b))

            self.rise_copy(b).start()

        @pl.when(p.z > b)
        def _():
            @pl.when(p.z < p.batches - 1)
            def _():
                self.arrive(self.FALL, b, self.cut(self.rd, b))
                self.add(self.own(0, b), self.cut(self.rd, b))

            self.fall_copy(b).start()

    def result(self):
        p = self.p
        pl.when(p.z > 0)(lambda: self.arrive(self.RISE, p.z, self.cut(self.ru, p.z)))
        pl.when(p.z < p.batches - 1)(lambda: self.arrive(self.FALL, p.z, self.cut(self.rd, p.z)))

        @pl.when(p.z == 0)
        def _():
            ref = self.cut(self.ru, p.z)
            ref[...] = jnp.zeros(ref.shape, BF)

        @pl.when(p.z == p.batches - 1)
        def _():
            ref = self.cut(self.rd, p.z)
            ref[...] = jnp.zeros(ref.shape, BF)

        return (
            self.own(0, p.z)[...].astype(F32)
            + self.cut(self.ru, p.z)[...].astype(F32)
            + self.cut(self.rd, p.z)[...].astype(F32)
        )

    def sent(self):
        p = self.p
        for rel in range(4):
            self.twin_copy(rel).wait_send()
        for b in range(p.batches):
            self.far_copy(b).wait_send()
            self.side_copy(b).wait_send()
            self.deep_copy(b).wait_send()
            pl.when(p.z < b)(lambda b=b: self.rise_copy(b).wait_send())
            pl.when(p.z > b)(lambda b=b: self.fall_copy(b).wait_send())

    def steps(self):
        part = functools.partial
        out = [part(self.join, rel) for rel in (3, 1, 2, 0)]
        out += [part(self.relay, b) for b in self.order()]
        for b in self.order():
            out += [part(self.collect, b), part(self.chain, b)]
        return out


def rows_of_grid(s, grids, group, r0):
    side = s.sides[group]
    base = 0 if group == 0 else s.rows[0]
    first = (r0 - base) // 8
    cells = [grids[group][1 + (first + n) // side, 1 + lax.rem(first + n, side)] for n in range(10)]
    return jnp.concatenate(cells, axis=0)


def slope(v):
    gate = sigmoid(v)
    return gate * (1.0 + v * (1.0 - gate))


def backward_kernel(s, *refs):
    (gs1, gu1, gs2, gu2, taps1, taps2, xh1, xh2, xh3, xh4, z1, z3, dpre,
     r1, r2, r3, r4, last, norm, live_ref, inverse,
     dx, gsh1, gsh2, guo1, guo2, ng, square,
     ps, tr, fx, fa, rx, ry, ru, rd, pu, utr, ufx, ufa, urx, ury, uru, urd,
     nat, flip, d3, turn, planes, lines,
     load, tap_sem, tile_sem, halo_send, halo_recv, twin_s, twin_r, block_s, block_r, half_s, half_r,
     pl_send, pl_recv, ln_send, ln_recv) = refs
    p = Place(s.batches, s.slots)
    live = [live_ref[g] for g in range(2)]
    inv = [inverse[g] for g in range(2)]
    totals = Totals(p, 4, planes, lines, (pl_send, pl_recv, ln_send, ln_recv))
    d, mid, m = s.d, s.mid, s.m
    bounds = (0, mid, mid + d, 2 * mid + d, 2 * mid + 2 * d)

    def gain_bias(n):
        return norm[0:1, bounds[n] : bounds[n + 1]], norm[1:2, bounds[n] : bounds[n + 1]]

    p.greet()
    queue = []

    def tick(count):
        for _ in range(count):
            if queue:
                queue.pop(0)()

    def flush():
        while queue:
            queue.pop(0)()

    def cut_rows(ref, b):
        at = b * s.nb if isinstance(b, int) else pl.multiple_of(b * s.nb, 16)
        return ref.at[pl.ds(at, s.nb)]

    def cut_lanes(ref, b):
        at = b * s.uc if isinstance(b, int) else pl.multiple_of(b * s.uc, 128)
        return ref.at[:, pl.ds(at, s.uc)]

    def part_s(rel, core):
        return ps.at[rel, core]

    def part_u(rel, core):
        return pu.at[pl.ds(pl.multiple_of((p.rel[rel] * 2 + core) * s.ur, 16), s.ur)]

    sems = (twin_s, twin_r, block_s, block_r)

    def scatter(n):
        if n % 2 == 0:
            return Scatter(p, n, part_s, (tr, fx, fa, rx, ry, ru, rd), cut_rows, s.nb, 48, sems)
        return Scatter(p, n, part_u, (utr, ufx, ufa, urx, ury, uru, urd), cut_lanes, s.ur, 144, sems)

    for side, edge in ((0, p.slots - 1), (2, 0)):
        @pl.when(p.t == edge)
        def _(side=side):
            d3[side] = jnp.zeros(d3.shape[1:], BF)

    def norm_back(n, total, scale, dh, xhat, store, size, width):
        gain, _ = gain_bias(n)
        ng[0:1, bounds[n] : bounds[n + 1]] = total[2:3, :] + total[3:4, :]
        ng[1:2, bounds[n] : bounds[n + 1]] = total[0:1, :] + total[1:2, :]
        lead = [gain * scale[g : g + 1, :] for g in range(2)]
        mean = [total[g : g + 1, :] * inv[g] for g in range(2)]
        cross = [total[2 + g : 3 + g, :] * inv[g] for g in range(2)]

        def rows(group, r0, c):
            at = pl.ds(r0, size)
            v = lead[group] * (dh[at, :] - mean[group] - xhat[at, :] * cross[group])
            v = v.reshape(size // 8, 8, width) * live[group][None]
            store(at, v.reshape(size, width))
            return c

        chunks(s, size, rows)

    def upstream(n, dz, xhat, fetch, size, width):
        gain, bias = gain_bias(n)

        def body(group, r0, c):
            at = pl.ds(r0, size)
            xv = xhat[at, :]
            v = fetch(group, r0) * slope(xv * gain + bias)
            dz[at, :] = v
            return (c[0] + jnp.sum(v.reshape(size // 8, 8, width), axis=0),
                    c[1] + jnp.sum((v * xv).reshape(size // 8, 8, width), axis=0))

        zero = jnp.zeros((8, width), F32)
        small, large = chunks(s, size, body, (zero, zero))
        rows = [jnp.sum(v * live[g], axis=0, keepdims=True) for v, g in
                ((small[0], 0), (large[0], 1), (small[1], 0), (large[1], 1))]
        return jnp.concatenate(rows, axis=0)

    def transpose():
        def body(j, _):
            at = pl.ds(pl.multiple_of(j * 128, 128), 128)
            flip[at, :] = nat[:, at].T
            return 0

        lax.fori_loop(0, mid // 128, body, 0)

    def fetch_into(src, dst, sem):
        c = pltpu.make_async_copy(src, dst, load.at[sem])
        c.start()
        return c

    def narrow_store(at, v):
        d3[1, at, :] = v.astype(BF)

    def nat_store(at, v):
        nat[at, :] = v.astype(BF)

    def first(up, xh):
        c1, c2 = fetch_into(dpre, up, 0), fetch_into(xh4, xh, 1)
        c1.wait()
        c2.wait()
        norm_back(3, last[...], r4[...], up, xh, narrow_store, 80, d)

    pl.run_scoped(first, pltpu.VMEM((m, d), F32), pltpu.VMEM((m, d), F32))
    zero_padding(s, d3.at[1], d)

    def temporal(stage, index, n, whole, zs, xhs, scale):
        def halo(side):
            to = p.t + 1 if side == 2 else p.t - 1
            return send(d3.at[1], d3.at[side], halo_send.at[stage, side // 2], halo_recv.at[stage, side // 2],
                        (p.z, to))

        def run(dz, xh, wu):
            pl.when(p.t < p.slots - 1)(lambda: halo(2).start())
            pl.when(p.t > 0)(lambda: halo(0).start())
            cz = fetch_into(zs, nat, 2)
            cw = fetch_into(whole, wu, 3)
            cx = fetch_into(xhs, xh, 4)
            cz.wait()
            transpose()
            cw.wait()

            def grads(k):
                for lo, width in wide_cuts(mid):
                    y = lax.dot_general(d3[k], wu[k * mid + lo : k * mid + lo + width, :], NT_DIMS,
                                        preferred_element_type=F32)
                    if k == 1:
                        dz[:, lo : lo + width] = y
                    else:
                        dz[:, lo : lo + width] += y
                pu[k * mid : (k + 1) * mid, :] = jnp.dot(
                    flip[...], d3[k], preferred_element_type=F32
                ).astype(BF)

            grads(1)
            tick(2)
            pl.when(p.t < p.slots - 1)(lambda: halo(0).wait_recv())
            grads(0)
            pl.when(p.t > 0)(lambda: halo(2).wait_recv())
            grads(2)
            sc = scatter(index)
            for rel in (3, 1, 2, 0):
                sc.twin(rel)
            queue.extend(sc.steps())
            cx.wait()

            def fetch(group, r0):
                return dz[pl.ds(r0, 16), :]

            total = totals.run(2 * stage, upstream(n, dz, xh, fetch, 16, mid))
            norm_back(n, total, scale, dz, xh, nat_store, 16, mid)

        pl.run_scoped(run, pltpu.VMEM((m, mid), F32), pltpu.VMEM((m, mid), F32), pltpu.VMEM((3 * mid, d), BF))
        zero_padding(s, nat, mid)
        pl.when(p.t < p.slots - 1)(lambda: halo(2).wait_send())
        pl.when(p.t > 0)(lambda: halo(0).wait_send())

    def finish_u(n, ref):
        sc = scatter(n)
        g = sc.result()
        ref[...] = g
        sc.sent()
        return jnp.sum(g * g, axis=0, keepdims=True)

    def finish_s(n, ref):
        sc = scatter(n)
        g = sc.result()
        turn[...] = g.T
        mine = turn[pl.ds(pl.multiple_of(p.core * (s.kw // 2), 16), s.kw // 2), :]
        ref[p.core] = mine
        copy = send(turn.at[pl.ds(pl.multiple_of((1 - p.core) * (s.kw // 2), 16), s.kw // 2)], ref.at[p.core],
                    half_s.at[n // 2], half_r.at[n // 2], p.device(TWIN))
        copy.start()
        sc.sent()
        send(turn.at[pl.ds(0, s.kw // 2)], ref.at[1 - p.core], half_s.at[n // 2], half_r.at[n // 2],
             p.device(TWIN)).wait_recv()
        copy.wait_send()
        return jnp.sum(jnp.sum((g * g).reshape(s.nb, s.kw // 128, 128), axis=0), axis=0, keepdims=True)

    pieces = []
    for tap in range(9):
        lo, end, found = tap * d, (tap + 1) * d, []
        while lo < end:
            hi = min(end, (lo // s.kw + 1) * s.kw)
            found.append((lo // s.kw, lo % s.kw, lo - tap * d, hi - lo))
            lo = hi
        pieces.append(found)

    def spatial(index, whole, taps, grids, tap_buf, tile):
        rels = (3, 1, 2, 0)

        def tap_load(i):
            return pltpu.make_async_copy(taps.at[p.rel[rels[i]]], tap_buf.at[i % 2], tap_sem.at[i])

        def tile_loads(tap):
            return [
                pltpu.make_async_copy(
                    whole.at[slab, :, pl.ds(lane, width)], tile.at[tap % 2, :, pl.ds(at, width)],
                    tile_sem.at[tap, n],
                )
                for n, (slab, lane, at, width) in enumerate(pieces[tap])
            ]

        tap_load(0).start()
        tap_load(1).start()
        for c in tile_loads(0):
            c.start()
        transpose()
        for grid in grids:
            def clear(i, _, grid=grid):
                grid[i] = jnp.zeros(grid.shape[1:], F32)
                return 0

            lax.fori_loop(0, grid.shape[0], clear, 0)
        sc = scatter(index)
        for i, rel in enumerate(rels):
            tap_load(i).wait()
            for lo, width in wide_cuts(s.kw):
                y = jnp.dot(flip[...], tap_buf[i % 2, :, lo : lo + width], preferred_element_type=F32).astype(BF)
                for n in range(2 * s.batches):
                    b, core = n // 2, n % 2
                    ps[rel, core, b * s.nb : (b + 1) * s.nb, lo : lo + width] = y[n * s.nb : (n + 1) * s.nb]
            sc.twin(rel)
            if i + 2 < 4:
                tap_load(i + 2).start()
        queue.extend(sc.steps())
        for tap in range(9):
            if tap + 1 < 9:
                for c in tile_loads(tap + 1):
                    c.start()
            for c in tile_loads(tap):
                c.wait()
            i, j = tap // 3, tap % 3
            y = jnp.dot(nat[...], tile[tap % 2], preferred_element_type=F32)
            base = 0
            for group in range(2):
                side = s.sides[group]
                part = y[base : base + s.cells[group] * 8].reshape(side, side, 8, d)
                grids[group][i : i + side, j : j + side] += part
                base += s.rows[group]
            tick(1)
        clear_pad_cells(s, grids)

    def spatial_types():
        return (
            pltpu.VMEM((s.sides[0] + 2, s.sides[0] + 2, 8, d), F32),
            pltpu.VMEM((s.sides[1] + 2, s.sides[1] + 2, 8, d), F32),
            pltpu.VMEM((2, m, s.kw), BF), pltpu.VMEM((2, mid, d), BF),
            pltpu.VMEM((m, d), F32), pltpu.VMEM((m, d), F32),
        )

    temporal(0, 3, 2, gu2, z3, xh3, r3[...])

    def second(grid_s, grid_l, tap_buf, tile, b, xh):
        cx = fetch_into(xh2, xh, 5)
        flush()
        sums = finish_u(3, guo2)
        spatial(2, gs2, taps2, (grid_s, grid_l), tap_buf, tile)
        cx.wait()

        def fetch(group, r0):
            return rows_of_grid(s, (grid_s, grid_l), group, r0)

        total = totals.run(1, upstream(1, b, xh, fetch, 80, d))
        norm_back(1, total, r2[...], b, xh, narrow_store, 80, d)
        return sums

    sums = pl.run_scoped(second, *spatial_types())
    zero_padding(s, d3.at[1], d)
    temporal(1, 1, 0, gu1, z1, xh1, r1[...])

    def final(grid_s, grid_l, tap_buf, tile, b, up, sums=sums):
        cx = fetch_into(dpre, up, 6)
        flush()
        sums = sums + finish_u(1, guo1) + finish_s(2, gsh2)
        totals.run(4, jnp.broadcast_to(sums, (4, 128)))
        spatial(0, gs1, taps1, (grid_s, grid_l), tap_buf, tile)
        cx.wait()

        def rows(group, r0, c):
            dx[pl.ds(r0, 80), :] = rows_of_grid(s, (grid_s, grid_l), group, r0) + up[pl.ds(r0, 80), :]
            return c

        chunks(s, 80, rows)
        flush()
        return sums + finish_s(0, gsh1)

    sums = pl.run_scoped(final, *spatial_types())
    square[...] = totals.run(3, jnp.broadcast_to(sums, (4, 128)))


def backward_call(s, saved, norm, live, inverse):
    any_, vmem, smem = (pl.BlockSpec(memory_space=m) for m in (pl.ANY, pltpu.VMEM, pltpu.SMEM))
    S, V, dma = jax.ShapeDtypeStruct, pltpu.VMEM, pltpu.SemaphoreType.DMA
    m, d, mid, nb, kw = s.m, s.d, s.mid, s.batches, s.kw
    half = nb // 2
    outs = (S((m, d), F32), S((2, kw // 2, s.nb), F32), S((2, kw // 2, s.nb), F32),
            S((s.ur, s.uc), F32), S((s.ur, s.uc), F32), S((2, 2 * (mid + d)), F32), S((4, 128), F32))
    rows = nb * s.nb
    scratch = [
        V((4, 2, rows, kw), BF), V((4, rows, kw), BF), V((half * s.nb, kw), BF), V((half * s.nb, kw), BF),
        V((rows, kw), BF), V((rows, kw), BF), V((rows, kw), BF), V((rows, kw), BF),
        V((3 * mid, d), BF), V((4, s.ur, d), BF), V((s.ur, d // 2), BF), V((s.ur, d // 2), BF),
        V((s.ur, d), BF), V((s.ur, d), BF), V((s.ur, d), BF), V((s.ur, d), BF),
        V((m, mid), BF), V((mid, m), BF), V((3, m, d), BF), V((kw, s.nb), F32),
        V((5, s.slots, 4, mid), F32), V((5, nb, 4, mid), F32),
        dma((8,)), dma((4,)), dma((9, 3)), dma((2, 2)), dma((2, 2)),
        dma((4, 4)), dma((4, 4)), dma((4, 5, nb)), dma((4, 5, nb)), dma((2,)), dma((2,)),
        dma((5, s.slots)), dma((5, s.slots)), dma((5, nb)), dma((5, nb)),
    ]
    return pl.pallas_call(
        functools.partial(backward_kernel, s),
        out_shape=outs,
        in_specs=[any_] * 13 + [vmem] * 7 + [smem],
        out_specs=(vmem,) * 7,
        scratch_shapes=scratch,
        compiler_params=pltpu.CompilerParams(
            collective_id=1, has_side_effects=True, vmem_limit_bytes=63 * 2**20
        ),
        name="backward",
    )(*saved, norm, live, inverse)


def body(batches, slots, *args):
    x_small, x_large = args[0], args[1]
    if not fits(x_small.shape, x_large.shape, batches, slots):
        return plain_body(*args)
    return fast_body(Shape(x_small.shape, x_large.shape, batches, slots), *args)


def fast_body(
    s,
    x_small,
    x_large,
    grad_small,
    grad_large,
    clip_counts,
    first_spatial,
    first_temporal,
    second_spatial,
    second_temporal,
    norm_params,
    first_spatial_momentum,
    first_temporal_momentum,
    second_spatial_momentum,
    second_temporal_momentum,
    norm_momentum,
    first_spatial_variance,
    first_temporal_variance,
    second_spatial_variance,
    second_temporal_variance,
    norm_variance,
):
    z = lax.axis_index("batch")
    slots = jnp.arange(s.clips, dtype=jnp.int32)
    counts = lax.dynamic_index_in_dim(clip_counts, z, 1, keepdims=False)
    live = (slots[None, :] < counts[:, None]).astype(F32)[:, :, None]
    totals = jnp.sum(clip_counts, axis=1).astype(F32) * (s.slots * jnp.array(s.cells, F32))
    inverse = 1.0 / totals
    x = cell_major(s, x_small, x_large)
    grad = cell_major(s, grad_small, grad_large)
    res = forward_call(
        s, x, grad, halves(s, first_spatial), first_temporal.astype(BF), halves(s, second_spatial),
        second_temporal.astype(BF), norm_params, live, inverse,
    )
    out_small, out_large = clip_major(s, res[12])
    saved = res[:12] + res[13:]
    dx, gs1, gs2, gu1, gu2, grad_params, square = backward_call(s, saved, norm_params, live, inverse)
    in_small, in_large = clip_major(s, dx)

    def whole(g):
        return g.transpose(1, 0, 2).reshape(g.shape[1], 2 * g.shape[2])

    grad_norm = jnp.sqrt(jnp.sum(square[0]) + jnp.sum(grad_params * grad_params))
    factor = THRESHOLD / jnp.maximum(grad_norm, THRESHOLD)
    one = adamw(first_spatial, whole(gs1), first_spatial_momentum, first_spatial_variance, factor,
                WEIGHT_RATE, WEIGHT_DECAY)
    two = adamw(first_temporal, gu1, first_temporal_momentum, first_temporal_variance, factor,
                WEIGHT_RATE, WEIGHT_DECAY)
    three = adamw(second_spatial, whole(gs2), second_spatial_momentum, second_spatial_variance, factor,
                  WEIGHT_RATE, WEIGHT_DECAY)
    four = adamw(second_temporal, gu2, second_temporal_momentum, second_temporal_variance, factor,
                 WEIGHT_RATE, WEIGHT_DECAY)
    norms = adamw(norm_params, grad_params, norm_momentum, norm_variance, factor, NORM_RATE, 0.0)
    return (out_small, out_large, in_small, in_large, grad_norm) + one + two + three + four + norms


def solution(mesh):
    return jax.shard_map(
        functools.partial(body, mesh.shape["batch"], mesh.shape["tm"]),
        mesh=mesh,
        in_specs=(
            P("batch", "tm", None, None),
            P("batch", "tm", None, None),
            P("batch", "tm", None, None),
            P("batch", "tm", None, None),
            P(),
            P("tm", "batch"),
            P("tm", "batch"),
            P("tm", "batch"),
            P("tm", "batch"),
            P(),
            P("tm", "batch"),
            P("tm", "batch"),
            P("tm", "batch"),
            P("tm", "batch"),
            P(),
            P("tm", "batch"),
            P("tm", "batch"),
            P("tm", "batch"),
            P("tm", "batch"),
            P(),
        ),
        out_specs=(
            P("batch", "tm", None, None),
            P("batch", "tm", None, None),
            P("batch", "tm", None, None),
            P("batch", "tm", None, None),
            P(),
            P("tm", "batch"),
            P("tm", "batch"),
            P("tm", "batch"),
            P("tm", "batch"),
            P("tm", "batch"),
            P("tm", "batch"),
            P("tm", "batch"),
            P("tm", "batch"),
            P("tm", "batch"),
            P("tm", "batch"),
            P("tm", "batch"),
            P("tm", "batch"),
            P(),
            P(),
            P(),
        ),
        check_vma=False,
    )
```

```python
import contextlib
import functools
import math

import jax
import jax.numpy as jnp
from jax import lax
from jax.experimental import pallas as pl
from jax.experimental.pallas import tpu as pltpu
from jax.sharding import PartitionSpec as P

D = 512
MID = 1152
HS = 7
HL = 10
STEP = 10


NORM_EPS = 1e-05
THRESHOLD = 1.0
BETA_ONE = 0.9
BETA_TWO = 0.999
WEIGHT_RATE = 0.03
NORM_RATE = 0.25
WEIGHT_DECAY = 0.05
ADAM_EPS = 1e-08


def padded_2(value, sides, width):
    for axis, dim in sides:
        size, length = (lax.axis_size(axis), value.shape[dim])
        up = [(i, (i + 1) % size) for i in range(size - 1)]
        down = [(j, i) for i, j in up]
        last = lax.slice_in_dim(value, length - width, length, axis=dim)
        first = lax.slice_in_dim(value, 0, width, axis=dim)
        before = lax.ppermute(last, axis, up)
        after = lax.ppermute(first, axis, down)
        value = jnp.concatenate([before, value, after], axis=dim)
    return value


def silu_slope(input_value):
    sigmoid_value = jax.nn.sigmoid(input_value)
    return sigmoid_value * (1.0 + input_value * (1.0 - sigmoid_value))


def spatial_taps(field, side):
    clips, frames, cells, channels = field.shape
    grid = field.reshape(clips, frames, side, side, channels)
    padded = jnp.pad(grid, ((0, 0), (0, 0), (1, 1), (1, 1), (0, 0)))
    pieces = [
        padded[:, :, row : row + side, column : column + side, :]
        for row in range(3)
        for column in range(3)
    ]
    return jnp.concatenate(pieces, axis=-1).reshape(clips * frames * cells, 9 * channels)


def spatial_forward(field_small, field_large, weight):
    taps_small = spatial_taps(field_small, HS)
    taps_large = spatial_taps(field_large, HL)
    result_small = jnp.dot(taps_small, weight, preferred_element_type=jnp.float32).reshape(
        field_small.shape[:3] + (weight.shape[1],)
    )
    result_large = jnp.dot(taps_large, weight, preferred_element_type=jnp.float32).reshape(
        field_large.shape[:3] + (weight.shape[1],)
    )
    return (jnp.concatenate([result_small, result_large], axis=2), taps_small, taps_large)


def spatial_backward(upstream_rows, weight, shape, side):
    clips, frames, cells, channels = shape
    columns = lax.dot_general(
        upstream_rows, weight, (((1,), (1,)), ((), ())), preferred_element_type=jnp.float32
    )
    columns = columns.reshape(clips, frames, side, side, 9 * channels)
    padded = jnp.pad(columns, ((0, 0), (0, 0), (1, 1), (1, 1), (0, 0)))
    final_result = None
    for row in range(3):
        for column in range(3):
            offset = (3 * row + column) * channels
            window = padded[
                :,
                :,
                2 - row : 2 - row + side,
                2 - column : 2 - column + side,
                offset : offset + channels,
            ]
            final_result = window if final_result is None else final_result + window
    return final_result.reshape(clips, frames, cells, channels)


def temporal_forward(field, weight):
    padded = padded_2(field, (("tm", 1),), 1)
    frames = field.shape[1]
    pieces = jnp.concatenate([padded[:, shift : shift + frames] for shift in range(3)], axis=-1)
    rows = pieces.reshape(-1, pieces.shape[-1])
    final_result = jnp.dot(rows, weight, preferred_element_type=jnp.float32).reshape(
        field.shape[:3] + (weight.shape[1],)
    )
    return (final_result, rows)


def temporal_backward(upstream_gradient, weight):
    padded = padded_2(upstream_gradient, (("tm", 1),), 1)
    frames = upstream_gradient.shape[1]
    pieces = jnp.concatenate(
        [padded[:, 2 - shift : 2 - shift + frames] for shift in range(3)], axis=-1
    )
    rows = pieces.reshape(-1, pieces.shape[-1])
    kernel = (
        weight.reshape(3, -1, weight.shape[1]).transpose(1, 0, 2).reshape(-1, 3 * weight.shape[1])
    )
    final_result = lax.dot_general(
        rows, kernel, (((1,), (1,)), ((), ())), preferred_element_type=jnp.float32
    )
    return final_result.reshape(upstream_gradient.shape[:3] + (kernel.shape[0],))


def group_totals(leading_part, trailing_part, active_flags, split_point):
    leading_cells = jnp.sum(active_flags * leading_part, axis=(0, 1))
    trailing_cells = jnp.sum(active_flags * trailing_part, axis=(0, 1))
    first_groups = jnp.stack(
        [jnp.sum(leading_cells[:split_point], axis=0), jnp.sum(leading_cells[split_point:], axis=0)]
    )
    second_groups = jnp.stack(
        [
            jnp.sum(trailing_cells[:split_point], axis=0),
            jnp.sum(trailing_cells[split_point:], axis=0),
        ]
    )
    return (first_groups, second_groups)


def per_cell(stat, split_point, cells):
    channels = stat.shape[1]
    return jnp.concatenate(
        [
            jnp.broadcast_to(stat[0], (split_point, channels)),
            jnp.broadcast_to(stat[1], (cells - split_point, channels)),
        ],
        axis=0,
    )


def norm_forward_pass(
    input_value, active_flags, split_point, grand_totals, norm_gain_vector, norm_shift_bias
):
    running_sums, squared_values = group_totals(
        input_value, input_value * input_value, active_flags, split_point
    )
    running_sums, squared_values = lax.psum((running_sums, squared_values), ("batch", "tm"))
    mean = running_sums / grand_totals[:, None]
    scale = lax.rsqrt(squared_values / grand_totals[:, None] - mean * mean + NORM_EPS)
    cells = input_value.shape[2]
    cell_scale = per_cell(scale, split_point, cells)
    normalized_values = (input_value - per_cell(mean, split_point, cells)) * cell_scale
    return (normalized_values * norm_gain_vector + norm_shift_bias, normalized_values, cell_scale)


def norm_reverse_pass(
    upstream_gradient,
    normalized_values,
    cell_scale,
    norm_gain_vector,
    active_flags,
    split_point,
    grand_totals,
):
    running_sums, cross_product = group_totals(
        upstream_gradient, upstream_gradient * normalized_values, active_flags, split_point
    )
    running_sums, cross_product = lax.psum((running_sums, cross_product), ("batch", "tm"))
    cells = upstream_gradient.shape[2]
    upstream_average = per_cell(running_sums / grand_totals[:, None], split_point, cells)
    cross_average = per_cell(cross_product / grand_totals[:, None], split_point, cells)
    final_result = (
        active_flags
        * (norm_gain_vector * cell_scale)
        * (upstream_gradient - upstream_average - normalized_values * cross_average)
    )
    return (final_result, jnp.sum(cross_product, axis=0), jnp.sum(running_sums, axis=0))


def reduce_weight(pairs, depth, width):
    total = jnp.zeros((depth // lax.axis_size("tm") * lax.axis_size("tm"), width), jnp.float32)
    for left, right in pairs:
        total = total + lax.dot_general(
            left, right, (((0,), (0,)), ((), ())), preferred_element_type=jnp.float32
        )
    shared = lax.psum_scatter(total.astype(jnp.bfloat16), "tm", scatter_dimension=0, tiled=True)
    return lax.psum_scatter(shared, "batch", scatter_dimension=1, tiled=True).astype(jnp.float32)


def own_square(shard):
    local = jnp.sum(shard * shard)
    return local


def adamw(weight, gradient, momentum, variance, factor, rate, decay):
    clipped = gradient * factor
    new_momentum = BETA_ONE * momentum + (1.0 - BETA_ONE) * clipped
    new_variance = BETA_TWO * variance + (1.0 - BETA_TWO) * clipped * clipped
    corrected = new_momentum / (1.0 - BETA_ONE**STEP)
    spread = jnp.sqrt(new_variance / (1.0 - BETA_TWO**STEP))
    new_weight = weight - rate * (corrected / (spread + ADAM_EPS) + decay * weight)
    return (new_weight, new_momentum, new_variance)


def plain_body(
    x_small,
    x_large,
    small_output_gradient,
    large_output_gradient,
    clip_counts,
    first_spatial,
    first_temporal,
    second_spatial,
    second_temporal,
    norm_params,
    first_spatial_momentum,
    first_temporal_momentum,
    second_spatial_momentum,
    second_temporal_momentum,
    norm_momentum,
    first_spatial_variance,
    first_temporal_variance,
    second_spatial_variance,
    second_temporal_variance,
    norm_variance,
):
    low_one = first_spatial.astype(jnp.bfloat16)
    low_two = first_temporal.astype(jnp.bfloat16)
    low_three = second_spatial.astype(jnp.bfloat16)
    low_four = second_temporal.astype(jnp.bfloat16)
    columns = (
        lax.all_gather(low_one, "batch", axis=1, tiled=True),
        lax.all_gather(low_two, "batch", axis=1, tiled=True),
        lax.all_gather(low_three, "batch", axis=1, tiled=True),
        lax.all_gather(low_four, "batch", axis=1, tiled=True),
    )
    spatial_one, temporal_one, spatial_two, temporal_two = (
        lax.all_gather(columns[0], "tm", axis=0, tiled=True),
        lax.all_gather(columns[1], "tm", axis=0, tiled=True),
        lax.all_gather(columns[2], "tm", axis=0, tiled=True),
        lax.all_gather(columns[3], "tm", axis=0, tiled=True),
    )
    clips = x_small.shape[0]
    split_point = x_small.shape[2]
    large_cells = x_large.shape[2]
    batch_index = lax.axis_index("batch")
    slots = jnp.arange(clips, dtype=jnp.int32)
    live_small = (slots < clip_counts[0, batch_index]).astype(jnp.float32)
    live_large = (slots < clip_counts[1, batch_index]).astype(jnp.float32)
    active_flags = jnp.concatenate(
        [
            jnp.broadcast_to(live_small[:, None, None, None], (clips, 1, split_point, 1)),
            jnp.broadcast_to(live_large[:, None, None, None], (clips, 1, large_cells, 1)),
        ],
        axis=2,
    )
    frames_total = x_small.shape[1] * lax.axis_size("tm")
    grand_totals = jnp.stack(
        [
            jnp.sum(clip_counts[0]).astype(jnp.float32) * frames_total * split_point,
            jnp.sum(clip_counts[1]).astype(jnp.float32) * frames_total * large_cells,
        ]
    )
    bounds = (0, MID, MID + D, 2 * MID + D, 2 * MID + 2 * D)
    gain_vectors = [norm_params[0, bounds[index] : bounds[index + 1]] for index in range(4)]
    bias_vectors = [norm_params[1, bounds[index] : bounds[index + 1]] for index in range(4)]
    first_convolved, taps_one_small, taps_one_large = spatial_forward(x_small, x_large, spatial_one)
    hidden_one, normed_one, scale_one = norm_forward_pass(
        first_convolved, active_flags, split_point, grand_totals, gain_vectors[0], bias_vectors[0]
    )
    act_one = jax.nn.silu(hidden_one).astype(jnp.bfloat16)
    second_convolved, rows_two = temporal_forward(act_one, temporal_one)
    hidden_two, normed_two, scale_two = norm_forward_pass(
        second_convolved, active_flags, split_point, grand_totals, gain_vectors[1], bias_vectors[1]
    )
    act_two = jax.nn.silu(hidden_two).astype(jnp.bfloat16)
    third_convolved, taps_three_small, taps_three_large = spatial_forward(
        act_two[:, :, :split_point], act_two[:, :, split_point:], spatial_two
    )
    hidden_three, normed_three, scale_three = norm_forward_pass(
        third_convolved, active_flags, split_point, grand_totals, gain_vectors[2], bias_vectors[2]
    )
    act_three = jax.nn.silu(hidden_three).astype(jnp.bfloat16)
    fourth_convolved, rows_four = temporal_forward(act_three, temporal_two)
    hidden_four, fourth_normalized, fourth_scale = norm_forward_pass(
        fourth_convolved, active_flags, split_point, grand_totals, gain_vectors[3], bias_vectors[3]
    )
    residual_in = jnp.concatenate([x_small, x_large], axis=2).astype(jnp.float32)
    output_preactivation = hidden_four + residual_in
    block_output = active_flags * jax.nn.silu(output_preactivation)
    upstream_gradient = (
        jnp.concatenate([small_output_gradient, large_output_gradient], axis=2).astype(jnp.float32)
        * active_flags
    )
    passed_gradient = upstream_gradient * silu_slope(output_preactivation)
    squared_values = []
    grad_conv_four, gain_four, bias_four = norm_reverse_pass(
        passed_gradient,
        fourth_normalized,
        fourth_scale,
        gain_vectors[3],
        active_flags,
        split_point,
        grand_totals,
    )
    grad_conv_four = grad_conv_four.astype(jnp.bfloat16)
    rows_grad_four = grad_conv_four.reshape(-1, grad_conv_four.shape[-1])
    grad_second_temporal = reduce_weight(
        [(rows_four, rows_grad_four)], rows_four.shape[1], rows_grad_four.shape[1]
    )
    squared_values.append(own_square(grad_second_temporal))
    grad_act_three = temporal_backward(grad_conv_four, temporal_two)
    grad_conv_three, gain_three, bias_three = norm_reverse_pass(
        grad_act_three * silu_slope(hidden_three),
        normed_three,
        scale_three,
        gain_vectors[2],
        active_flags,
        split_point,
        grand_totals,
    )
    grad_conv_three = grad_conv_three.astype(jnp.bfloat16)
    rows_three_small = grad_conv_three[:, :, :split_point].reshape(-1, grad_conv_three.shape[-1])
    rows_three_large = grad_conv_three[:, :, split_point:].reshape(-1, grad_conv_three.shape[-1])
    grad_second_spatial = reduce_weight(
        [(taps_three_small, rows_three_small), (taps_three_large, rows_three_large)],
        taps_three_small.shape[1],
        rows_three_small.shape[1],
    )
    squared_values.append(own_square(grad_second_spatial))
    channels_mid = act_two.shape[-1]
    grad_act_two = jnp.concatenate(
        [
            spatial_backward(
                rows_three_small,
                spatial_two,
                (clips, act_two.shape[1], split_point, channels_mid),
                HS,
            ),
            spatial_backward(
                rows_three_large,
                spatial_two,
                (clips, act_two.shape[1], large_cells, channels_mid),
                HL,
            ),
        ],
        axis=2,
    )
    grad_conv_two, gain_two, bias_two = norm_reverse_pass(
        grad_act_two * silu_slope(hidden_two),
        normed_two,
        scale_two,
        gain_vectors[1],
        active_flags,
        split_point,
        grand_totals,
    )
    grad_conv_two = grad_conv_two.astype(jnp.bfloat16)
    rows_grad_two = grad_conv_two.reshape(-1, grad_conv_two.shape[-1])
    grad_first_temporal = reduce_weight(
        [(rows_two, rows_grad_two)], rows_two.shape[1], rows_grad_two.shape[1]
    )
    squared_values.append(own_square(grad_first_temporal))
    grad_act_one = temporal_backward(grad_conv_two, temporal_one)
    grad_conv_one, gain_one, bias_one = norm_reverse_pass(
        grad_act_one * silu_slope(hidden_one),
        normed_one,
        scale_one,
        gain_vectors[0],
        active_flags,
        split_point,
        grand_totals,
    )
    grad_conv_one = grad_conv_one.astype(jnp.bfloat16)
    rows_one_small = grad_conv_one[:, :, :split_point].reshape(-1, grad_conv_one.shape[-1])
    rows_one_large = grad_conv_one[:, :, split_point:].reshape(-1, grad_conv_one.shape[-1])
    grad_first_spatial = reduce_weight(
        [(taps_one_small, rows_one_small), (taps_one_large, rows_one_large)],
        taps_one_small.shape[1],
        rows_one_small.shape[1],
    )
    squared_values.append(own_square(grad_first_spatial))
    input_small = passed_gradient[:, :, :split_point] + spatial_backward(
        rows_one_small, spatial_one, x_small.shape, HS
    )
    input_large = passed_gradient[:, :, split_point:] + spatial_backward(
        rows_one_large, spatial_one, x_large.shape, HL
    )
    grad_params = jnp.stack(
        [
            jnp.concatenate([gain_one, gain_two, gain_three, gain_four]),
            jnp.concatenate([bias_one, bias_two, bias_three, bias_four]),
        ]
    )
    summed = lax.psum(
        (squared_values[0], squared_values[1], squared_values[2], squared_values[3]),
        ("batch", "tm"),
    )
    weight_square = summed[0] + summed[1] + summed[2] + summed[3]
    grad_norm = jnp.sqrt(weight_square + jnp.sum(grad_params * grad_params))
    factor = THRESHOLD / jnp.maximum(grad_norm, THRESHOLD)
    one = adamw(
        first_spatial,
        grad_first_spatial,
        first_spatial_momentum,
        first_spatial_variance,
        factor,
        WEIGHT_RATE,
        WEIGHT_DECAY,
    )
    two = adamw(
        first_temporal,
        grad_first_temporal,
        first_temporal_momentum,
        first_temporal_variance,
        factor,
        WEIGHT_RATE,
        WEIGHT_DECAY,
    )
    three = adamw(
        second_spatial,
        grad_second_spatial,
        second_spatial_momentum,
        second_spatial_variance,
        factor,
        WEIGHT_RATE,
        WEIGHT_DECAY,
    )
    four = adamw(
        second_temporal,
        grad_second_temporal,
        second_temporal_momentum,
        second_temporal_variance,
        factor,
        WEIGHT_RATE,
        WEIGHT_DECAY,
    )
    norms = adamw(norm_params, grad_params, norm_momentum, norm_variance, factor, NORM_RATE, 0.0)
    return (
        block_output[:, :, :split_point],
        block_output[:, :, split_point:],
        input_small,
        input_large,
        grad_norm,
        one[0],
        one[1],
        one[2],
        two[0],
        two[1],
        two[2],
        three[0],
        three[1],
        three[2],
        four[0],
        four[1],
        four[2],
        norms[0],
        norms[1],
        norms[2],
    )


BF = jnp.bfloat16
F32 = jnp.float32
MESH_ID = pl.DeviceIdType.MESH
NT_DIMS = (((1,), (1,)), ((), ()))
NN_DIMS = (((1,), (0,)), ((), ()))
scope = lambda name: contextlib.nullcontext()
UP, DOWN, ACROSS, ALONG, TWIN = range(5)


class Place:
    def __init__(self, batches, slots):
        self.batches, self.slots = batches, slots
        self.z = lax.axis_index("batch")
        self.t = lax.axis_index("tm")
        self.core = lax.rem(self.t, 2)
        self.slab = self.t // 2
        self.slabs = slots // 2
        side = lax.rem(self.slab, 2)
        deep = self.slab // 2
        self.side_slab = deep * 2 + (1 - side)
        self.deep_slab = (1 - deep) * 2 + side
        self.far_slab = (1 - deep) * 2 + (1 - side)
        self.rel = (self.slab, self.side_slab, self.deep_slab, self.far_slab)
        self.twin = self.t + 1 - 2 * self.core

    def device(self, way):
        if way == UP:
            return (self.z + 1, self.t)
        if way == DOWN:
            return (self.z - 1, self.t)
        if way == ACROSS:
            return (self.z, self.side_slab * 2 + self.core)
        if way == ALONG:
            return (self.z, self.deep_slab * 2 + self.core)
        return (self.z, self.twin)

    def greet(self):
        barrier = pltpu.get_barrier_semaphore()
        for step in range(1, self.slots):
            pl.semaphore_signal(
                barrier, inc=1, device_id=(self.z, lax.rem(self.t + step, self.slots)),
                device_id_type=MESH_ID,
            )
        for step in range(1, self.batches):
            pl.semaphore_signal(
                barrier, inc=1, device_id=(lax.rem(self.z + step, self.batches), self.t),
                device_id_type=MESH_ID,
            )
        pl.semaphore_wait(barrier, self.slots + self.batches - 2)


def send(src, dst, send_sem, recv_sem, device):
    return pltpu.make_async_remote_copy(
        src_ref=src, dst_ref=dst, send_sem=send_sem, recv_sem=recv_sem,
        device_id=device, device_id_type=MESH_ID,
    )


class Totals:
    def __init__(self, place, rows, planes, lines, sems):
        self.place, self.rows, self.planes, self.lines = place, rows, planes, lines
        self.plane_send, self.plane_recv, self.line_send, self.line_recv = sems

    def run(self, n, value):
        p = self.place
        width = value.shape[1]
        plane, line = self.planes.at[n], self.lines.at[n]
        plane[p.t, :, :width] = value

        def plane_copy(step):
            to = lax.rem(p.t + step, p.slots)
            ref = plane.at[p.t, :, pl.ds(0, width)]
            return send(ref, ref, self.plane_send.at[n, step], self.plane_recv.at[n, p.t], (p.z, to))

        def plane_wait(step):
            origin = lax.rem(p.t + p.slots - step, p.slots)
            ref = plane.at[origin, :, pl.ds(0, width)]
            send(ref, ref, self.plane_send.at[n, step], self.plane_recv.at[n, origin], (p.z, p.twin)).wait_recv()

        for step in range(1, p.slots):
            plane_copy(step).start()
        for step in range(1, p.slots):
            plane_wait(step)
        total = plane[0, :, :width]
        for slot in range(1, p.slots):
            total = total + plane[slot, :, :width]
        line[p.z, :, :width] = total

        def line_copy(step):
            to = lax.rem(p.z + step, p.batches)
            ref = line.at[p.z, :, pl.ds(0, width)]
            return send(ref, ref, self.line_send.at[n, step], self.line_recv.at[n, p.z], (to, p.t))

        def line_wait(step):
            origin = lax.rem(p.z + p.batches - step, p.batches)
            ref = line.at[origin, :, pl.ds(0, width)]
            send(ref, ref, self.line_send.at[n, step], self.line_recv.at[n, origin], (p.z, p.twin)).wait_recv()

        for step in range(1, p.batches):
            line_copy(step).start()
        for step in range(1, p.batches):
            line_wait(step)
        total = line[0, :, :width]
        for slot in range(1, p.batches):
            total = total + line[slot, :, :width]
        for step in range(1, p.slots):
            plane_copy(step).wait_send()
        for step in range(1, p.batches):
            line_copy(step).wait_send()
        return total


class Gather:
    def __init__(self, place, index, own, whole, block, sems):
        self.p, self.n, self.own, self.whole, self.block = place, index, own, whole, block
        self.send_sem, self.recv_sem, self.twin_sem = sems

    def copy(self, way, rel, batch, src=None):
        p = self.p
        core = p.core
        dst = self.whole.at[self.block(p.rel[rel], core, batch)]
        there = {ACROSS: {0: 1, 2: 3}, ALONG: {0: 2, 1: 3}}.get(way, {}).get(rel, rel)
        sem = self.twin_sem if way == TWIN else self.recv_sem
        return send(
            dst if src is None else src, dst, self.send_sem.at[self.n, way, rel, batch],
            sem.at[self.n, there, batch], p.device(way),
        )

    def wait(self, rel, batch, twin=False):
        p = self.p
        core = 1 - p.core if twin else p.core
        ref = self.whole.at[self.block(p.rel[rel], core, batch)]
        sem = self.twin_sem if twin else self.recv_sem
        send(ref, ref, self.send_sem.at[self.n, TWIN, rel, batch], sem.at[self.n, rel, batch],
             p.device(TWIN)).wait_recv()

    def at(self, k, fn):
        p = self.p
        if k == 0:
            fn(p.z)
            return
        pl.when(p.z - k >= 0)(lambda: fn(p.z - k))
        pl.when(p.z + k < p.batches)(lambda: fn(p.z + k))

    def start_line(self):
        p = self.p
        pl.when(p.z < p.batches - 1)(lambda: self.copy(UP, 0, p.z, self.own).start())
        pl.when(p.z > 0)(lambda: self.copy(DOWN, 0, p.z, self.own).start())
        self.copy(TWIN, 0, p.z, self.own).start()

    def start_plane(self):
        for way in (ACROSS, ALONG):
            self.copy(way, 0, self.p.z, self.own).start()

    def hop(self, k):
        p = self.p

        def below(b):
            self.wait(0, b)
            pl.when(p.z < p.batches - 1)(lambda: self.copy(UP, 0, b).start())
            self.copy(TWIN, 0, b).start()

        def above(b):
            self.wait(0, b)
            pl.when(p.z > 0)(lambda: self.copy(DOWN, 0, b).start())
            self.copy(TWIN, 0, b).start()

        pl.when(p.z - k >= 0)(lambda: below(p.z - k))
        pl.when(p.z + k < p.batches)(lambda: above(p.z + k))

    def spread(self, k, ways=(ACROSS, ALONG)):
        def one(b):
            for way in ways:
                self.copy(way, 0, b).start()

        self.at(k, one)

    def across(self, k):
        self.spread(k, (ACROSS,))

    def along(self, k):
        self.spread(k, (ALONG,))

    def from_side(self, k):
        half = self.p.batches // 2

        def one(b):
            self.wait(1, b)
            pl.when(b < half)(lambda: self.copy(ALONG, 1, b).start())
            self.copy(TWIN, 1, b).start()

        self.at(k, one)

    def from_deep(self, k):
        half = self.p.batches // 2

        def one(b):
            self.wait(2, b)
            pl.when(b >= half)(lambda: self.copy(ACROSS, 2, b).start())
            self.copy(TWIN, 2, b).start()

        self.at(k, one)

    def plane(self, k):
        self.from_side(k)
        self.from_deep(k)

    def far(self, k):
        def one(b):
            self.wait(3, b)
            self.copy(TWIN, 3, b).start()

        self.at(k, one)

    def twins(self, rel):
        def body(b, _):
            self.wait(rel, b, twin=True)
            return 0

        lax.fori_loop(0, self.p.batches, body, 0)

    def act(self, word):
        kind = word[0]
        if kind == "z":
            self.start_line()
        elif kind == "x":
            self.start_plane()
        else:
            {"h": self.hop, "s": self.spread, "a": self.across, "l": self.along, "p": self.plane, "f": self.far,
             "u": self.from_side, "v": self.from_deep}[kind](int(word[1]))

    def finish(self):
        p = self.p
        half = p.batches // 2

        def body(b, _):
            pl.when((b <= p.z) & (p.z < p.batches - 1))(lambda: self.copy(UP, 0, b, self.own).wait_send())
            pl.when((b >= p.z) & (p.z > 0))(lambda: self.copy(DOWN, 0, b, self.own).wait_send())
            for way in (ACROSS, ALONG):
                self.copy(way, 0, b, self.own).wait_send()
            for rel in range(4):
                self.copy(TWIN, rel, b, self.own).wait_send()
            pl.when(b < half)(lambda: self.copy(ALONG, 1, b, self.own).wait_send())
            pl.when(b >= half)(lambda: self.copy(ACROSS, 2, b, self.own).wait_send())
            return 0

        lax.fori_loop(0, p.batches, body, 0)


class Halo:
    def __init__(self, place, stage, src, dst, relay, sems, cut):
        self.p, self.n, self.src, self.dst, self.buf, self.cut = place, stage, src, dst, relay, cut
        self.send_sem, self.recv_sem, self.pass_send, self.pass_recv = sems
        self.mid = place.slots // 2

    def part(self, ref, piece):
        rows = ref.shape[0]
        return ref.at[pl.ds(0, self.cut)] if piece == 0 else ref.at[pl.ds(self.cut, rows - self.cut)]

    def piece(self, side, piece, to):
        return send(self.part(self.src(side), piece), self.part(self.dst(side), piece),
                    self.send_sem.at[self.n, side, piece], self.recv_sem.at[self.n, side, piece],
                    (self.p.z, to))

    def detour(self, side):
        to = self.p.slots - 1 if side == 0 else 0
        return send(self.part(self.src(side), 1), self.buf, self.send_sem.at[self.n, side, 1],
                    self.pass_recv.at[self.n], (self.p.z, to))

    def passing(self, side):
        to = self.mid if side == 0 else self.mid - 1
        return send(self.buf, self.part(self.dst(side), 1), self.pass_send.at[self.n],
                    self.recv_sem.at[self.n, side, 1], (self.p.z, to))

    def sends(self, side):
        return self.p.t < self.p.slots - 1 if side == 0 else self.p.t > 0

    def receives(self, side):
        return self.p.t > 0 if side == 0 else self.p.t < self.p.slots - 1

    def start(self, side):
        p = self.p
        to = p.t + 1 if side == 0 else p.t - 1
        crossing = p.t == (self.mid - 1 if side == 0 else self.mid)

        @pl.when(self.sends(side))
        def _():
            pl.when(crossing)(lambda: self.detour(side).start())
            self.piece(side, 0, to).start()
            pl.when(jnp.logical_not(crossing))(lambda: self.piece(side, 1, to).start())

    def relay(self):
        p = self.p
        for side, t in ((0, p.slots - 1), (1, 0)):
            @pl.when(p.t == t)
            def _(side=side):
                send(self.buf, self.buf, self.pass_send.at[self.n], self.pass_recv.at[self.n],
                     p.device(TWIN)).wait_recv()
                self.passing(side).start()

    def wait(self, side):
        @pl.when(self.receives(side))
        def _():
            for piece in range(2):
                self.piece(side, piece, self.p.twin).wait_recv()

    def done(self):
        p = self.p
        for side in range(2):
            @pl.when(self.sends(side))
            def _(side=side):
                for piece in range(2):
                    self.piece(side, piece, p.twin).wait_send()
        for side, t in ((0, p.slots - 1), (1, 0)):
            pl.when(p.t == t)(lambda side=side: self.passing(side).wait_send())


def sigmoid(v):
    return 0.5 * jnp.tanh(0.5 * v) + 0.5


class Shape:
    def __init__(self, x_small, x_large, batches, slots):
        self.clips = x_small[0]
        self.cells = (x_small[2], x_large[2])
        self.sides = (math.isqrt(x_small[2]), math.isqrt(x_large[2]))
        self.d = x_small[3]
        self.padded = tuple(n + n % 2 for n in self.cells)
        self.rows = tuple(n * self.clips for n in self.padded)
        self.m = sum(self.rows)
        self.mid = MID
        self.k = 9 * self.d
        self.batches, self.slots = batches, slots
        self.slabs = slots // 2
        self.kw = self.k // self.slabs
        self.nb = self.mid // (2 * batches)
        self.ur = 3 * self.mid // slots
        self.uc = self.d // batches
        self.cut = -(-self.m // 32) * 16


def fits(x_small, x_large, batches, slots):
    s = Shape(x_small, x_large, batches, slots)
    return (
        s.clips == 8 and x_small[1] == 1 and slots == 8 and batches == 4
        and all(side * side == cells for side, cells in zip(s.sides, s.cells))
        and all(r % 80 == 0 for r in s.rows)
        and s.kw % 128 == 0 and s.mid % (32 * batches) == 0 and s.ur % 16 == 0 and s.uc % 128 == 0
    )


def chunks(s, size, fn, carry=None, unroll=1):
    out = []
    base = 0
    for group, rows in enumerate(s.rows):
        def body(i, c, group=group, base=base):
            return fn(group, pl.multiple_of(base + i * size, size if base % size == 0 else 16), c)

        out.append(lax.fori_loop(0, rows // size, body, carry if carry is not None else 0, unroll=unroll))
        base += rows
    return out


def sums_of(s, load, live, width):
    def body(group, r0, c):
        values = load(group, r0, 80)
        return tuple(t + jnp.sum(v.reshape(10, 8, width), axis=0) for t, v in zip(c, values))

    zero = jnp.zeros((8, width), F32)
    small, large = chunks(s, 80, body, (zero, zero))
    rows = [jnp.sum(v * live[g], axis=0, keepdims=True) for v, g in
            ((small[0], 0), (large[0], 1), (small[1], 0), (large[1], 1))]
    return jnp.concatenate(rows, axis=0)


def build_taps(s, grids, taps):
    pieces = []
    for tap in range(9):
        lo = tap * s.d
        end = lo + s.d
        while lo < end:
            hi = min(end, (lo // s.kw + 1) * s.kw)
            pieces.append((tap, lo - tap * s.d, lo // s.kw, lo % s.kw, hi - lo))
            lo = hi
    base = 0
    for group in range(2):
        side, cells = s.sides[group], s.cells[group]
        grid = grids[group]
        for tap, channel, slab, lane, width in pieces:
            i, j = tap // 3, tap % 3
            if side % 2 == 0:
                n = 2 * side * 8

                def body(r, _):
                    window = grid[pl.ds(i + 2 * r, 2), j : j + side, :, channel : channel + width]
                    taps[slab, pl.ds(pl.multiple_of(base + r * n, 16), n), lane : lane + width] = (
                        window.reshape(n, width).astype(BF)
                    )
                    return 0

                lax.fori_loop(0, side // 2, body, 0)
            else:
                window = grid[i : i + side, j : j + side, :, channel : channel + width]
                window = window.reshape(cells * 8, width)
                window = jnp.concatenate(
                    [window, jnp.zeros((s.rows[group] - cells * 8, width), F32)], axis=0
                ) if s.rows[group] > cells * 8 else window
                taps[slab, base : base + s.rows[group], lane : lane + width] = window.astype(BF)
        base += s.rows[group]


def fill_grid(s, grids, group, cell, value):
    side = s.sides[group]
    grids[group][1 + cell // side, 1 + lax.rem(cell, side)] = value


def zero_padding(s, ref, width):
    base = 0
    for group in range(2):
        base += s.rows[group]
        spare = (s.padded[group] - s.cells[group]) * s.clips
        if spare:
            size = -(-spare // 16) * 16
            keep = lax.broadcasted_iota(jnp.int32, (size, width), 0) < size - spare
            value = ref[base - size : base, :].astype(F32)
            ref[base - size : base, :] = jnp.where(keep, value, 0.0).astype(ref.dtype)


def grid_of_rows(s, grids, group, r0, value):
    side = s.sides[group]
    base = 0 if group == 0 else s.rows[0]
    first = (r0 - base) // 8
    split = value.reshape(10, 8, s.d)
    for n in range(10):
        cell = first + n
        grids[group][1 + cell // side, 1 + lax.rem(cell, side)] = split[n]


def clear_pad_cells(s, grids):
    for group in range(2):
        side = s.sides[group]
        for cell in range(s.cells[group], s.padded[group]):
            grids[group][1 + cell // side, 1 + cell % side] = jnp.zeros((8, s.d), F32)


def moments(total, inverse, width):
    mean = [total[g : g + 1, :] * inverse[g] for g in range(2)]
    scale = [
        lax.rsqrt(total[2 + g : 3 + g, :] * inverse[g] - mean[g] * mean[g] + NORM_EPS) for g in range(2)
    ]
    return mean, scale


def wide_cuts(width):
    half = -(-width // 256) * 128
    return ((0, half), (half, width - half))


def forward_kernel(s, *refs):
    (x, grad, sw1, uw1, sw2, uw2, norm, live_ref, inverse,
     gs1, gu1, gs2, gu2, taps1_o, taps2_o, xh1_o, xh2_o, xh3_o, xh4_o, z1_o, z3_o, out_o, dpre_o,
     r1_o, r2_o, r3_o, r4_o, last_o,
     tb1, tb2, own1, own2, wb, wub, taps, a, z, grid_s, grid_l, b, hs, hr, planes, lines,
     ag_send, ag_recv, ag_twin, tb_send, tb_recv, local, load, hs_send, hs_recv, pass_send, pass_recv, relay, out, dpre,
     pl_send, pl_recv, ln_send, ln_recv) = refs
    p = Place(s.batches, s.slots)
    live = [live_ref[g] for g in range(2)]
    inv = [inverse[g] for g in range(2)]
    totals = Totals(p, 4, planes, lines, (pl_send, pl_recv, ln_send, ln_recv))
    d, mid = s.d, s.mid
    bounds = (0, mid, mid + d, 2 * mid + d, 2 * mid + 2 * d)

    def gain_bias(n):
        return norm[0:1, bounds[n] : bounds[n + 1]], norm[1:2, bounds[n] : bounds[n + 1]]

    with scope("greet"):
        p.greet()

    def twin_copy(n, src, dst):
        return send(
            src.at[1 - p.core], dst.at[pl.ds(pl.multiple_of(p.core * (s.kw // 2), 16), s.kw // 2)],
            tb_send.at[n], tb_recv.at[n], p.device(TWIN),
        )

    def twin_wait(n, src, dst):
        send(
            src.at[1 - p.core], dst.at[pl.ds(pl.multiple_of((1 - p.core) * (s.kw // 2), 16), s.kw // 2)],
            tb_send.at[n], tb_recv.at[n], p.device(TWIN),
        ).wait_recv()

    for n, src, dst in ((0, sw1, tb1), (1, sw2, tb2)):
        twin_copy(n, src, dst).start()
        dst[pl.ds(pl.multiple_of(p.core * (s.kw // 2), 16), s.kw // 2)] = src[p.core]

    def s_block(slab, core, batch):
        return (slab, pl.ds(pl.multiple_of((batch * 2 + core) * s.nb, 16), s.nb))

    def u_block(slab, core, batch):
        return (pl.ds(pl.multiple_of((slab * 2 + core) * s.ur, 16), s.ur),
                pl.ds(pl.multiple_of(batch * s.uc, 128), s.uc))

    sems = (ag_send, ag_recv, ag_twin)
    gather = [
        Gather(p, 0, own1, gs1, s_block, sems),
        Gather(p, 1, uw1, gu1, u_block, sems),
        Gather(p, 2, own2, gs2, s_block, sems),
        Gather(p, 3, uw2, gu2, u_block, sems),
    ]

    def keep_own(n):
        g = gather[n]
        return pltpu.make_async_copy(g.own, g.whole.at[g.block(p.slab, p.core, p.z)], local.at[n])

    def go(words):
        with scope("gather " + words):
            for word in words.split():
                gather[int(word[0])].act(word[1:])

    with scope("own"):
        twin_wait(0, sw1, tb1)
        own1[...] = tb1[...].T
        go("0z 0x")
        keep_own(0).start()
        twin_wait(1, sw2, tb2)
        own2[...] = tb2[...].T
    keep_own(1).start()
    keep_own(2).start()
    keep_own(3).start()
    for side, edge in ((0, 0), (1, p.slots - 1)):
        @pl.when(p.t == edge)
        def _(side=side):
            hr[side] = jnp.zeros(hr.shape[1:], BF)

    grids = (grid_s, grid_l)
    for grid in grids:
        def clear(i, _, grid=grid):
            grid[i] = jnp.zeros(grid.shape[1:], F32)
            return 0

        lax.fori_loop(0, grid.shape[0], clear, 0)

    def x_rows(group, r0, c):
        grid_of_rows(s, grids, group, r0, x[pl.ds(r0, 80), :].astype(F32))
        return c

    with scope("taps x"):
        chunks(s, 80, x_rows)
        clear_pad_cells(s, grids)
        build_taps(s, grids, taps)
    taps_copy = pltpu.make_async_copy(taps, taps1_o, local.at[4])
    taps_copy.start()

    def slab_load(whole, rel, half):
        lo, width = wide_cuts(mid)[half]
        rows = pl.ds(lo, width)
        return pltpu.make_async_copy(whole.at[p.rel[rel], rows], wb.at[rel, rows], load.at[rel, half])

    def conv_slab(whole, rel, first):
        for half, (lo, width) in enumerate(wide_cuts(mid)):
            slab_load(whole, rel, half).wait()
            y = lax.dot_general(taps[p.rel[rel]], wb[rel, lo : lo + width, :], NT_DIMS, preferred_element_type=F32)
            if first:
                a[:, lo : lo + width] = y
            else:
                a[:, lo : lo + width] += y

    def spatial(n, whole, order, words):
        g = gather[n]
        keep_own(n).wait()
        for i, rel in enumerate(order):
            go(words[2 * i])
            with scope("twins"):
                g.twins(rel)
            for half in range(2):
                slab_load(whole, rel, half).start()
            go(words[2 * i + 1])
            with scope("slab"):
                conv_slab(whole, rel, i == 0)

    def stats(load_rows, width):
        return sums_of(s, load_rows, live, width)

    def wide_norm(index, n, zo, xo, ro, sem, words, weight):
        def load_rows(group, r0, size):
            v = a[pl.ds(r0, size), :]
            return v, v * v

        with scope("wide stats"):
            local_sums = stats(load_rows, mid)
        go(words[0])
        with scope("total"):
            total = totals.run(index, local_sums)
        weight_load(*weight)
        go(words[1])
        mean, scale = moments(total, inv, mid)
        ro[...] = jnp.concatenate(scale, axis=0)
        gain, bias = gain_bias(n)

        def rows(group, r0, c):
            xhat = (a[pl.ds(r0, 16), :] - mean[group]) * scale[group]
            a[pl.ds(r0, 16), :] = xhat
            h = xhat * gain + bias
            z[pl.ds(r0, 16), :] = (h * sigmoid(h)).astype(BF)
            return c

        with scope("wide norm"):
            chunks(s, 16, rows)
        zero_padding(s, z, mid)
        xc = pltpu.make_async_copy(a, xo, local.at[sem])
        zc = pltpu.make_async_copy(z, zo, local.at[sem + 1])
        xc.start()
        zc.start()
        return xc, zc

    def u_load(n, whole):
        return pltpu.make_async_copy(whole, wub, load.at[4, n])

    halos = [
        Halo(p, n, lambda side: hs.at[side], lambda side: hr.at[side], relay,
             (hs_send, hs_recv, pass_send, pass_recv), s.cut)
        for n in range(2)
    ]

    def weight_load(n, index):
        with scope("u weight"):
            for rel in range(4):
                gather[index].twins(rel)
            keep_own(index).wait()
            u_load(n, gather[index].whole).start()

    def temporal(n, words):
        with scope("u conv"):
            u_load(n, gather[1].whole).wait()
            hs[0] = jnp.dot(z[...], wub[:mid, :], preferred_element_type=F32).astype(BF)
            halos[n].start(0)
            hs[1] = jnp.dot(z[...], wub[2 * mid :, :], preferred_element_type=F32).astype(BF)
            halos[n].start(1)
            b[...] = jnp.dot(z[...], wub[mid : 2 * mid, :], preferred_element_type=F32)
        go(words)
        with scope("halo wait"):
            halos[n].relay()
            halos[n].wait(0)
            halos[n].wait(1)

    def narrow_total(index):
        def load_rows(group, r0, size):
            v = b[pl.ds(r0, size), :] + hr[0, pl.ds(r0, size), :].astype(F32) + hr[1, pl.ds(r0, size), :].astype(F32)
            b[pl.ds(r0, size), :] = v
            return v, v * v

        with scope("narrow stats"):
            local_sums = stats(load_rows, d)
        with scope("total"):
            return totals.run(index, local_sums)

    go("1z 0h1 0s1 0p0 1h1 0h2 0s2 0p1 0f0 1h2 0h3 0s3 1h3")
    spatial(0, gs1, (0, 1, 2, 3), ("0p2 0f1", "", "0p3", "1x 1s1 1s2 1s3", "0f2", "", "0f3 2z", "1p0 1f0"))
    xc1, zc1 = wide_norm(0, 0, z1_o, xh1_o, r1_o, 5, ("1p1 1f1 1p2 1f2 1p3 1f3", "2x"), (0, 1))
    temporal(0, "2h1 2l1 2h2 2l2 2h3 2l3")
    total = narrow_total(1)
    go("2a1 2a2 2a3 3z")
    mean2, scale2 = moments(total, inv, d)
    r2_o[...] = jnp.concatenate(scale2, axis=0)
    gain2, bias2 = gain_bias(1)

    def second(group, r0, c):
        xhat = (b[pl.ds(r0, 80), :] - mean2[group]) * scale2[group]
        b[pl.ds(r0, 80), :] = xhat
        h = xhat * gain2 + bias2
        grid_of_rows(s, grids, group, r0, (h * sigmoid(h)).astype(BF).astype(F32))
        return c

    with scope("norm2"):
        chunks(s, 80, second)
        clear_pad_cells(s, grids)
    xc2 = pltpu.make_async_copy(b, xh2_o, local.at[7])
    xc2.start()
    halos[0].done()
    taps_copy.wait()
    with scope("taps z2"):
        build_taps(s, grids, taps)
    taps_copy2 = pltpu.make_async_copy(taps, taps2_o, local.at[8])
    taps_copy2.start()
    xc1.wait()
    spatial(2, gs2, (0, 2, 1, 3), ("", "2v0 2v1 2v2 2v3", "2u0 2u1 3h1", "", "2u2 2u3 3h2", "3x 3s1 3s2", "2f0 2f1 2f2 2f3 3h3 3s3", ""))
    zc1.wait()
    xc3, zc3 = wide_norm(2, 2, z3_o, xh3_o, r3_o, 9, ("3p0 3f0 3p1 3f1 3p2 3f2 3p3 3f3", ""), (1, 3))
    xc2.wait()
    temporal(1, "")
    total = narrow_total(3)
    mean4, scale4 = moments(total, inv, d)
    r4_o[...] = jnp.concatenate(scale4, axis=0)
    gain4, bias4 = gain_bias(3)

    def last(group, r0, c):
        xhat = (b[pl.ds(r0, 80), :] - mean4[group]) * scale4[group]
        b[pl.ds(r0, 80), :] = xhat
        pre = xhat * gain4 + bias4 + x[pl.ds(r0, 80), :].astype(F32)
        gate = sigmoid(pre)
        alive = jnp.broadcast_to(live[group][None], (10, 8, d)).reshape(80, d)
        out[pl.ds(r0, 80), :] = alive * (pre * gate)
        up = alive * grad[pl.ds(r0, 80), :].astype(F32) * (gate * (1.0 + pre * (1.0 - gate)))
        dpre[pl.ds(r0, 80), :] = up
        return c

    with scope("norm4"):
        chunks(s, 80, last)
        zero_padding(s, dpre, d)
    xc4 = pltpu.make_async_copy(b, xh4_o, local.at[11])
    xc4.start()
    outs = [pltpu.make_async_copy(out, out_o, local.at[12]), pltpu.make_async_copy(dpre, dpre_o, local.at[13])]
    for c in outs:
        c.start()

    def last_rows(group, r0, size):
        v = dpre[pl.ds(r0, size), :]
        return v, v * b[pl.ds(r0, size), :]

    with scope("last stats"):
        local_sums = stats(last_rows, d)
    with scope("total"):
        last_o[...] = totals.run(4, local_sums)
    halos[1].done()
    with scope("finish"):
        for g in gather:
            g.finish()
    for n, src, dst in ((0, sw1, tb1), (1, sw2, tb2)):
        twin_copy(n, src, dst).wait_send()
    for c in (taps_copy2, zc3, xc3, xc4, *outs):
        c.wait()


def forward_call(s, x, grad, sw1, uw1, sw2, uw2, norm, live, inverse):
    any_, vmem, smem = (pl.BlockSpec(memory_space=m) for m in (pl.ANY, pltpu.VMEM, pltpu.SMEM))
    S = jax.ShapeDtypeStruct
    m, d, mid = s.m, s.d, s.mid
    gs = S((s.slabs, mid, s.kw), BF)
    gu = S((3 * mid, d), BF)
    taps = S((s.slabs, m, s.kw), BF)
    wide, narrow = S((m, mid), F32), S((m, d), F32)
    zs = S((m, mid), BF)
    outs = (gs, gu, gs, gu, taps, taps, wide, narrow, wide, narrow, zs, zs, narrow, narrow,
            S((2, mid), F32), S((2, d), F32), S((2, mid), F32), S((2, d), F32), S((4, d), F32))
    specs = (any_,) * 14 + (vmem,) * 5
    dma, V = pltpu.SemaphoreType.DMA, pltpu.VMEM
    nb = s.batches
    n_sums = 5
    scratch = [
        V((s.kw, s.nb), BF), V((s.kw, s.nb), BF), V((s.nb, s.kw), BF), V((s.nb, s.kw), BF),
        V((s.slabs, mid, s.kw), BF), V((3 * mid, d), BF), V((s.slabs, m, s.kw), BF),
        V((m, mid), F32), V((m, mid), BF),
        V((s.sides[0] + 2, s.sides[0] + 2, 8, d), F32), V((s.sides[1] + 2, s.sides[1] + 2, 8, d), F32),
        V((m, d), F32), V((2, m, d), BF), V((2, m, d), BF),
        V((n_sums, s.slots, 4, mid), F32), V((n_sums, nb, 4, mid), F32),
        dma((4, 5, 4, nb)), dma((4, 4, nb)), dma((4, 4, nb)), dma((2,)), dma((2,)), dma((14,)), dma((5, 2)),
        dma((2, 2, 2)), dma((2, 2, 2)), dma((2,)), dma((2,)), V((m - s.cut, d), BF),
        V((m, d), F32), V((m, d), F32),
        dma((n_sums, s.slots)), dma((n_sums, s.slots)), dma((n_sums, nb)), dma((n_sums, nb)),
    ]
    return pl.pallas_call(
        functools.partial(forward_kernel, s),
        out_shape=outs,
        in_specs=[vmem, vmem, vmem, any_, vmem, any_, vmem, vmem, smem],
        out_specs=specs,
        scratch_shapes=scratch,
        compiler_params=pltpu.CompilerParams(
            collective_id=0, has_side_effects=True, vmem_limit_bytes=63 * 2**20
        ),
        name="forward",
    )(x, grad, sw1, uw1, sw2, uw2, norm, live, inverse)


def cell_major(s, small, large):
    parts = []
    for group, v in enumerate((small, large)):
        v = v.reshape(s.clips, s.cells[group], s.d).transpose(1, 0, 2)
        parts.append(jnp.pad(v, ((0, s.padded[group] - s.cells[group]), (0, 0), (0, 0))))
    return jnp.concatenate(parts, axis=0).reshape(s.m, s.d)


def clip_major(s, v):
    v = v.reshape(-1, s.clips, s.d)
    parts, base = [], 0
    for group in range(2):
        part = v[base : base + s.cells[group]].transpose(1, 0, 2)
        parts.append(part.reshape(s.clips, 1, s.cells[group], s.d))
        base += s.padded[group]
    return parts


def halves(s, w):
    return w.astype(BF).reshape(w.shape[0], 2, s.nb).transpose(1, 0, 2)


def add_into(dst, src, rows, step):
    def body(i, _):
        at = pl.ds(pl.multiple_of(i * step, 16), step)
        dst[at, :] = (dst[at, :].astype(F32) + src[at, :].astype(F32)).astype(BF)
        return 0

    lax.fori_loop(0, rows // step, body, 0)


class Scatter:
    def __init__(self, place, index, part, bufs, cut, rows, step, sems):
        self.p, self.n, self.part, self.cut, self.rows, self.step = place, index, part, cut, rows, step
        self.tr, self.fx, self.fa, self.rx, self.ry, self.ru, self.rd = bufs
        self.twin_s, self.twin_r, self.block_s, self.block_r = sems
        self.half = place.batches // 2

    FAR, SIDE, DEEP, RISE, FALL = range(5)

    def twin_copy(self, rel):
        p = self.p
        return send(self.part(rel, 1 - p.core), self.tr.at[rel], self.twin_s.at[self.n, rel],
                    self.twin_r.at[self.n, rel], p.device(TWIN))

    def block_copy(self, kind, b, src, dst, way):
        return send(src, dst, self.block_s.at[self.n, kind, b], self.block_r.at[self.n, kind, b],
                    self.p.device(way))

    def own(self, rel, b):
        return self.cut(self.part(rel, self.p.core), b)

    def far_copy(self, b):
        if b < self.half:
            return self.block_copy(self.FAR, b, self.own(3, b), self.cut(self.fx, b), ACROSS)
        return self.block_copy(self.FAR, b, self.own(3, b), self.cut(self.fa, b - self.half), ALONG)

    def side_copy(self, b):
        return self.block_copy(self.SIDE, b, self.own(1, b), self.cut(self.rx, b), ACROSS)

    def deep_copy(self, b):
        return self.block_copy(self.DEEP, b, self.own(2, b), self.cut(self.ry, b), ALONG)

    def rise_copy(self, b):
        return self.block_copy(self.RISE, b, self.own(0, b), self.cut(self.ru, b), UP)

    def fall_copy(self, b):
        return self.block_copy(self.FALL, b, self.own(0, b), self.cut(self.rd, b), DOWN)

    def arrive(self, kind, b, ref):
        self.block_copy(kind, b, ref, ref, TWIN).wait_recv()

    def add(self, dst, src):
        add_into(dst, src, self.rows, self.step)

    def order(self):
        n = self.p.batches
        out = []
        for i in range(n // 2):
            out += [n - 1 - i, i]
        return out

    def twin(self, rel):
        self.twin_copy(rel).start()

    def join(self, rel):
        p = self.p
        self.twin_copy(rel).wait_recv()
        for b in self.order():
            self.add(self.own(rel, b), self.cut(self.tr.at[rel], b))
            if rel == 3:
                self.far_copy(b).start()
            if rel == 1 and b < self.half:
                self.side_copy(b).start()
            if rel == 2 and b >= self.half:
                self.deep_copy(b).start()

    def relay(self, b):
        if b < self.half:
            src = self.cut(self.fx, b)
            self.arrive(self.FAR, b, src)
            self.add(self.own(2, b), src)
            self.deep_copy(b).start()
        else:
            src = self.cut(self.fa, b - self.half)
            self.arrive(self.FAR, b, src)
            self.add(self.own(1, b), src)
            self.side_copy(b).start()

    def collect(self, b):
        for kind, buf in ((self.SIDE, self.rx), (self.DEEP, self.ry)):
            src = self.cut(buf, b)
            self.arrive(kind, b, src)
            self.add(self.own(0, b), src)

    def chain(self, b):
        p = self.p

        @pl.when(p.z < b)
        def _():
            @pl.when(p.z > 0)
            def _():
                self.arrive(self.RISE, b, self.cut(self.ru, b))
                self.add(self.own(0, b), self.cut(self.ru, b))

            self.rise_copy(b).start()

        @pl.when(p.z > b)
        def _():
            @pl.when(p.z < p.batches - 1)
            def _():
                self.arrive(self.FALL, b, self.cut(self.rd, b))
                self.add(self.own(0, b), self.cut(self.rd, b))

            self.fall_copy(b).start()

    def tail(self):
        p = self.p

        @pl.when(p.z < self.half)
        def _():
            for b in range(p.batches - 1, -1, -1):
                self.collect(b)
                self.chain(b)

        @pl.when(p.z >= self.half)
        def _():
            for b in range(p.batches):
                self.collect(b)
                self.chain(b)

    def result(self):
        p = self.p
        pl.when(p.z > 0)(lambda: self.arrive(self.RISE, p.z, self.cut(self.ru, p.z)))
        pl.when(p.z < p.batches - 1)(lambda: self.arrive(self.FALL, p.z, self.cut(self.rd, p.z)))

        @pl.when(p.z == 0)
        def _():
            ref = self.cut(self.ru, p.z)
            ref[...] = jnp.zeros(ref.shape, BF)

        @pl.when(p.z == p.batches - 1)
        def _():
            ref = self.cut(self.rd, p.z)
            ref[...] = jnp.zeros(ref.shape, BF)

        return (
            self.own(0, p.z)[...].astype(F32)
            + self.cut(self.ru, p.z)[...].astype(F32)
            + self.cut(self.rd, p.z)[...].astype(F32)
        )

    def sent(self):
        p = self.p
        for rel in range(4):
            self.twin_copy(rel).wait_send()
        for b in range(p.batches):
            self.far_copy(b).wait_send()
            self.side_copy(b).wait_send()
            self.deep_copy(b).wait_send()
            pl.when(p.z < b)(lambda b=b: self.rise_copy(b).wait_send())
            pl.when(p.z > b)(lambda b=b: self.fall_copy(b).wait_send())

    def act(self, word):
        if word == "t":
            self.tail()
        else:
            {"j": self.join, "r": self.relay}[word[0]](int(word[1]))


class LineScatter(Scatter):
    def rise(self, rel, b):
        return send(self.own(rel, b), self.cut(self.ru.at[rel], b), self.line_s.at[self.n, 0, rel, b],
                    self.line_r.at[self.n, 0, rel, b], self.p.device(UP))

    def fall(self, rel, b):
        return send(self.own(rel, b), self.cut(self.rd.at[rel], b), self.line_s.at[self.n, 1, rel, b],
                    self.line_r.at[self.n, 1, rel, b], self.p.device(DOWN))

    def landed(self, way, rel, b):
        buf = (self.ru, self.rd)[way]
        ref = self.cut(buf.at[rel], b)
        send(ref, ref, self.line_s.at[self.n, way, rel, b], self.line_r.at[self.n, way, rel, b],
             self.p.device(TWIN)).wait_recv()
        return ref

    def join(self, rel):
        p = self.p
        self.twin_copy(rel).wait_recv()
        add_into(self.part(rel, p.core), self.tr.at[rel], self.rows, self.step)

    def ends(self, up, down):
        p = self.p

        @pl.when(p.z == 0)
        def _():
            for rel in (3, 1, 2, 0):
                self.rise(rel, up).start()

        @pl.when(p.z == p.batches - 1)
        def _():
            for rel in (3, 1, 2, 0):
                self.fall(rel, down).start()

    def chain(self, stage):
        p = self.p

        @pl.when(p.z == stage)
        def _():
            for b in range(p.batches - 1, stage, -1):
                for rel in (3, 1, 2, 0):
                    self.add(self.own(rel, b), self.landed(0, rel, b))
                    self.rise(rel, b).start()

        @pl.when(p.z == p.batches - 1 - stage)
        def _():
            for b in range(p.batches - 1 - stage):
                for rel in (3, 1, 2, 0):
                    self.add(self.own(rel, b), self.landed(1, rel, b))
                    self.fall(rel, b).start()

    def settle(self, rel):
        p = self.p
        at = self.own(rel, p.z)
        pl.when(p.z > 0)(lambda: self.add(at, self.landed(0, rel, p.z)))
        pl.when(p.z < p.batches - 1)(lambda: self.add(at, self.landed(1, rel, p.z)))

    def cross(self, kind, rel, dst, way):
        return self.block_copy(kind, 0, self.own(rel, self.p.z), dst, way)

    def corner(self):
        self.settle(3)
        self.cross(self.FAR, 3, self.fx, ACROSS).start()
        self.settle(1)
        self.cross(self.SIDE, 1, self.rx, ACROSS).start()
        self.settle(2)

    def turn(self):
        self.arrive(self.FAR, 0, self.fx)
        self.add(self.own(2, self.p.z), self.fx)
        self.cross(self.DEEP, 2, self.ry, ALONG).start()
        self.settle(0)

    def result(self):
        self.arrive(self.SIDE, 0, self.rx)
        self.arrive(self.DEEP, 0, self.ry)
        return (self.own(0, self.p.z)[...].astype(F32) + self.rx[...].astype(F32) + self.ry[...].astype(F32))

    def sent(self):
        p = self.p
        for rel in range(4):
            self.twin_copy(rel).wait_send()
            for b in range(p.batches):
                pl.when(p.z < b)(lambda rel=rel, b=b: self.rise(rel, b).wait_send())
                pl.when(p.z > b)(lambda rel=rel, b=b: self.fall(rel, b).wait_send())
        self.cross(self.FAR, 3, self.fx, ACROSS).wait_send()
        self.cross(self.SIDE, 1, self.rx, ACROSS).wait_send()
        self.cross(self.DEEP, 2, self.ry, ALONG).wait_send()

    def act(self, word):
        if word[0] == "j":
            self.join(int(word[1]))
        elif word[0] == "k":
            self.chain(int(word[1]))
        elif word[0] == "z":
            self.ends(int(word[1]), int(word[2]))
        else:
            {"c": self.corner, "t": self.turn}[word]()


def rows_of_grid(s, grids, group, r0):
    side = s.sides[group]
    base = 0 if group == 0 else s.rows[0]
    first = (r0 - base) // 8
    cells = [grids[group][1 + (first + n) // side, 1 + lax.rem(first + n, side)] for n in range(10)]
    return jnp.concatenate(cells, axis=0)


def slope(v):
    gate = sigmoid(v)
    return gate * (1.0 + v * (1.0 - gate))


def backward_kernel(s, *refs):
    (gs1, gu1, gs2, gu2, taps1, taps2, xh1, xh2, xh3, xh4, z1, z3, dpre,
     r1, r2, r3, r4, last, norm, live_ref, inverse,
     dx, gso1, gso2, guo1, guo2, ng, square,
     ps, tr, fx, fa, rx, ry, ru, rd, pu, utr, ufx, urx, ury, uru, urd, relay,
     nat, flip, d3, turn, gsh, planes, lines,
     load, tap_sem, tile_sem, halo_send, halo_recv, pass_send, pass_recv, line_s, line_r, twin_s, twin_r, block_s, block_r, half_s, half_r,
     pl_send, pl_recv, ln_send, ln_recv) = refs
    p = Place(s.batches, s.slots)
    live = [live_ref[g] for g in range(2)]
    inv = [inverse[g] for g in range(2)]
    totals = Totals(p, 4, planes, lines, (pl_send, pl_recv, ln_send, ln_recv))
    d, mid, m = s.d, s.mid, s.m
    bounds = (0, mid, mid + d, 2 * mid + d, 2 * mid + 2 * d)

    def gain_bias(n):
        return norm[0:1, bounds[n] : bounds[n + 1]], norm[1:2, bounds[n] : bounds[n + 1]]

    with scope("greet"):
        p.greet()
    def go(words):
        with scope("reduce " + words):
            for word in words.split():
                scatter(int(word[0])).act(word[1:])

    def cut_rows(ref, b):
        at = b * s.nb if isinstance(b, int) else pl.multiple_of(b * s.nb, 16)
        return ref.at[pl.ds(at, s.nb)]

    def cut_lanes(ref, b):
        at = b * s.uc if isinstance(b, int) else pl.multiple_of(b * s.uc, 128)
        return ref.at[:, pl.ds(at, s.uc)]

    def part_s(rel, core):
        return ps.at[rel, core]

    def part_u(rel, core):
        return pu.at[pl.ds(pl.multiple_of((p.rel[rel] * 2 + core) * s.ur, 16), s.ur)]

    sems = (twin_s, twin_r, block_s, block_r)

    def scatter(n):
        if n % 2 == 0:
            return Scatter(p, n, part_s, (tr, fx, fa, rx, ry, ru, rd), cut_rows, s.nb, 48, sems)
        sc = LineScatter(p, n, part_u, (utr, ufx, None, urx, ury, uru, urd), cut_lanes, s.ur, 144, sems)
        sc.line_s, sc.line_r = line_s, line_r
        return sc

    for side, edge in ((0, p.slots - 1), (2, 0)):
        @pl.when(p.t == edge)
        def _(side=side):
            d3[side] = jnp.zeros(d3.shape[1:], BF)

    def norm_back(n, total, scale, dh, xhat, store, size, width):
        gain, _ = gain_bias(n)
        ng[0:1, bounds[n] : bounds[n + 1]] = total[2:3, :] + total[3:4, :]
        ng[1:2, bounds[n] : bounds[n + 1]] = total[0:1, :] + total[1:2, :]
        lead = [gain * scale[g : g + 1, :] for g in range(2)]
        mean = [total[g : g + 1, :] * inv[g] for g in range(2)]
        cross = [total[2 + g : 3 + g, :] * inv[g] for g in range(2)]

        def rows(group, r0, c):
            at = pl.ds(r0, size)
            v = lead[group] * (dh[at, :] - mean[group] - xhat[at, :] * cross[group])
            v = v.reshape(size // 8, 8, width) * live[group][None]
            store(at, v.reshape(size, width))
            return c

        chunks(s, size, rows)

    def upstream(n, dz, xhat, fetch, size, width):
        gain, bias = gain_bias(n)

        def body(group, r0, c):
            at = pl.ds(r0, size)
            xv = xhat[at, :]
            v = fetch(group, r0) * slope(xv * gain + bias)
            dz[at, :] = v
            return (c[0] + jnp.sum(v.reshape(size // 8, 8, width), axis=0),
                    c[1] + jnp.sum((v * xv).reshape(size // 8, 8, width), axis=0))

        zero = jnp.zeros((8, width), F32)
        small, large = chunks(s, size, body, (zero, zero))
        rows = [jnp.sum(v * live[g], axis=0, keepdims=True) for v, g in
                ((small[0], 0), (large[0], 1), (small[1], 0), (large[1], 1))]
        return jnp.concatenate(rows, axis=0)

    def transpose():
        def body(j, _):
            at = pl.ds(pl.multiple_of(j * 128, 128), 128)
            flip[at, :] = nat[:, at].T
            return 0

        with scope("transpose"):
            lax.fori_loop(0, mid // 128, body, 0)

    def fetch_into(src, dst, sem):
        c = pltpu.make_async_copy(src, dst, load.at[sem])
        c.start()
        return c

    def narrow_store(at, v):
        d3[1, at, :] = v.astype(BF)

    def nat_store(at, v):
        nat[at, :] = v.astype(BF)

    def first(up, xh):
        c1, c2 = fetch_into(dpre, up, 0), fetch_into(xh4, xh, 1)
        c1.wait()
        c2.wait()
        norm_back(3, last[...], r4[...], up, xh, narrow_store, 80, d)

    fetch_into(z3, nat, 2)
    with scope("norm4 back"):
        pl.run_scoped(first, pltpu.VMEM((m, d), F32), pltpu.VMEM((m, d), F32))
    zero_padding(s, d3.at[1], d)

    def temporal(stage, index, n, whole, zs, xhs, scale, words, before, finish):
        halo = Halo(p, stage, lambda side: d3.at[1], lambda side: d3.at[2 - 2 * side], relay,
                    (halo_send, halo_recv, pass_send, pass_recv), s.cut)

        def run(dz, xh, wu):
            halo.start(0)
            halo.start(1)
            cz = pltpu.make_async_copy(zs, nat, load.at[2])
            if stage:
                cz.start()
            cw = fetch_into(whole, wu, 3)
            cx = fetch_into(xhs, xh, 4)
            cz.wait()
            transpose()
            cw.wait()

            def grads(k):
                for lo, width in wide_cuts(mid):
                    y = lax.dot_general(d3[k], wu[k * mid + lo : k * mid + lo + width, :], NT_DIMS,
                                        preferred_element_type=F32)
                    if k == 1:
                        dz[:, lo : lo + width] = y
                    else:
                        dz[:, lo : lo + width] += y
                pu[k * mid : (k + 1) * mid, :] = jnp.dot(
                    flip[...], d3[k], preferred_element_type=F32
                ).astype(BF)

            extra = before()
            with scope("u grads"):
                grads(1)
            go(words[0])
            with scope("halo wait"):
                halo.relay()
                halo.wait(1)
            with scope("u grads"):
                grads(0)
            with scope("halo wait"):
                halo.wait(0)
            go(words[3])
            with scope("u grads"):
                grads(2)
            sc = scatter(index)
            for rel in (3, 1, 2, 0):
                sc.twin(rel)
            go(words[1])
            cx.wait()

            def fetch(group, r0):
                return dz[pl.ds(r0, 16), :]

            with scope("upstream"):
                local_sums = upstream(n, dz, xh, fetch, 16, mid)
            go(words[2])
            extra = extra + finish()
            with scope("total"):
                total = totals.run(2 * stage, local_sums)
            with scope("norm back"):
                norm_back(n, total, scale, dz, xh, nat_store, 16, mid)
            return extra

        extra = pl.run_scoped(run, pltpu.VMEM((m, mid), F32), pltpu.VMEM((m, mid), F32), pltpu.VMEM((3 * mid, d), BF))
        zero_padding(s, nat, mid)
        halo.done()
        return extra

    def finish_u(n, ref):
        sc = scatter(n)
        g = sc.result()
        ref[...] = g
        sc.sent()
        return jnp.sum(g * g, axis=0, keepdims=True)

    def finish_s(n, out):
        sc = scatter(n)
        ref = gsh
        g = sc.result()
        turn[...] = g.T
        mine = turn[pl.ds(pl.multiple_of(p.core * (s.kw // 2), 16), s.kw // 2), :]
        ref[p.core] = mine
        copy = send(turn.at[pl.ds(pl.multiple_of((1 - p.core) * (s.kw // 2), 16), s.kw // 2)], ref.at[p.core],
                    half_s.at[n // 2], half_r.at[n // 2], p.device(TWIN))
        copy.start()
        sc.sent()
        send(turn.at[pl.ds(0, s.kw // 2)], ref.at[1 - p.core], half_s.at[n // 2], half_r.at[n // 2],
             p.device(TWIN)).wait_recv()
        copy.wait_send()
        keep = pltpu.make_async_copy(ref, out, load.at[8])
        keep.start()
        keep.wait()
        return jnp.sum(jnp.sum((g * g).reshape(s.nb, s.kw // 128, 128), axis=0), axis=0, keepdims=True)

    pieces = []
    for tap in range(9):
        lo, end, found = tap * d, (tap + 1) * d, []
        while lo < end:
            hi = min(end, (lo // s.kw + 1) * s.kw)
            found.append((lo // s.kw, lo % s.kw, lo - tap * d, hi - lo))
            lo = hi
        pieces.append(found)

    def spatial(index, whole, taps, grids, tap_buf, tile, words, tap_words, early):
        rels = (3, 1, 2, 0)

        def tap_load(i):
            return pltpu.make_async_copy(taps.at[p.rel[rels[i]]], tap_buf.at[i % 2], tap_sem.at[i])

        def tile_loads(tap):
            return [
                pltpu.make_async_copy(
                    whole.at[slab, :, pl.ds(lane, width)], tile.at[tap % 2, :, pl.ds(at, width)],
                    tile_sem.at[tap, n],
                )
                for n, (slab, lane, at, width) in enumerate(pieces[tap])
            ]

        tap_load(0).start()
        tap_load(1).start()
        for c in tile_loads(0):
            c.start()
        go(early)
        transpose()
        for grid in grids:
            def clear(i, _, grid=grid):
                grid[i] = jnp.zeros(grid.shape[1:], F32)
                return 0

            lax.fori_loop(0, grid.shape[0], clear, 0)
        sc = scatter(index)
        for i, rel in enumerate(rels):
            tap_load(i).wait()
            with scope("dw slab"):
                for lo, width in wide_cuts(s.kw):
                    y = jnp.dot(flip[...], tap_buf[i % 2, :, lo : lo + width], preferred_element_type=F32).astype(BF)
                    for n in range(2 * s.batches):
                        b, core = n // 2, n % 2
                        ps[rel, core, b * s.nb : (b + 1) * s.nb, lo : lo + width] = y[n * s.nb : (n + 1) * s.nb]
            sc.twin(rel)
            if i + 2 < 4:
                tap_load(i + 2).start()
            go(words[i])
        for tap in range(9):
            if tap + 1 < 9:
                for c in tile_loads(tap + 1):
                    c.start()
            for c in tile_loads(tap):
                c.wait()
            i, j = tap // 3, tap % 3
            with scope("dx tap"):
                y = jnp.dot(nat[...], tile[tap % 2], preferred_element_type=F32)
                base = 0
                for group in range(2):
                    side = s.sides[group]
                    part = y[base : base + s.cells[group] * 8].reshape(side, side, 8, d)
                    grids[group][i : i + side, j : j + side] += part
                    base += s.rows[group]
            go(tap_words[tap])
        clear_pad_cells(s, grids)

    def spatial_types():
        return (
            pltpu.VMEM((s.sides[0] + 2, s.sides[0] + 2, 8, d), F32),
            pltpu.VMEM((s.sides[1] + 2, s.sides[1] + 2, 8, d), F32),
            pltpu.VMEM((2, m, s.kw), BF), pltpu.VMEM((2, mid, d), BF),
            pltpu.VMEM((m, d), F32), pltpu.VMEM((m, d), F32),
        )

    nothing = jnp.zeros((1, 128), F32)
    temporal(0, 3, 2, gu2, z3, xh3, r3[...], ("", "", "3j3 3j1 3j2 3j0", ""), lambda: nothing, lambda: nothing)

    def second(grid_s, grid_l, tap_buf, tile, b, xh):
        cx = fetch_into(xh2, xh, 5)
        spatial(2, gs2, taps2, (grid_s, grid_l), tap_buf, tile,
                ("", "2j3", "2j1", "2j2"),
                ("2j0 3k1", "", "2r0 2r1", "", "3k2", "", "", "", ""), "3z30 3z21 3z12")
        cx.wait()

        def fetch(group, r0):
            return rows_of_grid(s, (grid_s, grid_l), group, r0)

        with scope("upstream"):
            local_sums = upstream(1, b, xh, fetch, 80, d)
        with scope("total"):
            total = totals.run(1, local_sums)
        with scope("norm back"):
            norm_back(1, total, r2[...], b, xh, narrow_store, 80, d)

    pl.run_scoped(second, *spatial_types())
    zero_padding(s, d3.at[1], d)

    def finish_second():
        with scope("finish s"):
            return finish_s(2, gso2)

    def finish_first():
        go("3c 3t")
        with scope("finish u"):
            return finish_u(3, guo2)

    sums = temporal(1, 1, 0, gu1, z1, xh1, r1[...],
                    ("2r3 2r2", "", "2t 1j3 1j1 1j2 1j0", ""), finish_first, finish_second)

    def final(grid_s, grid_l, tap_buf, tile, b, up):
        cx = fetch_into(dpre, up, 6)
        spatial(0, gs1, taps1, (grid_s, grid_l), tap_buf, tile,
                ("", "0j3", "0j1", "0j2"),
                ("0j0 1k1", "", "", "0r0 0r3 0r1 0r2", "", "1k2", "", "", ""), "1z30 1z21 1z12")
        cx.wait()

        def rows(group, r0, c):
            b[pl.ds(r0, 80), :] = rows_of_grid(s, (grid_s, grid_l), group, r0) + up[pl.ds(r0, 80), :]
            return c

        with scope("dx"):
            chunks(s, 80, rows)
        cd = fetch_into(b, dx, 7)
        go("0t")
        go("1c")
        go("1t")
        with scope("finish u"):
            sums = finish_u(1, guo1)
        with scope("finish s"):
            sums = sums + finish_s(0, gso1)
        cd.wait()
        return sums

    sums = sums + pl.run_scoped(final, *spatial_types())
    with scope("total"):
        square[...] = totals.run(3, jnp.broadcast_to(sums, (4, 128)))


def backward_call(s, saved, norm, live, inverse):
    any_, vmem, smem = (pl.BlockSpec(memory_space=m) for m in (pl.ANY, pltpu.VMEM, pltpu.SMEM))
    S, V, dma = jax.ShapeDtypeStruct, pltpu.VMEM, pltpu.SemaphoreType.DMA
    m, d, mid, nb, kw = s.m, s.d, s.mid, s.batches, s.kw
    half = nb // 2
    outs = (S((m, d), F32), S((2, kw // 2, s.nb), F32), S((2, kw // 2, s.nb), F32),
            S((s.ur, s.uc), F32), S((s.ur, s.uc), F32), S((2, 2 * (mid + d)), F32), S((4, 128), F32))
    rows = nb * s.nb
    scratch = [
        V((4, 2, rows, kw), BF), V((4, rows, kw), BF), V((half * s.nb, kw), BF), V((half * s.nb, kw), BF),
        V((rows, kw), BF), V((rows, kw), BF), V((rows, kw), BF), V((rows, kw), BF),
        V((3 * mid, d), BF), V((4, s.ur, d), BF), V((s.ur, s.uc), BF), V((s.ur, s.uc), BF), V((s.ur, s.uc), BF),
        V((4, s.ur, d), BF), V((4, s.ur, d), BF), V((m - s.cut, d), BF),
        V((m, mid), BF), V((mid, m), BF), V((3, m, d), BF), V((kw, s.nb), F32),
        V((2, kw // 2, s.nb), F32),
        V((4, s.slots, 4, mid), F32), V((4, nb, 4, mid), F32),
        dma((9,)), dma((4,)), dma((9, 3)), dma((2, 2, 2)), dma((2, 2, 2)), dma((2,)), dma((2,)),
        dma((4, 2, 4, nb)), dma((4, 2, 4, nb)),
        dma((4, 4)), dma((4, 4)), dma((4, 5, nb)), dma((4, 5, nb)), dma((2,)), dma((2,)),
        dma((4, s.slots)), dma((4, s.slots)), dma((4, nb)), dma((4, nb)),
    ]
    return pl.pallas_call(
        functools.partial(backward_kernel, s),
        out_shape=outs,
        in_specs=[any_] * 13 + [vmem] * 7 + [smem],
        out_specs=(any_,) * 3 + (vmem,) * 4,
        scratch_shapes=scratch,
        compiler_params=pltpu.CompilerParams(
            collective_id=1, has_side_effects=True, vmem_limit_bytes=63 * 2**20
        ),
        name="backward",
    )(*saved, norm, live, inverse)


def body(batches, slots, *args):
    x_small, x_large = args[0], args[1]
    if not fits(x_small.shape, x_large.shape, batches, slots):
        return plain_body(*args)
    return fast_body(Shape(x_small.shape, x_large.shape, batches, slots), *args)


def fast_body(
    s,
    x_small,
    x_large,
    grad_small,
    grad_large,
    clip_counts,
    first_spatial,
    first_temporal,
    second_spatial,
    second_temporal,
    norm_params,
    first_spatial_momentum,
    first_temporal_momentum,
    second_spatial_momentum,
    second_temporal_momentum,
    norm_momentum,
    first_spatial_variance,
    first_temporal_variance,
    second_spatial_variance,
    second_temporal_variance,
    norm_variance,
):
    z = lax.axis_index("batch")
    slots = jnp.arange(s.clips, dtype=jnp.int32)
    counts = lax.dynamic_index_in_dim(clip_counts, z, 1, keepdims=False)
    live = (slots[None, :] < counts[:, None]).astype(F32)[:, :, None]
    totals = jnp.sum(clip_counts, axis=1).astype(F32) * (s.slots * jnp.array(s.cells, F32))
    inverse = 1.0 / totals
    x = cell_major(s, x_small, x_large)
    grad = cell_major(s, grad_small, grad_large)
    res = forward_call(
        s, x, grad, halves(s, first_spatial), first_temporal.astype(BF), halves(s, second_spatial),
        second_temporal.astype(BF), norm_params, live, inverse,
    )
    out_small, out_large = clip_major(s, res[12])
    saved = res[:12] + res[13:]
    dx, gs1, gs2, gu1, gu2, grad_params, square = backward_call(s, saved, norm_params, live, inverse)
    in_small, in_large = clip_major(s, dx)

    def whole(g):
        return g.transpose(1, 0, 2).reshape(g.shape[1], 2 * g.shape[2])

    grad_norm = jnp.sqrt(jnp.sum(square[0]) + jnp.sum(grad_params * grad_params))
    factor = THRESHOLD / jnp.maximum(grad_norm, THRESHOLD)
    one = adamw(first_spatial, whole(gs1), first_spatial_momentum, first_spatial_variance, factor,
                WEIGHT_RATE, WEIGHT_DECAY)
    two = adamw(first_temporal, gu1, first_temporal_momentum, first_temporal_variance, factor,
                WEIGHT_RATE, WEIGHT_DECAY)
    three = adamw(second_spatial, whole(gs2), second_spatial_momentum, second_spatial_variance, factor,
                  WEIGHT_RATE, WEIGHT_DECAY)
    four = adamw(second_temporal, gu2, second_temporal_momentum, second_temporal_variance, factor,
                 WEIGHT_RATE, WEIGHT_DECAY)
    norms = adamw(norm_params, grad_params, norm_momentum, norm_variance, factor, NORM_RATE, 0.0)
    return (out_small, out_large, in_small, in_large, grad_norm) + one + two + three + four + norms


def solution(mesh):
    return jax.shard_map(
        functools.partial(body, mesh.shape["batch"], mesh.shape["tm"]),
        mesh=mesh,
        in_specs=(
            P("batch", "tm", None, None),
            P("batch", "tm", None, None),
            P("batch", "tm", None, None),
            P("batch", "tm", None, None),
            P(),
            P("tm", "batch"),
            P("tm", "batch"),
            P("tm", "batch"),
            P("tm", "batch"),
            P(),
            P("tm", "batch"),
            P("tm", "batch"),
            P("tm", "batch"),
            P("tm", "batch"),
            P(),
            P("tm", "batch"),
            P("tm", "batch"),
            P("tm", "batch"),
            P("tm", "batch"),
            P(),
        ),
        out_specs=(
            P("batch", "tm", None, None),
            P("batch", "tm", None, None),
            P("batch", "tm", None, None),
            P("batch", "tm", None, None),
            P(),
            P("tm", "batch"),
            P("tm", "batch"),
            P("tm", "batch"),
            P("tm", "batch"),
            P("tm", "batch"),
            P("tm", "batch"),
            P("tm", "batch"),
            P("tm", "batch"),
            P("tm", "batch"),
            P("tm", "batch"),
            P("tm", "batch"),
            P("tm", "batch"),
            P(),
            P(),
            P(),
        ),
        check_vma=False,
    )
```

```python
import contextlib
import functools
import math

import jax
import jax.numpy as jnp
from jax import lax
from jax.experimental import pallas as pl
from jax.experimental.pallas import tpu as pltpu
from jax.sharding import PartitionSpec as P

D = 512
MID = 1152
HS = 7
HL = 10
STEP = 10


NORM_EPS = 1e-05
THRESHOLD = 1.0
BETA_ONE = 0.9
BETA_TWO = 0.999
WEIGHT_RATE = 0.03
NORM_RATE = 0.25
WEIGHT_DECAY = 0.05
ADAM_EPS = 1e-08


def padded_2(value, sides, width):
    for axis, dim in sides:
        size, length = (lax.axis_size(axis), value.shape[dim])
        up = [(i, (i + 1) % size) for i in range(size - 1)]
        down = [(j, i) for i, j in up]
        last = lax.slice_in_dim(value, length - width, length, axis=dim)
        first = lax.slice_in_dim(value, 0, width, axis=dim)
        before = lax.ppermute(last, axis, up)
        after = lax.ppermute(first, axis, down)
        value = jnp.concatenate([before, value, after], axis=dim)
    return value


def silu_slope(input_value):
    sigmoid_value = jax.nn.sigmoid(input_value)
    return sigmoid_value * (1.0 + input_value * (1.0 - sigmoid_value))


def spatial_taps(field, side):
    clips, frames, cells, channels = field.shape
    grid = field.reshape(clips, frames, side, side, channels)
    padded = jnp.pad(grid, ((0, 0), (0, 0), (1, 1), (1, 1), (0, 0)))
    pieces = [
        padded[:, :, row : row + side, column : column + side, :]
        for row in range(3)
        for column in range(3)
    ]
    return jnp.concatenate(pieces, axis=-1).reshape(clips * frames * cells, 9 * channels)


def spatial_forward(field_small, field_large, weight):
    taps_small = spatial_taps(field_small, HS)
    taps_large = spatial_taps(field_large, HL)
    result_small = jnp.dot(taps_small, weight, preferred_element_type=jnp.float32).reshape(
        field_small.shape[:3] + (weight.shape[1],)
    )
    result_large = jnp.dot(taps_large, weight, preferred_element_type=jnp.float32).reshape(
        field_large.shape[:3] + (weight.shape[1],)
    )
    return (jnp.concatenate([result_small, result_large], axis=2), taps_small, taps_large)


def spatial_backward(upstream_rows, weight, shape, side):
    clips, frames, cells, channels = shape
    columns = lax.dot_general(
        upstream_rows, weight, (((1,), (1,)), ((), ())), preferred_element_type=jnp.float32
    )
    columns = columns.reshape(clips, frames, side, side, 9 * channels)
    padded = jnp.pad(columns, ((0, 0), (0, 0), (1, 1), (1, 1), (0, 0)))
    final_result = None
    for row in range(3):
        for column in range(3):
            offset = (3 * row + column) * channels
            window = padded[
                :,
                :,
                2 - row : 2 - row + side,
                2 - column : 2 - column + side,
                offset : offset + channels,
            ]
            final_result = window if final_result is None else final_result + window
    return final_result.reshape(clips, frames, cells, channels)


def temporal_forward(field, weight):
    padded = padded_2(field, (("tm", 1),), 1)
    frames = field.shape[1]
    pieces = jnp.concatenate([padded[:, shift : shift + frames] for shift in range(3)], axis=-1)
    rows = pieces.reshape(-1, pieces.shape[-1])
    final_result = jnp.dot(rows, weight, preferred_element_type=jnp.float32).reshape(
        field.shape[:3] + (weight.shape[1],)
    )
    return (final_result, rows)


def temporal_backward(upstream_gradient, weight):
    padded = padded_2(upstream_gradient, (("tm", 1),), 1)
    frames = upstream_gradient.shape[1]
    pieces = jnp.concatenate(
        [padded[:, 2 - shift : 2 - shift + frames] for shift in range(3)], axis=-1
    )
    rows = pieces.reshape(-1, pieces.shape[-1])
    kernel = (
        weight.reshape(3, -1, weight.shape[1]).transpose(1, 0, 2).reshape(-1, 3 * weight.shape[1])
    )
    final_result = lax.dot_general(
        rows, kernel, (((1,), (1,)), ((), ())), preferred_element_type=jnp.float32
    )
    return final_result.reshape(upstream_gradient.shape[:3] + (kernel.shape[0],))


def group_totals(leading_part, trailing_part, active_flags, split_point):
    leading_cells = jnp.sum(active_flags * leading_part, axis=(0, 1))
    trailing_cells = jnp.sum(active_flags * trailing_part, axis=(0, 1))
    first_groups = jnp.stack(
        [jnp.sum(leading_cells[:split_point], axis=0), jnp.sum(leading_cells[split_point:], axis=0)]
    )
    second_groups = jnp.stack(
        [
            jnp.sum(trailing_cells[:split_point], axis=0),
            jnp.sum(trailing_cells[split_point:], axis=0),
        ]
    )
    return (first_groups, second_groups)


def per_cell(stat, split_point, cells):
    channels = stat.shape[1]
    return jnp.concatenate(
        [
            jnp.broadcast_to(stat[0], (split_point, channels)),
            jnp.broadcast_to(stat[1], (cells - split_point, channels)),
        ],
        axis=0,
    )


def norm_forward_pass(
    input_value, active_flags, split_point, grand_totals, norm_gain_vector, norm_shift_bias
):
    running_sums, squared_values = group_totals(
        input_value, input_value * input_value, active_flags, split_point
    )
    running_sums, squared_values = lax.psum((running_sums, squared_values), ("batch", "tm"))
    mean = running_sums / grand_totals[:, None]
    scale = lax.rsqrt(squared_values / grand_totals[:, None] - mean * mean + NORM_EPS)
    cells = input_value.shape[2]
    cell_scale = per_cell(scale, split_point, cells)
    normalized_values = (input_value - per_cell(mean, split_point, cells)) * cell_scale
    return (normalized_values * norm_gain_vector + norm_shift_bias, normalized_values, cell_scale)


def norm_reverse_pass(
    upstream_gradient,
    normalized_values,
    cell_scale,
    norm_gain_vector,
    active_flags,
    split_point,
    grand_totals,
):
    running_sums, cross_product = group_totals(
        upstream_gradient, upstream_gradient * normalized_values, active_flags, split_point
    )
    running_sums, cross_product = lax.psum((running_sums, cross_product), ("batch", "tm"))
    cells = upstream_gradient.shape[2]
    upstream_average = per_cell(running_sums / grand_totals[:, None], split_point, cells)
    cross_average = per_cell(cross_product / grand_totals[:, None], split_point, cells)
    final_result = (
        active_flags
        * (norm_gain_vector * cell_scale)
        * (upstream_gradient - upstream_average - normalized_values * cross_average)
    )
    return (final_result, jnp.sum(cross_product, axis=0), jnp.sum(running_sums, axis=0))


def reduce_weight(pairs, depth, width):
    total = jnp.zeros((depth // lax.axis_size("tm") * lax.axis_size("tm"), width), jnp.float32)
    for left, right in pairs:
        total = total + lax.dot_general(
            left, right, (((0,), (0,)), ((), ())), preferred_element_type=jnp.float32
        )
    shared = lax.psum_scatter(total.astype(jnp.bfloat16), "tm", scatter_dimension=0, tiled=True)
    return lax.psum_scatter(shared, "batch", scatter_dimension=1, tiled=True).astype(jnp.float32)


def own_square(shard):
    local = jnp.sum(shard * shard)
    return local


def adamw(weight, gradient, momentum, variance, factor, rate, decay):
    clipped = gradient * factor
    new_momentum = BETA_ONE * momentum + (1.0 - BETA_ONE) * clipped
    new_variance = BETA_TWO * variance + (1.0 - BETA_TWO) * clipped * clipped
    corrected = new_momentum / (1.0 - BETA_ONE**STEP)
    spread = jnp.sqrt(new_variance / (1.0 - BETA_TWO**STEP))
    new_weight = weight - rate * (corrected / (spread + ADAM_EPS) + decay * weight)
    return (new_weight, new_momentum, new_variance)


def plain_body(
    x_small,
    x_large,
    small_output_gradient,
    large_output_gradient,
    clip_counts,
    first_spatial,
    first_temporal,
    second_spatial,
    second_temporal,
    norm_params,
    first_spatial_momentum,
    first_temporal_momentum,
    second_spatial_momentum,
    second_temporal_momentum,
    norm_momentum,
    first_spatial_variance,
    first_temporal_variance,
    second_spatial_variance,
    second_temporal_variance,
    norm_variance,
):
    low_one = first_spatial.astype(jnp.bfloat16)
    low_two = first_temporal.astype(jnp.bfloat16)
    low_three = second_spatial.astype(jnp.bfloat16)
    low_four = second_temporal.astype(jnp.bfloat16)
    columns = (
        lax.all_gather(low_one, "batch", axis=1, tiled=True),
        lax.all_gather(low_two, "batch", axis=1, tiled=True),
        lax.all_gather(low_three, "batch", axis=1, tiled=True),
        lax.all_gather(low_four, "batch", axis=1, tiled=True),
    )
    spatial_one, temporal_one, spatial_two, temporal_two = (
        lax.all_gather(columns[0], "tm", axis=0, tiled=True),
        lax.all_gather(columns[1], "tm", axis=0, tiled=True),
        lax.all_gather(columns[2], "tm", axis=0, tiled=True),
        lax.all_gather(columns[3], "tm", axis=0, tiled=True),
    )
    clips = x_small.shape[0]
    split_point = x_small.shape[2]
    large_cells = x_large.shape[2]
    batch_index = lax.axis_index("batch")
    slots = jnp.arange(clips, dtype=jnp.int32)
    live_small = (slots < clip_counts[0, batch_index]).astype(jnp.float32)
    live_large = (slots < clip_counts[1, batch_index]).astype(jnp.float32)
    active_flags = jnp.concatenate(
        [
            jnp.broadcast_to(live_small[:, None, None, None], (clips, 1, split_point, 1)),
            jnp.broadcast_to(live_large[:, None, None, None], (clips, 1, large_cells, 1)),
        ],
        axis=2,
    )
    frames_total = x_small.shape[1] * lax.axis_size("tm")
    grand_totals = jnp.stack(
        [
            jnp.sum(clip_counts[0]).astype(jnp.float32) * frames_total * split_point,
            jnp.sum(clip_counts[1]).astype(jnp.float32) * frames_total * large_cells,
        ]
    )
    bounds = (0, MID, MID + D, 2 * MID + D, 2 * MID + 2 * D)
    gain_vectors = [norm_params[0, bounds[index] : bounds[index + 1]] for index in range(4)]
    bias_vectors = [norm_params[1, bounds[index] : bounds[index + 1]] for index in range(4)]
    first_convolved, taps_one_small, taps_one_large = spatial_forward(x_small, x_large, spatial_one)
    hidden_one, normed_one, scale_one = norm_forward_pass(
        first_convolved, active_flags, split_point, grand_totals, gain_vectors[0], bias_vectors[0]
    )
    act_one = jax.nn.silu(hidden_one).astype(jnp.bfloat16)
    second_convolved, rows_two = temporal_forward(act_one, temporal_one)
    hidden_two, normed_two, scale_two = norm_forward_pass(
        second_convolved, active_flags, split_point, grand_totals, gain_vectors[1], bias_vectors[1]
    )
    act_two = jax.nn.silu(hidden_two).astype(jnp.bfloat16)
    third_convolved, taps_three_small, taps_three_large = spatial_forward(
        act_two[:, :, :split_point], act_two[:, :, split_point:], spatial_two
    )
    hidden_three, normed_three, scale_three = norm_forward_pass(
        third_convolved, active_flags, split_point, grand_totals, gain_vectors[2], bias_vectors[2]
    )
    act_three = jax.nn.silu(hidden_three).astype(jnp.bfloat16)
    fourth_convolved, rows_four = temporal_forward(act_three, temporal_two)
    hidden_four, fourth_normalized, fourth_scale = norm_forward_pass(
        fourth_convolved, active_flags, split_point, grand_totals, gain_vectors[3], bias_vectors[3]
    )
    residual_in = jnp.concatenate([x_small, x_large], axis=2).astype(jnp.float32)
    output_preactivation = hidden_four + residual_in
    block_output = active_flags * jax.nn.silu(output_preactivation)
    upstream_gradient = (
        jnp.concatenate([small_output_gradient, large_output_gradient], axis=2).astype(jnp.float32)
        * active_flags
    )
    passed_gradient = upstream_gradient * silu_slope(output_preactivation)
    squared_values = []
    grad_conv_four, gain_four, bias_four = norm_reverse_pass(
        passed_gradient,
        fourth_normalized,
        fourth_scale,
        gain_vectors[3],
        active_flags,
        split_point,
        grand_totals,
    )
    grad_conv_four = grad_conv_four.astype(jnp.bfloat16)
    rows_grad_four = grad_conv_four.reshape(-1, grad_conv_four.shape[-1])
    grad_second_temporal = reduce_weight(
        [(rows_four, rows_grad_four)], rows_four.shape[1], rows_grad_four.shape[1]
    )
    squared_values.append(own_square(grad_second_temporal))
    grad_act_three = temporal_backward(grad_conv_four, temporal_two)
    grad_conv_three, gain_three, bias_three = norm_reverse_pass(
        grad_act_three * silu_slope(hidden_three),
        normed_three,
        scale_three,
        gain_vectors[2],
        active_flags,
        split_point,
        grand_totals,
    )
    grad_conv_three = grad_conv_three.astype(jnp.bfloat16)
    rows_three_small = grad_conv_three[:, :, :split_point].reshape(-1, grad_conv_three.shape[-1])
    rows_three_large = grad_conv_three[:, :, split_point:].reshape(-1, grad_conv_three.shape[-1])
    grad_second_spatial = reduce_weight(
        [(taps_three_small, rows_three_small), (taps_three_large, rows_three_large)],
        taps_three_small.shape[1],
        rows_three_small.shape[1],
    )
    squared_values.append(own_square(grad_second_spatial))
    channels_mid = act_two.shape[-1]
    grad_act_two = jnp.concatenate(
        [
            spatial_backward(
                rows_three_small,
                spatial_two,
                (clips, act_two.shape[1], split_point, channels_mid),
                HS,
            ),
            spatial_backward(
                rows_three_large,
                spatial_two,
                (clips, act_two.shape[1], large_cells, channels_mid),
                HL,
            ),
        ],
        axis=2,
    )
    grad_conv_two, gain_two, bias_two = norm_reverse_pass(
        grad_act_two * silu_slope(hidden_two),
        normed_two,
        scale_two,
        gain_vectors[1],
        active_flags,
        split_point,
        grand_totals,
    )
    grad_conv_two = grad_conv_two.astype(jnp.bfloat16)
    rows_grad_two = grad_conv_two.reshape(-1, grad_conv_two.shape[-1])
    grad_first_temporal = reduce_weight(
        [(rows_two, rows_grad_two)], rows_two.shape[1], rows_grad_two.shape[1]
    )
    squared_values.append(own_square(grad_first_temporal))
    grad_act_one = temporal_backward(grad_conv_two, temporal_one)
    grad_conv_one, gain_one, bias_one = norm_reverse_pass(
        grad_act_one * silu_slope(hidden_one),
        normed_one,
        scale_one,
        gain_vectors[0],
        active_flags,
        split_point,
        grand_totals,
    )
    grad_conv_one = grad_conv_one.astype(jnp.bfloat16)
    rows_one_small = grad_conv_one[:, :, :split_point].reshape(-1, grad_conv_one.shape[-1])
    rows_one_large = grad_conv_one[:, :, split_point:].reshape(-1, grad_conv_one.shape[-1])
    grad_first_spatial = reduce_weight(
        [(taps_one_small, rows_one_small), (taps_one_large, rows_one_large)],
        taps_one_small.shape[1],
        rows_one_small.shape[1],
    )
    squared_values.append(own_square(grad_first_spatial))
    input_small = passed_gradient[:, :, :split_point] + spatial_backward(
        rows_one_small, spatial_one, x_small.shape, HS
    )
    input_large = passed_gradient[:, :, split_point:] + spatial_backward(
        rows_one_large, spatial_one, x_large.shape, HL
    )
    grad_params = jnp.stack(
        [
            jnp.concatenate([gain_one, gain_two, gain_three, gain_four]),
            jnp.concatenate([bias_one, bias_two, bias_three, bias_four]),
        ]
    )
    summed = lax.psum(
        (squared_values[0], squared_values[1], squared_values[2], squared_values[3]),
        ("batch", "tm"),
    )
    weight_square = summed[0] + summed[1] + summed[2] + summed[3]
    grad_norm = jnp.sqrt(weight_square + jnp.sum(grad_params * grad_params))
    factor = THRESHOLD / jnp.maximum(grad_norm, THRESHOLD)
    one = adamw(
        first_spatial,
        grad_first_spatial,
        first_spatial_momentum,
        first_spatial_variance,
        factor,
        WEIGHT_RATE,
        WEIGHT_DECAY,
    )
    two = adamw(
        first_temporal,
        grad_first_temporal,
        first_temporal_momentum,
        first_temporal_variance,
        factor,
        WEIGHT_RATE,
        WEIGHT_DECAY,
    )
    three = adamw(
        second_spatial,
        grad_second_spatial,
        second_spatial_momentum,
        second_spatial_variance,
        factor,
        WEIGHT_RATE,
        WEIGHT_DECAY,
    )
    four = adamw(
        second_temporal,
        grad_second_temporal,
        second_temporal_momentum,
        second_temporal_variance,
        factor,
        WEIGHT_RATE,
        WEIGHT_DECAY,
    )
    norms = adamw(norm_params, grad_params, norm_momentum, norm_variance, factor, NORM_RATE, 0.0)
    return (
        block_output[:, :, :split_point],
        block_output[:, :, split_point:],
        input_small,
        input_large,
        grad_norm,
        one[0],
        one[1],
        one[2],
        two[0],
        two[1],
        two[2],
        three[0],
        three[1],
        three[2],
        four[0],
        four[1],
        four[2],
        norms[0],
        norms[1],
        norms[2],
    )


BF = jnp.bfloat16
F32 = jnp.float32
MESH_ID = pl.DeviceIdType.MESH
NT_DIMS = (((1,), (1,)), ((), ()))
NN_DIMS = (((1,), (0,)), ((), ()))
scope = lambda name: contextlib.nullcontext()
UP, DOWN, ACROSS, ALONG, TWIN = range(5)


class Place:
    def __init__(self, batches, slots):
        self.batches, self.slots = batches, slots
        self.z = lax.axis_index("batch")
        self.t = lax.axis_index("tm")
        self.core = lax.rem(self.t, 2)
        self.slab = self.t // 2
        self.slabs = slots // 2
        side = lax.rem(self.slab, 2)
        deep = self.slab // 2
        self.side_slab = deep * 2 + (1 - side)
        self.deep_slab = (1 - deep) * 2 + side
        self.far_slab = (1 - deep) * 2 + (1 - side)
        self.rel = (self.slab, self.side_slab, self.deep_slab, self.far_slab)
        self.twin = self.t + 1 - 2 * self.core

    def device(self, way):
        if way == UP:
            return (self.z + 1, self.t)
        if way == DOWN:
            return (self.z - 1, self.t)
        if way == ACROSS:
            return (self.z, self.side_slab * 2 + self.core)
        if way == ALONG:
            return (self.z, self.deep_slab * 2 + self.core)
        return (self.z, self.twin)

    def greet(self):
        barrier = pltpu.get_barrier_semaphore()
        for step in range(1, self.slots):
            pl.semaphore_signal(
                barrier, inc=1, device_id=(self.z, lax.rem(self.t + step, self.slots)),
                device_id_type=MESH_ID,
            )
        for step in range(1, self.batches):
            pl.semaphore_signal(
                barrier, inc=1, device_id=(lax.rem(self.z + step, self.batches), self.t),
                device_id_type=MESH_ID,
            )
        pl.semaphore_wait(barrier, self.slots + self.batches - 2)


def send(src, dst, send_sem, recv_sem, device):
    return pltpu.make_async_remote_copy(
        src_ref=src, dst_ref=dst, send_sem=send_sem, recv_sem=recv_sem,
        device_id=device, device_id_type=MESH_ID,
    )


class Totals:
    def __init__(self, place, rows, planes, lines, sems):
        self.p, self.rows, self.planes, self.lines = place, rows, planes, lines
        self.plane_send, self.plane_recv, self.line_send, self.line_recv = sems

    def plane_copy(self, n, step, width):
        p = self.p
        to = lax.rem(p.t + step, p.slots)
        ref = self.planes.at[n, p.t, :, pl.ds(0, width)]
        return send(ref, ref, self.plane_send.at[n, step], self.plane_recv.at[n, p.t], (p.z, to))

    def line_copy(self, n, step, width):
        p = self.p
        to = lax.rem(p.z + step, p.batches)
        ref = self.lines.at[n, p.z, :, pl.ds(0, width)]
        return send(ref, ref, self.line_send.at[n, step], self.line_recv.at[n, p.z], (to, p.t))

    def run(self, n, value, first=None, second=None):
        p = self.p
        width = value.shape[1]
        plane, line = self.planes.at[n], self.lines.at[n]
        plane[p.t, :, :width] = value
        for step in range(1, p.slots):
            self.plane_copy(n, step, width).start()
        if first is not None:
            first()
        for step in range(1, p.slots):
            origin = lax.rem(p.t + p.slots - step, p.slots)
            ref = plane.at[origin, :, pl.ds(0, width)]
            send(ref, ref, self.plane_send.at[n, step], self.plane_recv.at[n, origin],
                 (p.z, p.twin)).wait_recv()
        total = plane[0, :, :width]
        for slot in range(1, p.slots):
            total = total + plane[slot, :, :width]
        line[p.z, :, :width] = total
        for step in range(1, p.batches):
            self.line_copy(n, step, width).start()
        if second is not None:
            second()
        for step in range(1, p.batches):
            origin = lax.rem(p.z + p.batches - step, p.batches)
            ref = line.at[origin, :, pl.ds(0, width)]
            send(ref, ref, self.line_send.at[n, step], self.line_recv.at[n, origin],
                 (p.z, p.twin)).wait_recv()
        total = line[0, :, :width]
        for slot in range(1, p.batches):
            total = total + line[slot, :, :width]
        for step in range(1, p.slots):
            self.plane_copy(n, step, width).wait_send()
        for step in range(1, p.batches):
            self.line_copy(n, step, width).wait_send()
        return total


class Gather:
    def __init__(self, place, index, own, whole, block, sems):
        self.p, self.n, self.own, self.whole, self.block = place, index, own, whole, block
        self.send_sem, self.recv_sem, self.twin_sem = sems

    def copy(self, way, rel, batch, src=None):
        p = self.p
        core = p.core
        dst = self.whole.at[self.block(p.rel[rel], core, batch)]
        there = {ACROSS: {0: 1, 2: 3}, ALONG: {0: 2, 1: 3}}.get(way, {}).get(rel, rel)
        sem = self.twin_sem if way == TWIN else self.recv_sem
        return send(
            dst if src is None else src, dst, self.send_sem.at[self.n, way, rel, batch],
            sem.at[self.n, there, batch], p.device(way),
        )

    def wait(self, rel, batch, twin=False):
        p = self.p
        core = 1 - p.core if twin else p.core
        ref = self.whole.at[self.block(p.rel[rel], core, batch)]
        sem = self.twin_sem if twin else self.recv_sem
        send(ref, ref, self.send_sem.at[self.n, TWIN, rel, batch], sem.at[self.n, rel, batch],
             p.device(TWIN)).wait_recv()

    def at(self, k, fn):
        p = self.p
        if k == 0:
            fn(p.z)
            return
        pl.when(p.z - k >= 0)(lambda: fn(p.z - k))
        pl.when(p.z + k < p.batches)(lambda: fn(p.z + k))

    def start_line(self):
        p = self.p
        pl.when(p.z < p.batches - 1)(lambda: self.copy(UP, 0, p.z, self.own).start())
        pl.when(p.z > 0)(lambda: self.copy(DOWN, 0, p.z, self.own).start())
        self.copy(TWIN, 0, p.z, self.own).start()

    def start_plane(self):
        for way in (ACROSS, ALONG):
            self.copy(way, 0, self.p.z, self.own).start()

    def hop(self, k):
        p = self.p

        def below(b):
            self.wait(0, b)
            pl.when(p.z < p.batches - 1)(lambda: self.copy(UP, 0, b).start())
            self.copy(TWIN, 0, b).start()

        def above(b):
            self.wait(0, b)
            pl.when(p.z > 0)(lambda: self.copy(DOWN, 0, b).start())
            self.copy(TWIN, 0, b).start()

        pl.when(p.z - k >= 0)(lambda: below(p.z - k))
        pl.when(p.z + k < p.batches)(lambda: above(p.z + k))

    def spread(self, k, ways=(ACROSS, ALONG)):
        def one(b):
            for way in ways:
                self.copy(way, 0, b).start()

        self.at(k, one)

    def across(self, k):
        self.spread(k, (ACROSS,))

    def along(self, k):
        self.spread(k, (ALONG,))

    def from_side(self, k):
        half = self.p.batches // 2

        def one(b):
            self.wait(1, b)
            pl.when(b < half)(lambda: self.copy(ALONG, 1, b).start())
            self.copy(TWIN, 1, b).start()

        self.at(k, one)

    def from_deep(self, k):
        half = self.p.batches // 2

        def one(b):
            self.wait(2, b)
            pl.when(b >= half)(lambda: self.copy(ACROSS, 2, b).start())
            self.copy(TWIN, 2, b).start()

        self.at(k, one)

    def plane(self, k):
        self.from_side(k)
        self.from_deep(k)

    def far(self, k):
        def one(b):
            self.wait(3, b)
            self.copy(TWIN, 3, b).start()

        self.at(k, one)

    def twins(self, rel):
        def body(b, _):
            self.wait(rel, b, twin=True)
            return 0

        lax.fori_loop(0, self.p.batches, body, 0)

    def act(self, word):
        kind = word[0]
        if kind == "z":
            self.start_line()
        elif kind == "x":
            self.start_plane()
        else:
            {"h": self.hop, "s": self.spread, "a": self.across, "l": self.along, "p": self.plane, "f": self.far,
             "u": self.from_side, "v": self.from_deep}[kind](int(word[1]))

    def finish(self):
        p = self.p
        half = p.batches // 2

        def body(b, _):
            pl.when((b <= p.z) & (p.z < p.batches - 1))(lambda: self.copy(UP, 0, b, self.own).wait_send())
            pl.when((b >= p.z) & (p.z > 0))(lambda: self.copy(DOWN, 0, b, self.own).wait_send())
            for way in (ACROSS, ALONG):
                self.copy(way, 0, b, self.own).wait_send()
            for rel in range(4):
                self.copy(TWIN, rel, b, self.own).wait_send()
            pl.when(b < half)(lambda: self.copy(ALONG, 1, b, self.own).wait_send())
            pl.when(b >= half)(lambda: self.copy(ACROSS, 2, b, self.own).wait_send())
            return 0

        lax.fori_loop(0, p.batches, body, 0)


class FarLineGather(Gather):
    def line(self, rel, b, up=True, down=True):
        p = self.p
        if up:
            pl.when(p.z < p.batches - 1)(lambda: self.copy(UP, rel, b).start())
        if down:
            pl.when(p.z > 0)(lambda: self.copy(DOWN, rel, b).start())

    def side_own(self):
        z = self.p.z
        self.wait(1, z)
        self.copy(ALONG, 1, z).start()
        self.copy(TWIN, 1, z).start()

    def far_own(self):
        z = self.p.z
        self.wait(3, z)
        self.copy(TWIN, 3, z).start()
        self.line(3, z)

    def far_hop(self, k):
        p = self.p

        def below(b):
            self.wait(3, b)
            self.line(3, b, down=False)
            self.copy(TWIN, 3, b).start()

        def above(b):
            self.wait(3, b)
            self.line(3, b, up=False)
            self.copy(TWIN, 3, b).start()

        pl.when(p.z - k >= 0)(lambda: below(p.z - k))
        pl.when(p.z + k < p.batches)(lambda: above(p.z + k))

    def from_side(self, k):
        def one(b):
            self.wait(1, b)
            self.copy(TWIN, 1, b).start()

        self.at(k, one)

    def from_deep(self, k):
        def one(b):
            self.wait(2, b)
            self.copy(TWIN, 2, b).start()

        self.at(k, one)

    def act(self, word):
        if word == "c":
            self.side_own()
        elif word == "d":
            self.far_own()
        elif word[0] == "g":
            self.far_hop(int(word[1]))
        else:
            super().act(word)

    def finish(self):
        p = self.p
        self.copy(ALONG, 1, p.z, self.own).wait_send()

        def body(b, _):
            for rel in (0, 3):
                pl.when((b <= p.z) & (p.z < p.batches - 1))(
                    lambda: self.copy(UP, rel, b, self.own).wait_send())
                pl.when((b >= p.z) & (p.z > 0))(lambda: self.copy(DOWN, rel, b, self.own).wait_send())
            for way in (ACROSS, ALONG):
                self.copy(way, 0, b, self.own).wait_send()
            for rel in range(4):
                self.copy(TWIN, rel, b, self.own).wait_send()
            return 0

        lax.fori_loop(0, p.batches, body, 0)


class Halo:
    def __init__(self, place, stage, src, dst, relay, sems, cut):
        self.p, self.n, self.src, self.dst, self.buf, self.cut = place, stage, src, dst, relay, cut
        self.send_sem, self.recv_sem, self.pass_send, self.pass_recv = sems
        self.mid = place.slots // 2

    def part(self, ref, piece):
        rows = ref.shape[0]
        return ref.at[pl.ds(0, self.cut)] if piece == 0 else ref.at[pl.ds(self.cut, rows - self.cut)]

    def piece(self, side, piece, to):
        return send(self.part(self.src(side), piece), self.part(self.dst(side), piece),
                    self.send_sem.at[self.n, side, piece], self.recv_sem.at[self.n, side, piece],
                    (self.p.z, to))

    def detour(self, side):
        to = self.p.slots - 1 if side == 0 else 0
        return send(self.part(self.src(side), 1), self.buf, self.send_sem.at[self.n, side, 1],
                    self.pass_recv.at[self.n], (self.p.z, to))

    def passing(self, side):
        to = self.mid if side == 0 else self.mid - 1
        return send(self.buf, self.part(self.dst(side), 1), self.pass_send.at[self.n],
                    self.recv_sem.at[self.n, side, 1], (self.p.z, to))

    def sends(self, side):
        return self.p.t < self.p.slots - 1 if side == 0 else self.p.t > 0

    def receives(self, side):
        return self.p.t > 0 if side == 0 else self.p.t < self.p.slots - 1

    def start(self, side):
        p = self.p
        to = p.t + 1 if side == 0 else p.t - 1
        crossing = p.t == (self.mid - 1 if side == 0 else self.mid)

        @pl.when(self.sends(side))
        def _():
            pl.when(crossing)(lambda: self.detour(side).start())
            self.piece(side, 0, to).start()
            pl.when(jnp.logical_not(crossing))(lambda: self.piece(side, 1, to).start())

    def relay(self):
        p = self.p
        for side, t in ((0, p.slots - 1), (1, 0)):
            @pl.when(p.t == t)
            def _(side=side):
                send(self.buf, self.buf, self.pass_send.at[self.n], self.pass_recv.at[self.n],
                     p.device(TWIN)).wait_recv()
                self.passing(side).start()

    def wait(self, side):
        @pl.when(self.receives(side))
        def _():
            for piece in range(2):
                self.piece(side, piece, self.p.twin).wait_recv()

    def done(self):
        p = self.p
        for side in range(2):
            @pl.when(self.sends(side))
            def _(side=side):
                for piece in range(2):
                    self.piece(side, piece, p.twin).wait_send()
        for side, t in ((0, p.slots - 1), (1, 0)):
            pl.when(p.t == t)(lambda side=side: self.passing(side).wait_send())


def sigmoid(v):
    return 0.5 * jnp.tanh(0.5 * v) + 0.5


class Shape:
    def __init__(self, x_small, x_large, batches, slots):
        self.clips = x_small[0]
        self.cells = (x_small[2], x_large[2])
        self.sides = (math.isqrt(x_small[2]), math.isqrt(x_large[2]))
        self.d = x_small[3]
        self.padded = tuple(n + n % 2 for n in self.cells)
        self.rows = tuple(n * self.clips for n in self.padded)
        self.m = sum(self.rows)
        self.mid = MID
        self.k = 9 * self.d
        self.batches, self.slots = batches, slots
        self.slabs = slots // 2
        self.kw = self.k // self.slabs
        self.nb = self.mid // (2 * batches)
        self.ur = 3 * self.mid // slots
        self.uc = self.d // batches
        self.cut = -(-self.m // 32) * 16


def fits(x_small, x_large, batches, slots):
    s = Shape(x_small, x_large, batches, slots)
    return (
        s.clips == 8 and x_small[1] == 1 and slots == 8 and batches == 4
        and all(side * side == cells for side, cells in zip(s.sides, s.cells))
        and all(r % 80 == 0 for r in s.rows)
        and s.kw % 128 == 0 and s.mid % (32 * batches) == 0 and s.ur % 16 == 0 and s.uc % 128 == 0
    )


def chunks(s, size, fn, carry=None, unroll=1):
    out = []
    base = 0
    for group, rows in enumerate(s.rows):
        def body(i, c, group=group, base=base):
            return fn(group, pl.multiple_of(base + i * size, size if base % size == 0 else 16), c)

        out.append(lax.fori_loop(0, rows // size, body, carry if carry is not None else 0, unroll=unroll))
        base += rows
    return out


def sums_of(s, load, live, width):
    def body(group, r0, c):
        values = load(group, r0, 80)
        return tuple(t + jnp.sum(v.reshape(10, 8, width), axis=0) for t, v in zip(c, values))

    zero = jnp.zeros((8, width), F32)
    small, large = chunks(s, 80, body, (zero, zero))
    rows = [jnp.sum(v * live[g], axis=0, keepdims=True) for v, g in
            ((small[0], 0), (large[0], 1), (small[1], 0), (large[1], 1))]
    return jnp.concatenate(rows, axis=0)


def build_taps(s, grids, taps):
    pieces = []
    for tap in range(9):
        lo = tap * s.d
        end = lo + s.d
        while lo < end:
            hi = min(end, (lo // s.kw + 1) * s.kw)
            pieces.append((tap, lo - tap * s.d, lo // s.kw, lo % s.kw, hi - lo))
            lo = hi
    base = 0
    for group in range(2):
        side, cells = s.sides[group], s.cells[group]
        grid = grids[group]
        for tap, channel, slab, lane, width in pieces:
            i, j = tap // 3, tap % 3
            if side % 2 == 0:
                n = 2 * side * 8

                def body(r, _):
                    window = grid[pl.ds(i + 2 * r, 2), j : j + side, :, channel : channel + width]
                    taps[slab, pl.ds(pl.multiple_of(base + r * n, 16), n), lane : lane + width] = (
                        window.reshape(n, width).astype(BF)
                    )
                    return 0

                lax.fori_loop(0, side // 2, body, 0)
            else:
                window = grid[i : i + side, j : j + side, :, channel : channel + width]
                window = window.reshape(cells * 8, width)
                window = jnp.concatenate(
                    [window, jnp.zeros((s.rows[group] - cells * 8, width), F32)], axis=0
                ) if s.rows[group] > cells * 8 else window
                taps[slab, base : base + s.rows[group], lane : lane + width] = window.astype(BF)
        base += s.rows[group]


def fill_grid(s, grids, group, cell, value):
    side = s.sides[group]
    grids[group][1 + cell // side, 1 + lax.rem(cell, side)] = value


def zero_padding(s, ref, width):
    base = 0
    for group in range(2):
        base += s.rows[group]
        spare = (s.padded[group] - s.cells[group]) * s.clips
        if spare:
            size = -(-spare // 16) * 16
            keep = lax.broadcasted_iota(jnp.int32, (size, width), 0) < size - spare
            value = ref[base - size : base, :].astype(F32)
            ref[base - size : base, :] = jnp.where(keep, value, 0.0).astype(ref.dtype)


def grid_of_rows(s, grids, group, r0, value):
    side = s.sides[group]
    base = 0 if group == 0 else s.rows[0]
    first = (r0 - base) // 8
    split = value.reshape(10, 8, s.d)
    for n in range(10):
        cell = first + n
        grids[group][1 + cell // side, 1 + lax.rem(cell, side)] = split[n]


def clear_pad_cells(s, grids):
    for group in range(2):
        side = s.sides[group]
        for cell in range(s.cells[group], s.padded[group]):
            grids[group][1 + cell // side, 1 + cell % side] = jnp.zeros((8, s.d), F32)


def moments(total, inverse, width):
    mean = [total[g : g + 1, :] * inverse[g] for g in range(2)]
    scale = [
        lax.rsqrt(total[2 + g : 3 + g, :] * inverse[g] - mean[g] * mean[g] + NORM_EPS) for g in range(2)
    ]
    return mean, scale


def wide_cuts(width):
    half = -(-width // 256) * 128
    return ((0, half), (half, width - half))


def forward_kernel(s, *refs):
    (x, grad, sw1, uw1, sw2, uw2, norm, live_ref, inverse,
     gs1, gu1, gs2, gu2, taps1_o, taps2_o, xh1_o, xh2_o, xh3_o, xh4_o, z1_o, z3_o, out_o, dpre_o,
     r1_o, r2_o, r3_o, r4_o, last_o,
     tb1, tb2, own1, own2, wb, wub, taps, a, z, grid_s, grid_l, b, hs, hr, planes, lines,
     ag_send, ag_recv, ag_twin, tb_send, tb_recv, local, load, hs_send, hs_recv, pass_send, pass_recv, relay, out, dpre,
     pl_send, pl_recv, ln_send, ln_recv) = refs
    p = Place(s.batches, s.slots)
    live = [live_ref[g] for g in range(2)]
    inv = [inverse[g] for g in range(2)]
    totals = Totals(p, 4, planes, lines, (pl_send, pl_recv, ln_send, ln_recv))
    d, mid = s.d, s.mid
    bounds = (0, mid, mid + d, 2 * mid + d, 2 * mid + 2 * d)

    def gain_bias(n):
        return norm[0:1, bounds[n] : bounds[n + 1]], norm[1:2, bounds[n] : bounds[n + 1]]

    with scope("greet"):
        p.greet()

    def twin_copy(n, src, dst):
        return send(
            src.at[1 - p.core], dst.at[pl.ds(pl.multiple_of(p.core * (s.kw // 2), 16), s.kw // 2)],
            tb_send.at[n], tb_recv.at[n], p.device(TWIN),
        )

    def twin_wait(n, src, dst):
        send(
            src.at[1 - p.core], dst.at[pl.ds(pl.multiple_of((1 - p.core) * (s.kw // 2), 16), s.kw // 2)],
            tb_send.at[n], tb_recv.at[n], p.device(TWIN),
        ).wait_recv()

    for n, src, dst in ((0, sw1, tb1), (1, sw2, tb2)):
        twin_copy(n, src, dst).start()
        dst[pl.ds(pl.multiple_of(p.core * (s.kw // 2), 16), s.kw // 2)] = src[p.core]

    def s_block(slab, core, batch):
        return (slab, pl.ds(pl.multiple_of((batch * 2 + core) * s.nb, 16), s.nb))

    def u_block(slab, core, batch):
        return (pl.ds(pl.multiple_of((slab * 2 + core) * s.ur, 16), s.ur),
                pl.ds(pl.multiple_of(batch * s.uc, 128), s.uc))

    sems = (ag_send, ag_recv, ag_twin)
    gather = [
        Gather(p, 0, own1, gs1, s_block, sems),
        Gather(p, 1, uw1, gu1, u_block, sems),
        FarLineGather(p, 2, own2, gs2, s_block, sems),
        Gather(p, 3, uw2, gu2, u_block, sems),
    ]

    def keep_own(n):
        g = gather[n]
        return pltpu.make_async_copy(g.own, g.whole.at[g.block(p.slab, p.core, p.z)], local.at[n])

    def go(words):
        with scope("gather " + words):
            for word in words.split():
                gather[int(word[0])].act(word[1:])

    with scope("own"):
        twin_wait(0, sw1, tb1)
        own1[...] = tb1[...].T
        go("0z 0x")
        keep_own(0).start()
        twin_wait(1, sw2, tb2)
        own2[...] = tb2[...].T
    keep_own(1).start()
    keep_own(2).start()
    keep_own(3).start()
    for side, edge in ((0, 0), (1, p.slots - 1)):
        @pl.when(p.t == edge)
        def _(side=side):
            hr[side] = jnp.zeros(hr.shape[1:], BF)

    grids = (grid_s, grid_l)
    for grid in grids:
        def clear(i, _, grid=grid):
            grid[i] = jnp.zeros(grid.shape[1:], F32)
            return 0

        lax.fori_loop(0, grid.shape[0], clear, 0)

    def x_rows(group, r0, c):
        grid_of_rows(s, grids, group, r0, x[pl.ds(r0, 80), :].astype(F32))
        return c

    with scope("taps x"):
        chunks(s, 80, x_rows)
        clear_pad_cells(s, grids)
        build_taps(s, grids, taps)
    taps_copy = pltpu.make_async_copy(taps, taps1_o, local.at[4])
    taps_copy.start()

    def slab_load(whole, rel, half):
        lo, width = wide_cuts(mid)[half]
        rows = pl.ds(lo, width)
        return pltpu.make_async_copy(whole.at[p.rel[rel], rows], wb.at[rel, rows], load.at[rel, half])

    def conv_slab(whole, rel, first):
        for half, (lo, width) in enumerate(wide_cuts(mid)):
            slab_load(whole, rel, half).wait()
            y = lax.dot_general(taps[p.rel[rel]], wb[rel, lo : lo + width, :], NT_DIMS, preferred_element_type=F32)
            if first:
                a[:, lo : lo + width] = y
            else:
                a[:, lo : lo + width] += y

    def spatial(n, whole, order, words):
        g = gather[n]
        keep_own(n).wait()
        for i, rel in enumerate(order):
            go(words[2 * i])
            with scope("twins"):
                g.twins(rel)
            for half in range(2):
                slab_load(whole, rel, half).start()
            go(words[2 * i + 1])
            with scope("slab"):
                conv_slab(whole, rel, i == 0)

    def stats(load_rows, width):
        return sums_of(s, load_rows, live, width)

    def wide_norm(index, n, zo, xo, ro, sem, words, weight):
        def load_rows(group, r0, size):
            v = a[pl.ds(r0, size), :]
            return v, v * v

        with scope("wide stats"):
            local_sums = stats(load_rows, mid)
        go(words[0])
        with scope("total"):
            total = totals.run(index, local_sums)
        weight_load(*weight)
        go(words[1])
        mean, scale = moments(total, inv, mid)
        ro[...] = jnp.concatenate(scale, axis=0)
        gain, bias = gain_bias(n)

        def rows(group, r0, c):
            xhat = (a[pl.ds(r0, 16), :] - mean[group]) * scale[group]
            a[pl.ds(r0, 16), :] = xhat
            h = xhat * gain + bias
            z[pl.ds(r0, 16), :] = (h * sigmoid(h)).astype(BF)
            return c

        with scope("wide norm"):
            chunks(s, 16, rows)
        zero_padding(s, z, mid)
        xc = pltpu.make_async_copy(a, xo, local.at[sem])
        zc = pltpu.make_async_copy(z, zo, local.at[sem + 1])
        xc.start()
        zc.start()
        return xc, zc

    def u_load(n, whole):
        return pltpu.make_async_copy(whole, wub, load.at[4, n])

    halos = [
        Halo(p, n, lambda side: hs.at[side], lambda side: hr.at[side], relay,
             (hs_send, hs_recv, pass_send, pass_recv), s.cut)
        for n in range(2)
    ]

    def weight_load(n, index):
        with scope("u weight"):
            for rel in range(4):
                gather[index].twins(rel)
            keep_own(index).wait()
            u_load(n, gather[index].whole).start()

    def temporal(n, words):
        with scope("u conv"):
            u_load(n, gather[1].whole).wait()
            hs[0] = jnp.dot(z[...], wub[:mid, :], preferred_element_type=F32).astype(BF)
            halos[n].start(0)
            hs[1] = jnp.dot(z[...], wub[2 * mid :, :], preferred_element_type=F32).astype(BF)
            halos[n].start(1)
            b[...] = jnp.dot(z[...], wub[mid : 2 * mid, :], preferred_element_type=F32)
        go(words[0])
        with scope("relay"):
            halos[n].relay()
        go(words[1])
        with scope("halo wait"):
            halos[n].wait(0)
            halos[n].wait(1)

    def narrow_total(index):
        def load_rows(group, r0, size):
            v = b[pl.ds(r0, size), :] + hr[0, pl.ds(r0, size), :].astype(F32) + hr[1, pl.ds(r0, size), :].astype(F32)
            b[pl.ds(r0, size), :] = v
            return v, v * v

        with scope("narrow stats"):
            local_sums = stats(load_rows, d)
        with scope("total"):
            return totals.run(index, local_sums)

    go("0h1 0s1 0p0 0h2 0s2 0p1 0f0 0h3 0s3 1z")
    spatial(0, gs1, (0, 1, 2, 3), ("", "", "0p2 0f1 1h1 0p3 1h2", "1x 1s1 1h3 1s2 1s3", "0f2", "1p0", "0f3 1p1 1f0", "2z"))
    xc1, zc1 = wide_norm(0, 0, z1_o, xh1_o, r1_o, 5, ("1p2 1f1 1p3 1f2 1f3", "2x 2h1 3z"), (0, 1))
    temporal(0, ("", "2c 2l1 2h2 2l2 2d 3h1 2h3 2l3 2g1 3h2"))
    total = narrow_total(1)
    go("2a1 3h3 3x 3s1 3s2 3s3 2a2 2a3 2g2")
    mean2, scale2 = moments(total, inv, d)
    r2_o[...] = jnp.concatenate(scale2, axis=0)
    gain2, bias2 = gain_bias(1)

    def second(group, r0, c):
        xhat = (b[pl.ds(r0, 80), :] - mean2[group]) * scale2[group]
        b[pl.ds(r0, 80), :] = xhat
        h = xhat * gain2 + bias2
        grid_of_rows(s, grids, group, r0, (h * sigmoid(h)).astype(BF).astype(F32))
        return c

    with scope("norm2"):
        chunks(s, 80, second)
        clear_pad_cells(s, grids)
    xc2 = pltpu.make_async_copy(b, xh2_o, local.at[7])
    xc2.start()
    halos[0].done()
    taps_copy.wait()
    with scope("taps z2"):
        build_taps(s, grids, taps)
    taps_copy2 = pltpu.make_async_copy(taps, taps2_o, local.at[8])
    taps_copy2.start()
    xc1.wait()
    spatial(2, gs2, (0, 2, 3, 1), ("", "2v0 2v1 2v2 2v3", "", "2g3", "", "3p0 3p1 3f0", "2u1 2u2 2u3", "3p2 3f1"))
    zc1.wait()
    xc3, zc3 = wide_norm(2, 2, z3_o, xh3_o, r3_o, 9, ("3p3 3f2 3f3", ""), (1, 3))
    xc2.wait()
    temporal(1, ("", ""))
    total = narrow_total(3)
    mean4, scale4 = moments(total, inv, d)
    r4_o[...] = jnp.concatenate(scale4, axis=0)
    gain4, bias4 = gain_bias(3)

    def last(group, r0, c):
        xhat = (b[pl.ds(r0, 80), :] - mean4[group]) * scale4[group]
        b[pl.ds(r0, 80), :] = xhat
        pre = xhat * gain4 + bias4 + x[pl.ds(r0, 80), :].astype(F32)
        gate = sigmoid(pre)
        alive = jnp.broadcast_to(live[group][None], (10, 8, d)).reshape(80, d)
        out[pl.ds(r0, 80), :] = alive * (pre * gate)
        up = alive * grad[pl.ds(r0, 80), :].astype(F32) * (gate * (1.0 + pre * (1.0 - gate)))
        dpre[pl.ds(r0, 80), :] = up
        return c

    with scope("norm4"):
        chunks(s, 80, last)
        zero_padding(s, dpre, d)
    xc4 = pltpu.make_async_copy(b, xh4_o, local.at[11])
    xc4.start()
    outs = [pltpu.make_async_copy(out, out_o, local.at[12]), pltpu.make_async_copy(dpre, dpre_o, local.at[13])]
    for c in outs:
        c.start()

    def last_rows(group, r0, size):
        v = dpre[pl.ds(r0, size), :]
        return v, v * b[pl.ds(r0, size), :]

    with scope("last stats"):
        local_sums = stats(last_rows, d)
    with scope("total"):
        last_o[...] = totals.run(4, local_sums)
    halos[1].done()
    with scope("finish"):
        for g in gather:
            g.finish()
    for n, src, dst in ((0, sw1, tb1), (1, sw2, tb2)):
        twin_copy(n, src, dst).wait_send()
    for c in (taps_copy2, zc3, xc3, xc4, *outs):
        c.wait()


def forward_call(s, x, grad, sw1, uw1, sw2, uw2, norm, live, inverse):
    any_, vmem, smem = (pl.BlockSpec(memory_space=m) for m in (pl.ANY, pltpu.VMEM, pltpu.SMEM))
    S = jax.ShapeDtypeStruct
    m, d, mid = s.m, s.d, s.mid
    gs = S((s.slabs, mid, s.kw), BF)
    gu = S((3 * mid, d), BF)
    taps = S((s.slabs, m, s.kw), BF)
    wide, narrow = S((m, mid), F32), S((m, d), F32)
    zs = S((m, mid), BF)
    outs = (gs, gu, gs, gu, taps, taps, wide, narrow, wide, narrow, zs, zs, narrow, narrow,
            S((2, mid), F32), S((2, d), F32), S((2, mid), F32), S((2, d), F32), S((4, d), F32))
    specs = (any_,) * 14 + (vmem,) * 5
    dma, V = pltpu.SemaphoreType.DMA, pltpu.VMEM
    nb = s.batches
    n_sums = 5
    scratch = [
        V((s.kw, s.nb), BF), V((s.kw, s.nb), BF), V((s.nb, s.kw), BF), V((s.nb, s.kw), BF),
        V((s.slabs, mid, s.kw), BF), V((3 * mid, d), BF), V((s.slabs, m, s.kw), BF),
        V((m, mid), F32), V((m, mid), BF),
        V((s.sides[0] + 2, s.sides[0] + 2, 8, d), F32), V((s.sides[1] + 2, s.sides[1] + 2, 8, d), F32),
        V((m, d), F32), V((2, m, d), BF), V((2, m, d), BF),
        V((n_sums, s.slots, 4, mid), F32), V((n_sums, nb, 4, mid), F32),
        dma((4, 5, 4, nb)), dma((4, 4, nb)), dma((4, 4, nb)), dma((2,)), dma((2,)), dma((14,)), dma((5, 2)),
        dma((2, 2, 2)), dma((2, 2, 2)), dma((2,)), dma((2,)), V((m - s.cut, d), BF),
        V((m, d), F32), V((m, d), F32),
        dma((n_sums, s.slots)), dma((n_sums, s.slots)), dma((n_sums, nb)), dma((n_sums, nb)),
    ]
    return pl.pallas_call(
        functools.partial(forward_kernel, s),
        out_shape=outs,
        in_specs=[vmem, vmem, vmem, any_, vmem, any_, vmem, vmem, smem],
        out_specs=specs,
        scratch_shapes=scratch,
        compiler_params=pltpu.CompilerParams(
            collective_id=0, has_side_effects=True, vmem_limit_bytes=63 * 2**20
        ),
        name="forward",
    )(x, grad, sw1, uw1, sw2, uw2, norm, live, inverse)


def cell_major(s, small, large):
    parts = []
    for group, v in enumerate((small, large)):
        v = v.reshape(s.clips, s.cells[group], s.d).transpose(1, 0, 2)
        parts.append(jnp.pad(v, ((0, s.padded[group] - s.cells[group]), (0, 0), (0, 0))))
    return jnp.concatenate(parts, axis=0).reshape(s.m, s.d)


def clip_major(s, v):
    v = v.reshape(-1, s.clips, s.d)
    parts, base = [], 0
    for group in range(2):
        part = v[base : base + s.cells[group]].transpose(1, 0, 2)
        parts.append(part.reshape(s.clips, 1, s.cells[group], s.d))
        base += s.padded[group]
    return parts


def halves(s, w):
    return w.astype(BF).reshape(w.shape[0], 2, s.nb).transpose(1, 0, 2)


def add_into(dst, src, rows, step):
    def body(i, _):
        at = pl.ds(pl.multiple_of(i * step, 16), step)
        dst[at, :] = (dst[at, :].astype(F32) + src[at, :].astype(F32)).astype(BF)
        return 0

    lax.fori_loop(0, rows // step, body, 0)


class Scatter:
    def __init__(self, place, index, part, bufs, cut, rows, step, sems):
        self.p, self.n, self.part, self.cut, self.rows, self.step = place, index, part, cut, rows, step
        self.tr, self.fx, self.fa, self.rx, self.ry, self.ru, self.rd = bufs[:7]
        self.twin_s, self.twin_r, self.block_s, self.block_r = sems
        self.half = place.batches // 2

    FAR, SIDE, DEEP, RISE, FALL = range(5)

    def twin_copy(self, rel):
        p = self.p
        return send(self.part(rel, 1 - p.core), self.tr.at[rel], self.twin_s.at[self.n, rel],
                    self.twin_r.at[self.n, rel], p.device(TWIN))

    def block_copy(self, kind, b, src, dst, way):
        return send(src, dst, self.block_s.at[self.n, kind, b], self.block_r.at[self.n, kind, b],
                    self.p.device(way))

    def own(self, rel, b):
        return self.cut(self.part(rel, self.p.core), b)

    def far_copy(self, b):
        if b < self.half:
            return self.block_copy(self.FAR, b, self.own(3, b), self.cut(self.fx, b), ACROSS)
        return self.block_copy(self.FAR, b, self.own(3, b), self.cut(self.fa, b - self.half), ALONG)

    def side_copy(self, b):
        return self.block_copy(self.SIDE, b, self.own(1, b), self.cut(self.rx, b), ACROSS)

    def deep_copy(self, b):
        return self.block_copy(self.DEEP, b, self.own(2, b), self.cut(self.ry, b), ALONG)

    def rise_copy(self, b):
        return self.block_copy(self.RISE, b, self.own(0, b), self.cut(self.ru, b + 1), UP)

    def fall_copy(self, b):
        return self.block_copy(self.FALL, b, self.own(0, b), self.cut(self.ru, b), DOWN)

    def arrive(self, kind, b, ref):
        self.block_copy(kind, b, ref, ref, TWIN).wait_recv()

    def add(self, dst, src):
        add_into(dst, src, self.rows, self.step)

    def order(self):
        n = self.p.batches
        out = []
        for i in range(n // 2):
            out += [n - 1 - i, i]
        return out

    def twin(self, rel):
        self.twin_copy(rel).start()

    def join(self, rel):
        p = self.p
        self.twin_copy(rel).wait_recv()
        for b in self.order():
            self.add(self.own(rel, b), self.cut(self.tr.at[rel], b))
            if rel == 3:
                self.far_copy(b).start()
            if rel == 1 and b < self.half:
                self.side_copy(b).start()
            if rel == 2 and b >= self.half:
                self.deep_copy(b).start()

    def relay(self, b):
        if b < self.half:
            src = self.cut(self.fx, b)
            self.arrive(self.FAR, b, src)
            self.add(self.own(2, b), src)
            self.deep_copy(b).start()
        else:
            src = self.cut(self.fa, b - self.half)
            self.arrive(self.FAR, b, src)
            self.add(self.own(1, b), src)
            self.side_copy(b).start()

    def collect(self, b):
        for kind, buf in ((self.SIDE, self.rx), (self.DEEP, self.ry)):
            src = self.cut(buf, b)
            self.arrive(kind, b, src)
            self.add(self.own(0, b), src)

    def gather_own(self):
        p = self.p
        n = p.batches

        @pl.when(p.z < self.half)
        def _():
            for b in range(n - 1, -1, -1):
                self.collect(b)
                if b:
                    pl.when(p.z == 0)(lambda b=b: self.rise_copy(b).start())

        @pl.when(p.z >= self.half)
        def _():
            for b in range(n):
                self.collect(b)
                if b < n - 1:
                    pl.when(p.z == n - 1)(lambda b=b: self.fall_copy(b).start())

    def chain(self, stage):
        p = self.p

        @pl.when(p.z == stage)
        def _():
            for b in range(p.batches - 1, stage, -1):
                src = self.cut(self.ru, b + 1)
                self.arrive(self.RISE, b, src)
                self.add(self.own(0, b), src)
                self.rise_copy(b).start()

        @pl.when(p.z == p.batches - 1 - stage)
        def _():
            for b in range(p.batches - 1 - stage):
                src = self.cut(self.ru, b)
                self.arrive(self.FALL, b, src)
                self.add(self.own(0, b), src)
                self.fall_copy(b).start()

    def result(self):
        p = self.p
        up, down = self.cut(self.ru, p.z + 1), self.cut(self.ru, p.z)
        pl.when(p.z > 0)(lambda: self.arrive(self.RISE, p.z, up))
        pl.when(p.z < p.batches - 1)(lambda: self.arrive(self.FALL, p.z, down))

        @pl.when(p.z == 0)
        def _():
            up[...] = jnp.zeros(up.shape, BF)

        @pl.when(p.z == p.batches - 1)
        def _():
            down[...] = jnp.zeros(down.shape, BF)

        return self.own(0, p.z)[...].astype(F32) + up[...].astype(F32) + down[...].astype(F32)

    def sent(self, rel):
        p = self.p
        self.twin_copy(rel).wait_send()
        for b in range(p.batches):
            if rel == 3:
                self.far_copy(b).wait_send()
            elif rel == 1:
                self.side_copy(b).wait_send()
            elif rel == 2:
                self.deep_copy(b).wait_send()
            else:
                pl.when(p.z < b)(lambda b=b: self.rise_copy(b).wait_send())
                pl.when(p.z > b)(lambda b=b: self.fall_copy(b).wait_send())

    def act(self, word):
        if word == "c":
            self.gather_own()
        else:
            {"j": self.join, "r": self.relay, "k": self.chain}[word[0]](int(word[1]))


class LineScatter(Scatter):
    def rise(self, rel, b):
        return send(self.own(rel, b), self.cut(self.ru.at[rel], b + 1), self.line_s.at[self.n, 0, rel, b],
                    self.line_r.at[self.n, 0, rel, b], self.p.device(UP))

    def fall(self, rel, b):
        return send(self.own(rel, b), self.cut(self.ru.at[rel], b), self.line_s.at[self.n, 1, rel, b],
                    self.line_r.at[self.n, 1, rel, b], self.p.device(DOWN))

    def landed(self, way, rel, b):
        ref = self.cut(self.ru.at[rel], b + 1 - way)
        send(ref, ref, self.line_s.at[self.n, way, rel, b], self.line_r.at[self.n, way, rel, b],
             self.p.device(TWIN)).wait_recv()
        return ref

    def join(self, rel):
        p = self.p
        self.twin_copy(rel).wait_recv()
        add_into(self.part(rel, p.core), self.tr.at[rel], self.rows, self.step)

    def ends(self, up, down):
        p = self.p

        @pl.when(p.z == 0)
        def _():
            for rel in (3, 1, 2, 0):
                self.rise(rel, up).start()

        @pl.when(p.z == p.batches - 1)
        def _():
            for rel in (3, 1, 2, 0):
                self.fall(rel, down).start()

    def chain(self, stage):
        p = self.p

        @pl.when(p.z == stage)
        def _():
            for b in range(p.batches - 1, stage, -1):
                for rel in (3, 1, 2, 0):
                    self.add(self.own(rel, b), self.landed(0, rel, b))
                    self.rise(rel, b).start()

        @pl.when(p.z == p.batches - 1 - stage)
        def _():
            for b in range(p.batches - 1 - stage):
                for rel in (3, 1, 2, 0):
                    self.add(self.own(rel, b), self.landed(1, rel, b))
                    self.fall(rel, b).start()

    def settle(self, rel):
        p = self.p
        at = self.own(rel, p.z)
        pl.when(p.z > 0)(lambda: self.add(at, self.landed(0, rel, p.z)))
        pl.when(p.z < p.batches - 1)(lambda: self.add(at, self.landed(1, rel, p.z)))

    def cross(self, kind, rel, dst, way):
        return self.block_copy(kind, 0, self.own(rel, self.p.z), dst, way)

    def corner(self):
        self.settle(3)
        self.cross(self.FAR, 3, self.fx, ACROSS).start()
        self.settle(1)
        self.cross(self.SIDE, 1, self.rx, ACROSS).start()
        self.settle(2)

    def turn(self):
        self.arrive(self.FAR, 0, self.fx)
        self.add(self.own(2, self.p.z), self.fx)
        self.cross(self.DEEP, 2, self.ry, ALONG).start()
        self.settle(0)

    def result(self):
        self.arrive(self.SIDE, 0, self.rx)
        self.arrive(self.DEEP, 0, self.ry)
        return (self.own(0, self.p.z)[...].astype(F32) + self.rx[...].astype(F32) + self.ry[...].astype(F32))

    def sent(self):
        p = self.p
        for rel in range(4):
            self.twin_copy(rel).wait_send()
            for b in range(p.batches):
                pl.when(p.z < b)(lambda rel=rel, b=b: self.rise(rel, b).wait_send())
                pl.when(p.z > b)(lambda rel=rel, b=b: self.fall(rel, b).wait_send())
        self.cross(self.FAR, 3, self.fx, ACROSS).wait_send()
        self.cross(self.SIDE, 1, self.rx, ACROSS).wait_send()
        self.cross(self.DEEP, 2, self.ry, ALONG).wait_send()

    def act(self, word):
        if word[0] == "j":
            self.join(int(word[1]))
        elif word[0] == "k":
            self.chain(int(word[1]))
        elif word[0] == "z":
            self.ends(int(word[1]), int(word[2]))
        else:
            {"c": self.corner, "t": self.turn}[word]()


def rows_of_grid(s, grids, group, r0):
    side = s.sides[group]
    base = 0 if group == 0 else s.rows[0]
    first = (r0 - base) // 8
    cells = [grids[group][1 + (first + n) // side, 1 + lax.rem(first + n, side)] for n in range(10)]
    return jnp.concatenate(cells, axis=0)


def slope(v):
    gate = sigmoid(v)
    return gate * (1.0 + v * (1.0 - gate))


def backward_kernel(s, *refs):
    (gs1, gu1, gs2, gu2, taps1, taps2, xh1, xh2, xh3, xh4, z1, z3, dpre,
     r1, r2, r3, r4, last, norm, live_ref, inverse,
     dx, gso1, gso2, guo1, guo2, ng, square,
     ps, tr, fx, fa, rx1, ry1, rz1, rx2, ry2, rz2, pu, utr, ufx, urx, ury, urz, relay,
     nat, flip, d3, turn, planes, lines,
     load, tap_sem, tile_sem, halo_send, halo_recv, pass_send, pass_recv, line_s, line_r, twin_s, twin_r, block_s, block_r, half_s, half_r,
     pl_send, pl_recv, ln_send, ln_recv) = refs
    p = Place(s.batches, s.slots)
    live = [live_ref[g] for g in range(2)]
    inv = [inverse[g] for g in range(2)]
    totals = Totals(p, 4, planes, lines, (pl_send, pl_recv, ln_send, ln_recv))
    d, mid, m = s.d, s.mid, s.m
    bounds = (0, mid, mid + d, 2 * mid + d, 2 * mid + 2 * d)

    def gain_bias(n):
        return norm[0:1, bounds[n] : bounds[n + 1]], norm[1:2, bounds[n] : bounds[n + 1]]

    with scope("greet"):
        p.greet()
    def go(words):
        with scope("reduce " + words):
            for word in words.split():
                scatter(int(word[0])).act(word[1:])

    def cut_rows(ref, b):
        at = b * s.nb if isinstance(b, int) else pl.multiple_of(b * s.nb, 16)
        return ref.at[pl.ds(at, s.nb)]

    def cut_lanes(ref, b):
        at = b * s.uc if isinstance(b, int) else pl.multiple_of(b * s.uc, 128)
        return ref.at[:, pl.ds(at, s.uc)]

    def slot(n, rel):
        return 4 if n == 0 and rel == 0 else rel

    def part_s(n, rel, core):
        return ps.at[slot(n, rel), core]

    def part_u(rel, core):
        return pu.at[pl.ds(pl.multiple_of((p.rel[rel] * 2 + core) * s.ur, 16), s.ur)]

    sems = (twin_s, twin_r, block_s, block_r)

    def scatter(n):
        if n % 2 == 0:
            rx, ry, rz = (rx1, ry1, rz1) if n == 0 else (rx2, ry2, rz2)
            return Scatter(p, n, functools.partial(part_s, n), (tr, fx, fa, rx, ry, rz, None), cut_rows, s.nb, 48, sems)
        sc = LineScatter(p, n, part_u, (utr, ufx, None, urx, ury, urz, None), cut_lanes, s.ur, 144, sems)
        sc.line_s, sc.line_r = line_s, line_r
        return sc

    for side, edge in ((0, p.slots - 1), (2, 0)):
        @pl.when(p.t == edge)
        def _(side=side):
            d3[side] = jnp.zeros(d3.shape[1:], BF)

    def norm_back(n, total, scale, dh, xhat, store, size, width):
        gain, _ = gain_bias(n)
        ng[0:1, bounds[n] : bounds[n + 1]] = total[2:3, :] + total[3:4, :]
        ng[1:2, bounds[n] : bounds[n + 1]] = total[0:1, :] + total[1:2, :]
        lead = [gain * scale[g : g + 1, :] for g in range(2)]
        mean = [total[g : g + 1, :] * inv[g] for g in range(2)]
        cross = [total[2 + g : 3 + g, :] * inv[g] for g in range(2)]

        def rows(group, r0, c):
            at = pl.ds(r0, size)
            v = lead[group] * (dh[at, :] - mean[group] - xhat[at, :] * cross[group])
            v = v.reshape(size // 8, 8, width) * live[group][None]
            store(at, v.reshape(size, width))
            return c

        chunks(s, size, rows)

    def upstream(n, dz, xhat, fetch, size, width):
        gain, bias = gain_bias(n)

        def body(group, r0, c):
            at = pl.ds(r0, size)
            xv = xhat[at, :]
            v = fetch(group, r0) * slope(xv * gain + bias)
            dz[at, :] = v
            return (c[0] + jnp.sum(v.reshape(size // 8, 8, width), axis=0),
                    c[1] + jnp.sum((v * xv).reshape(size // 8, 8, width), axis=0))

        zero = jnp.zeros((8, width), F32)
        small, large = chunks(s, size, body, (zero, zero))
        rows = [jnp.sum(v * live[g], axis=0, keepdims=True) for v, g in
                ((small[0], 0), (large[0], 1), (small[1], 0), (large[1], 1))]
        return jnp.concatenate(rows, axis=0)

    def transpose():
        def body(j, _):
            at = pl.ds(pl.multiple_of(j * 128, 128), 128)
            flip[at, :] = nat[:, at].T
            return 0

        with scope("transpose"):
            lax.fori_loop(0, mid // 128, body, 0)

    def fetch_into(src, dst, sem):
        c = pltpu.make_async_copy(src, dst, load.at[sem])
        c.start()
        return c

    def narrow_store(at, v):
        d3[1, at, :] = v.astype(BF)

    def nat_store(at, v):
        nat[at, :] = v.astype(BF)

    def first(up, xh):
        c1, c2 = fetch_into(dpre, up, 0), fetch_into(xh4, xh, 1)
        c1.wait()
        c2.wait()
        norm_back(3, last[...], r4[...], up, xh, narrow_store, 80, d)

    fetch_into(z3, nat, 2)
    with scope("norm4 back"):
        pl.run_scoped(first, pltpu.VMEM((m, d), F32), pltpu.VMEM((m, d), F32))
    zero_padding(s, d3.at[1], d)

    def temporal(stage, index, n, whole, zs, xhs, scale, words, finish):
        halo = Halo(p, stage, lambda side: d3.at[1], lambda side: d3.at[2 - 2 * side], relay,
                    (halo_send, halo_recv, pass_send, pass_recv), s.cut)

        def run(dz, xh, wu):
            halo.start(0)
            halo.start(1)
            cz = pltpu.make_async_copy(zs, nat, load.at[2])
            if stage:
                cz.start()
            cw = fetch_into(whole, wu, 3)
            cx = fetch_into(xhs, xh, 4)
            cz.wait()
            transpose()
            cw.wait()

            def field_grad(k):
                for lo, width in wide_cuts(mid):
                    y = lax.dot_general(d3[k], wu[k * mid + lo : k * mid + lo + width, :], NT_DIMS,
                                        preferred_element_type=F32)
                    if k == 1:
                        dz[:, lo : lo + width] = y
                    else:
                        dz[:, lo : lo + width] += y

            def weight_grad(k):
                with scope("u weight grad"):
                    pu[k * mid : (k + 1) * mid, :] = jnp.dot(
                        flip[...], d3[k], preferred_element_type=F32
                    ).astype(BF)

            with scope("u grads"):
                field_grad(1)
            with scope("relay"):
                halo.relay()
            go(words[0])
            with scope("halo wait"):
                halo.wait(1)
            with scope("u grads"):
                field_grad(0)
            with scope("halo wait"):
                halo.wait(0)
            go(words[2])
            with scope("u grads"):
                field_grad(2)
            cx.wait()

            def fetch(group, r0):
                return dz[pl.ds(r0, 16), :]

            with scope("upstream"):
                local_sums = upstream(n, dz, xh, fetch, 16, mid)
            extra = finish()
            with scope("total"):
                total = totals.run(2 * stage, local_sums, lambda: weight_grad(1),
                                   lambda: (weight_grad(0), weight_grad(2)) and None)
            sc = scatter(index)
            for rel in (3, 1, 2, 0):
                sc.twin(rel)
            with scope("norm back"):
                norm_back(n, total, scale, dz, xh, nat_store, 16, mid)
            go(words[1])
            return extra

        extra = pl.run_scoped(run, pltpu.VMEM((m, mid), F32), pltpu.VMEM((m, mid), F32), pltpu.VMEM((3 * mid, d), BF))
        zero_padding(s, nat, mid)
        halo.done()
        return extra

    def finish_u(n, ref):
        sc = scatter(n)
        g = sc.result()
        ref[...] = g
        sc.sent()
        return jnp.sum(g * g, axis=0, keepdims=True)

    def finish_s(n, out):
        sc = scatter(n)
        g = sc.result()
        turn[...] = g.T
        rows = s.kw // 2

        def half(core):
            return turn.at[pl.ds(pl.multiple_of(core * rows, 16), rows)]

        keep = pltpu.make_async_copy(half(p.core), out.at[p.core], load.at[8])
        keep.start()
        copy = send(half(1 - p.core), out.at[p.core], half_s.at[n // 2], half_r.at[n // 2], p.device(TWIN))
        copy.start()
        send(half(p.core), out.at[1 - p.core], half_s.at[n // 2], half_r.at[n // 2], p.device(TWIN)).wait_recv()
        copy.wait_send()
        keep.wait()
        return jnp.sum(jnp.sum((g * g).reshape(s.nb, s.kw // 128, 128), axis=0), axis=0, keepdims=True)

    pieces = []
    for tap in range(9):
        lo, end, found = tap * d, (tap + 1) * d, []
        while lo < end:
            hi = min(end, (lo // s.kw + 1) * s.kw)
            found.append((lo // s.kw, lo % s.kw, lo - tap * d, hi - lo))
            lo = hi
        pieces.append(found)

    def spatial(index, whole, taps, grids, tap_buf, tile, words, tap_words, early, ready):
        rels = (3, 1, 2, 0)

        def tap_load(i):
            return pltpu.make_async_copy(taps.at[p.rel[rels[i]]], tap_buf.at[i % 2], tap_sem.at[i])

        def tile_loads(tap):
            return [
                pltpu.make_async_copy(
                    whole.at[slab, :, pl.ds(lane, width)], tile.at[tap % 2, :, pl.ds(at, width)],
                    tile_sem.at[tap, n],
                )
                for n, (slab, lane, at, width) in enumerate(pieces[tap])
            ]

        tap_load(0).start()
        tap_load(1).start()
        for c in tile_loads(0):
            c.start()
        go(early)
        transpose()
        for grid in grids:
            def clear(i, _, grid=grid):
                grid[i] = jnp.zeros(grid.shape[1:], F32)
                return 0

            lax.fori_loop(0, grid.shape[0], clear, 0)
        sc = scatter(index)
        for i, rel in enumerate(rels):
            tap_load(i).wait()
            ready(rel)
            with scope("dw slab"):
                for lo, width in wide_cuts(s.kw):
                    y = jnp.dot(flip[...], tap_buf[i % 2, :, lo : lo + width], preferred_element_type=F32).astype(BF)
                    for n in range(2 * s.batches):
                        b, core = n // 2, n % 2
                        ps[slot(index, rel), core, b * s.nb : (b + 1) * s.nb, lo : lo + width] = y[n * s.nb : (n + 1) * s.nb]
            sc.twin(rel)
            if i + 2 < 4:
                tap_load(i + 2).start()
            go(words[i])
        for tap in range(9):
            if tap + 1 < 9:
                for c in tile_loads(tap + 1):
                    c.start()
            for c in tile_loads(tap):
                c.wait()
            i, j = tap // 3, tap % 3
            with scope("dx tap"):
                y = jnp.dot(nat[...], tile[tap % 2], preferred_element_type=F32)
                base = 0
                for group in range(2):
                    side = s.sides[group]
                    part = y[base : base + s.cells[group] * 8].reshape(side, side, 8, d)
                    grids[group][i : i + side, j : j + side] += part
                    base += s.rows[group]
            go(tap_words[tap])
        clear_pad_cells(s, grids)

    grid_types = (
        pltpu.VMEM((s.sides[0] + 2, s.sides[0] + 2, 8, d), F32),
        pltpu.VMEM((s.sides[1] + 2, s.sides[1] + 2, 8, d), F32),
    )
    load_types = (pltpu.VMEM((2, m, s.kw), BF), pltpu.VMEM((2, mid, d), BF))
    narrow_types = (pltpu.VMEM((m, d), F32), pltpu.VMEM((m, d), F32))

    nothing = jnp.zeros((1, 128), F32)
    temporal(0, 3, 2, gu2, z3, xh3, r3[...], ("", "3j3 3j1 3j2 3j0", ""), lambda: nothing)

    def second(*grids):
        pl.run_scoped(
            lambda tap_buf, tile: spatial(
                2, gs2, taps2, grids, tap_buf, tile, ("", "2j3", "2j1 3k1", "2j2"),
                ("2j0", "", "", "", "3k2", "", "", "", ""), "3z30 3z21 3z12", lambda rel: None),
            *load_types,
        )

        def rest(b, xh):
            fetch_into(xh2, xh, 5).wait()

            def fetch(group, r0):
                return rows_of_grid(s, grids, group, r0)

            with scope("upstream"):
                local_sums = upstream(1, b, xh, fetch, 80, d)
            with scope("total"):
                total = totals.run(1, local_sums)
            with scope("norm back"):
                norm_back(1, total, r2[...], b, xh, narrow_store, 80, d)

        pl.run_scoped(rest, *narrow_types)

    pl.run_scoped(second, *grid_types)
    zero_padding(s, d3.at[1], d)

    def finish_small():
        with scope("finish u"):
            return finish_u(3, guo2)

    sums = temporal(1, 1, 0, gu1, z1, xh1, r1[...],
                    ("3c 2r0 2r1 2r3 2r2", "2c 1j3 1j1 1j2 1j0 1z30 1z21 1z12", "3t"), finish_small)

    def final(*grids):
        def ready(rel):
            if rel:
                scatter(2).sent(rel)

        pl.run_scoped(
            lambda tap_buf, tile: spatial(
                0, gs1, taps1, grids, tap_buf, tile, ("", "0j3 2k1", "0j1", "0j2 2k2"),
                ("0j0", "", "0r0 0r3", "0r1 0r2", "1k1", "", "", "", "1k2"), "", ready),
            *load_types,
        )
        with scope("finish s"):
            sums = finish_s(2, gso2)
        scatter(2).sent(0)

        def rest(b, up):
            fetch_into(dpre, up, 6).wait()

            def rows(group, r0, c):
                b[pl.ds(r0, 80), :] = rows_of_grid(s, grids, group, r0) + up[pl.ds(r0, 80), :]
                return c

            with scope("dx"):
                chunks(s, 80, rows)
            cd = fetch_into(b, dx, 7)
            go("1c 0c")
            go("1t 0k1")
            go("0k2")
            with scope("finish u"):
                part = finish_u(1, guo1)
            with scope("finish s"):
                part = part + finish_s(0, gso1)
            cd.wait()
            for rel in range(4):
                scatter(0).sent(rel)
            return part

        return sums + pl.run_scoped(rest, *narrow_types)

    sums = sums + pl.run_scoped(final, *grid_types)
    with scope("total"):
        square[...] = totals.run(3, jnp.broadcast_to(sums, (4, 128)))


def backward_call(s, saved, norm, live, inverse):
    any_, vmem, smem = (pl.BlockSpec(memory_space=m) for m in (pl.ANY, pltpu.VMEM, pltpu.SMEM))
    S, V, dma = jax.ShapeDtypeStruct, pltpu.VMEM, pltpu.SemaphoreType.DMA
    m, d, mid, nb, kw = s.m, s.d, s.mid, s.batches, s.kw
    half = nb // 2
    outs = (S((m, d), F32), S((2, kw // 2, s.nb), F32), S((2, kw // 2, s.nb), F32),
            S((s.ur, s.uc), F32), S((s.ur, s.uc), F32), S((2, 2 * (mid + d)), F32), S((4, 128), F32))
    rows = nb * s.nb
    scratch = [
        V((5, 2, rows, kw), BF), V((4, rows, kw), BF), V((half * s.nb, kw), BF), V((half * s.nb, kw), BF),
        V((rows, kw), BF), V((rows, kw), BF), V((rows + s.nb, kw), BF),
        V((rows, kw), BF), V((rows, kw), BF), V((rows + s.nb, kw), BF),
        V((3 * mid, d), BF), V((4, s.ur, d), BF), V((s.ur, s.uc), BF), V((s.ur, s.uc), BF), V((s.ur, s.uc), BF),
        V((4, s.ur, d + s.uc), BF), V((m - s.cut, d), BF),
        V((m, mid), BF), V((mid, m), BF), V((3, m, d), BF), V((kw, s.nb), F32),
        V((4, s.slots, 4, mid), F32), V((4, nb, 4, mid), F32),
        dma((9,)), dma((4,)), dma((9, 3)), dma((2, 2, 2)), dma((2, 2, 2)), dma((2,)), dma((2,)),
        dma((4, 2, 4, nb)), dma((4, 2, 4, nb)),
        dma((4, 4)), dma((4, 4)), dma((4, 5, nb)), dma((4, 5, nb)), dma((2,)), dma((2,)),
        dma((4, s.slots)), dma((4, s.slots)), dma((4, nb)), dma((4, nb)),
    ]
    return pl.pallas_call(
        functools.partial(backward_kernel, s),
        out_shape=outs,
        in_specs=[any_] * 13 + [vmem] * 7 + [smem],
        out_specs=(any_,) * 3 + (vmem,) * 4,
        scratch_shapes=scratch,
        compiler_params=pltpu.CompilerParams(
            collective_id=1, has_side_effects=True, vmem_limit_bytes=63 * 2**20
        ),
        name="backward",
    )(*saved, norm, live, inverse)


def body(batches, slots, *args):
    x_small, x_large = args[0], args[1]
    if not fits(x_small.shape, x_large.shape, batches, slots):
        return plain_body(*args)
    return fast_body(Shape(x_small.shape, x_large.shape, batches, slots), *args)


def fast_body(
    s,
    x_small,
    x_large,
    grad_small,
    grad_large,
    clip_counts,
    first_spatial,
    first_temporal,
    second_spatial,
    second_temporal,
    norm_params,
    first_spatial_momentum,
    first_temporal_momentum,
    second_spatial_momentum,
    second_temporal_momentum,
    norm_momentum,
    first_spatial_variance,
    first_temporal_variance,
    second_spatial_variance,
    second_temporal_variance,
    norm_variance,
):
    z = lax.axis_index("batch")
    slots = jnp.arange(s.clips, dtype=jnp.int32)
    counts = lax.dynamic_index_in_dim(clip_counts, z, 1, keepdims=False)
    live = (slots[None, :] < counts[:, None]).astype(F32)[:, :, None]
    totals = jnp.sum(clip_counts, axis=1).astype(F32) * (s.slots * jnp.array(s.cells, F32))
    inverse = 1.0 / totals
    x = cell_major(s, x_small, x_large)
    grad = cell_major(s, grad_small, grad_large)
    res = forward_call(
        s, x, grad, halves(s, first_spatial), first_temporal.astype(BF), halves(s, second_spatial),
        second_temporal.astype(BF), norm_params, live, inverse,
    )
    out_small, out_large = clip_major(s, res[12])
    saved = res[:12] + res[13:]
    dx, gs1, gs2, gu1, gu2, grad_params, square = backward_call(s, saved, norm_params, live, inverse)
    in_small, in_large = clip_major(s, dx)

    def whole(g):
        return g.transpose(1, 0, 2).reshape(g.shape[1], 2 * g.shape[2])

    grad_norm = jnp.sqrt(jnp.sum(square[0]) + jnp.sum(grad_params * grad_params))
    factor = THRESHOLD / jnp.maximum(grad_norm, THRESHOLD)
    one = adamw(first_spatial, whole(gs1), first_spatial_momentum, first_spatial_variance, factor,
                WEIGHT_RATE, WEIGHT_DECAY)
    two = adamw(first_temporal, gu1, first_temporal_momentum, first_temporal_variance, factor,
                WEIGHT_RATE, WEIGHT_DECAY)
    three = adamw(second_spatial, whole(gs2), second_spatial_momentum, second_spatial_variance, factor,
                  WEIGHT_RATE, WEIGHT_DECAY)
    four = adamw(second_temporal, gu2, second_temporal_momentum, second_temporal_variance, factor,
                 WEIGHT_RATE, WEIGHT_DECAY)
    norms = adamw(norm_params, grad_params, norm_momentum, norm_variance, factor, NORM_RATE, 0.0)
    return (out_small, out_large, in_small, in_large, grad_norm) + one + two + three + four + norms


def solution(mesh):
    return jax.shard_map(
        functools.partial(body, mesh.shape["batch"], mesh.shape["tm"]),
        mesh=mesh,
        in_specs=(
            P("batch", "tm", None, None),
            P("batch", "tm", None, None),
            P("batch", "tm", None, None),
            P("batch", "tm", None, None),
            P(),
            P("tm", "batch"),
            P("tm", "batch"),
            P("tm", "batch"),
            P("tm", "batch"),
            P(),
            P("tm", "batch"),
            P("tm", "batch"),
            P("tm", "batch"),
            P("tm", "batch"),
            P(),
            P("tm", "batch"),
            P("tm", "batch"),
            P("tm", "batch"),
            P("tm", "batch"),
            P(),
        ),
        out_specs=(
            P("batch", "tm", None, None),
            P("batch", "tm", None, None),
            P("batch", "tm", None, None),
            P("batch", "tm", None, None),
            P(),
            P("tm", "batch"),
            P("tm", "batch"),
            P("tm", "batch"),
            P("tm", "batch"),
            P("tm", "batch"),
            P("tm", "batch"),
            P("tm", "batch"),
            P("tm", "batch"),
            P("tm", "batch"),
            P("tm", "batch"),
            P("tm", "batch"),
            P("tm", "batch"),
            P(),
            P(),
            P(),
        ),
        check_vma=False,
    )
```

```python
import contextlib
import functools
import math

import jax
import jax.numpy as jnp
from jax import lax
from jax.experimental import pallas as pl
from jax.experimental.pallas import tpu as pltpu
from jax.sharding import PartitionSpec as P

D = 512
MID = 1152
HS = 7
HL = 10
STEP = 10


NORM_EPS = 1e-05
THRESHOLD = 1.0
BETA_ONE = 0.9
BETA_TWO = 0.999
WEIGHT_RATE = 0.03
NORM_RATE = 0.25
WEIGHT_DECAY = 0.05
ADAM_EPS = 1e-08


def padded_2(value, sides, width):
    for axis, dim in sides:
        size, length = (lax.axis_size(axis), value.shape[dim])
        up = [(i, (i + 1) % size) for i in range(size - 1)]
        down = [(j, i) for i, j in up]
        last = lax.slice_in_dim(value, length - width, length, axis=dim)
        first = lax.slice_in_dim(value, 0, width, axis=dim)
        before = lax.ppermute(last, axis, up)
        after = lax.ppermute(first, axis, down)
        value = jnp.concatenate([before, value, after], axis=dim)
    return value


def silu_slope(input_value):
    sigmoid_value = jax.nn.sigmoid(input_value)
    return sigmoid_value * (1.0 + input_value * (1.0 - sigmoid_value))


def spatial_taps(field, side):
    clips, frames, cells, channels = field.shape
    grid = field.reshape(clips, frames, side, side, channels)
    padded = jnp.pad(grid, ((0, 0), (0, 0), (1, 1), (1, 1), (0, 0)))
    pieces = [
        padded[:, :, row : row + side, column : column + side, :]
        for row in range(3)
        for column in range(3)
    ]
    return jnp.concatenate(pieces, axis=-1).reshape(clips * frames * cells, 9 * channels)


def spatial_forward(field_small, field_large, weight):
    taps_small = spatial_taps(field_small, HS)
    taps_large = spatial_taps(field_large, HL)
    result_small = jnp.dot(taps_small, weight, preferred_element_type=jnp.float32).reshape(
        field_small.shape[:3] + (weight.shape[1],)
    )
    result_large = jnp.dot(taps_large, weight, preferred_element_type=jnp.float32).reshape(
        field_large.shape[:3] + (weight.shape[1],)
    )
    return (jnp.concatenate([result_small, result_large], axis=2), taps_small, taps_large)


def spatial_backward(upstream_rows, weight, shape, side):
    clips, frames, cells, channels = shape
    columns = lax.dot_general(
        upstream_rows, weight, (((1,), (1,)), ((), ())), preferred_element_type=jnp.float32
    )
    columns = columns.reshape(clips, frames, side, side, 9 * channels)
    padded = jnp.pad(columns, ((0, 0), (0, 0), (1, 1), (1, 1), (0, 0)))
    final_result = None
    for row in range(3):
        for column in range(3):
            offset = (3 * row + column) * channels
            window = padded[
                :,
                :,
                2 - row : 2 - row + side,
                2 - column : 2 - column + side,
                offset : offset + channels,
            ]
            final_result = window if final_result is None else final_result + window
    return final_result.reshape(clips, frames, cells, channels)


def temporal_forward(field, weight):
    padded = padded_2(field, (("tm", 1),), 1)
    frames = field.shape[1]
    pieces = jnp.concatenate([padded[:, shift : shift + frames] for shift in range(3)], axis=-1)
    rows = pieces.reshape(-1, pieces.shape[-1])
    final_result = jnp.dot(rows, weight, preferred_element_type=jnp.float32).reshape(
        field.shape[:3] + (weight.shape[1],)
    )
    return (final_result, rows)


def temporal_backward(upstream_gradient, weight):
    padded = padded_2(upstream_gradient, (("tm", 1),), 1)
    frames = upstream_gradient.shape[1]
    pieces = jnp.concatenate(
        [padded[:, 2 - shift : 2 - shift + frames] for shift in range(3)], axis=-1
    )
    rows = pieces.reshape(-1, pieces.shape[-1])
    kernel = (
        weight.reshape(3, -1, weight.shape[1]).transpose(1, 0, 2).reshape(-1, 3 * weight.shape[1])
    )
    final_result = lax.dot_general(
        rows, kernel, (((1,), (1,)), ((), ())), preferred_element_type=jnp.float32
    )
    return final_result.reshape(upstream_gradient.shape[:3] + (kernel.shape[0],))


def group_totals(leading_part, trailing_part, active_flags, split_point):
    leading_cells = jnp.sum(active_flags * leading_part, axis=(0, 1))
    trailing_cells = jnp.sum(active_flags * trailing_part, axis=(0, 1))
    first_groups = jnp.stack(
        [jnp.sum(leading_cells[:split_point], axis=0), jnp.sum(leading_cells[split_point:], axis=0)]
    )
    second_groups = jnp.stack(
        [
            jnp.sum(trailing_cells[:split_point], axis=0),
            jnp.sum(trailing_cells[split_point:], axis=0),
        ]
    )
    return (first_groups, second_groups)


def per_cell(stat, split_point, cells):
    channels = stat.shape[1]
    return jnp.concatenate(
        [
            jnp.broadcast_to(stat[0], (split_point, channels)),
            jnp.broadcast_to(stat[1], (cells - split_point, channels)),
        ],
        axis=0,
    )


def norm_forward_pass(
    input_value, active_flags, split_point, grand_totals, norm_gain_vector, norm_shift_bias
):
    running_sums, squared_values = group_totals(
        input_value, input_value * input_value, active_flags, split_point
    )
    running_sums, squared_values = lax.psum((running_sums, squared_values), ("batch", "tm"))
    mean = running_sums / grand_totals[:, None]
    scale = lax.rsqrt(squared_values / grand_totals[:, None] - mean * mean + NORM_EPS)
    cells = input_value.shape[2]
    cell_scale = per_cell(scale, split_point, cells)
    normalized_values = (input_value - per_cell(mean, split_point, cells)) * cell_scale
    return (normalized_values * norm_gain_vector + norm_shift_bias, normalized_values, cell_scale)


def norm_reverse_pass(
    upstream_gradient,
    normalized_values,
    cell_scale,
    norm_gain_vector,
    active_flags,
    split_point,
    grand_totals,
):
    running_sums, cross_product = group_totals(
        upstream_gradient, upstream_gradient * normalized_values, active_flags, split_point
    )
    running_sums, cross_product = lax.psum((running_sums, cross_product), ("batch", "tm"))
    cells = upstream_gradient.shape[2]
    upstream_average = per_cell(running_sums / grand_totals[:, None], split_point, cells)
    cross_average = per_cell(cross_product / grand_totals[:, None], split_point, cells)
    final_result = (
        active_flags
        * (norm_gain_vector * cell_scale)
        * (upstream_gradient - upstream_average - normalized_values * cross_average)
    )
    return (final_result, jnp.sum(cross_product, axis=0), jnp.sum(running_sums, axis=0))


def reduce_weight(pairs, depth, width):
    total = jnp.zeros((depth // lax.axis_size("tm") * lax.axis_size("tm"), width), jnp.float32)
    for left, right in pairs:
        total = total + lax.dot_general(
            left, right, (((0,), (0,)), ((), ())), preferred_element_type=jnp.float32
        )
    shared = lax.psum_scatter(total.astype(jnp.bfloat16), "tm", scatter_dimension=0, tiled=True)
    return lax.psum_scatter(shared, "batch", scatter_dimension=1, tiled=True).astype(jnp.float32)


def own_square(shard):
    local = jnp.sum(shard * shard)
    return local


def adamw(weight, gradient, momentum, variance, factor, rate, decay):
    clipped = gradient * factor
    new_momentum = BETA_ONE * momentum + (1.0 - BETA_ONE) * clipped
    new_variance = BETA_TWO * variance + (1.0 - BETA_TWO) * clipped * clipped
    corrected = new_momentum / (1.0 - BETA_ONE**STEP)
    spread = jnp.sqrt(new_variance / (1.0 - BETA_TWO**STEP))
    new_weight = weight - rate * (corrected / (spread + ADAM_EPS) + decay * weight)
    return (new_weight, new_momentum, new_variance)


def plain_body(
    x_small,
    x_large,
    small_output_gradient,
    large_output_gradient,
    clip_counts,
    first_spatial,
    first_temporal,
    second_spatial,
    second_temporal,
    norm_params,
    first_spatial_momentum,
    first_temporal_momentum,
    second_spatial_momentum,
    second_temporal_momentum,
    norm_momentum,
    first_spatial_variance,
    first_temporal_variance,
    second_spatial_variance,
    second_temporal_variance,
    norm_variance,
):
    low_one = first_spatial.astype(jnp.bfloat16)
    low_two = first_temporal.astype(jnp.bfloat16)
    low_three = second_spatial.astype(jnp.bfloat16)
    low_four = second_temporal.astype(jnp.bfloat16)
    columns = (
        lax.all_gather(low_one, "batch", axis=1, tiled=True),
        lax.all_gather(low_two, "batch", axis=1, tiled=True),
        lax.all_gather(low_three, "batch", axis=1, tiled=True),
        lax.all_gather(low_four, "batch", axis=1, tiled=True),
    )
    spatial_one, temporal_one, spatial_two, temporal_two = (
        lax.all_gather(columns[0], "tm", axis=0, tiled=True),
        lax.all_gather(columns[1], "tm", axis=0, tiled=True),
        lax.all_gather(columns[2], "tm", axis=0, tiled=True),
        lax.all_gather(columns[3], "tm", axis=0, tiled=True),
    )
    clips = x_small.shape[0]
    split_point = x_small.shape[2]
    large_cells = x_large.shape[2]
    batch_index = lax.axis_index("batch")
    slots = jnp.arange(clips, dtype=jnp.int32)
    live_small = (slots < clip_counts[0, batch_index]).astype(jnp.float32)
    live_large = (slots < clip_counts[1, batch_index]).astype(jnp.float32)
    active_flags = jnp.concatenate(
        [
            jnp.broadcast_to(live_small[:, None, None, None], (clips, 1, split_point, 1)),
            jnp.broadcast_to(live_large[:, None, None, None], (clips, 1, large_cells, 1)),
        ],
        axis=2,
    )
    frames_total = x_small.shape[1] * lax.axis_size("tm")
    grand_totals = jnp.stack(
        [
            jnp.sum(clip_counts[0]).astype(jnp.float32) * frames_total * split_point,
            jnp.sum(clip_counts[1]).astype(jnp.float32) * frames_total * large_cells,
        ]
    )
    bounds = (0, MID, MID + D, 2 * MID + D, 2 * MID + 2 * D)
    gain_vectors = [norm_params[0, bounds[index] : bounds[index + 1]] for index in range(4)]
    bias_vectors = [norm_params[1, bounds[index] : bounds[index + 1]] for index in range(4)]
    first_convolved, taps_one_small, taps_one_large = spatial_forward(x_small, x_large, spatial_one)
    hidden_one, normed_one, scale_one = norm_forward_pass(
        first_convolved, active_flags, split_point, grand_totals, gain_vectors[0], bias_vectors[0]
    )
    act_one = jax.nn.silu(hidden_one).astype(jnp.bfloat16)
    second_convolved, rows_two = temporal_forward(act_one, temporal_one)
    hidden_two, normed_two, scale_two = norm_forward_pass(
        second_convolved, active_flags, split_point, grand_totals, gain_vectors[1], bias_vectors[1]
    )
    act_two = jax.nn.silu(hidden_two).astype(jnp.bfloat16)
    third_convolved, taps_three_small, taps_three_large = spatial_forward(
        act_two[:, :, :split_point], act_two[:, :, split_point:], spatial_two
    )
    hidden_three, normed_three, scale_three = norm_forward_pass(
        third_convolved, active_flags, split_point, grand_totals, gain_vectors[2], bias_vectors[2]
    )
    act_three = jax.nn.silu(hidden_three).astype(jnp.bfloat16)
    fourth_convolved, rows_four = temporal_forward(act_three, temporal_two)
    hidden_four, fourth_normalized, fourth_scale = norm_forward_pass(
        fourth_convolved, active_flags, split_point, grand_totals, gain_vectors[3], bias_vectors[3]
    )
    residual_in = jnp.concatenate([x_small, x_large], axis=2).astype(jnp.float32)
    output_preactivation = hidden_four + residual_in
    block_output = active_flags * jax.nn.silu(output_preactivation)
    upstream_gradient = (
        jnp.concatenate([small_output_gradient, large_output_gradient], axis=2).astype(jnp.float32)
        * active_flags
    )
    passed_gradient = upstream_gradient * silu_slope(output_preactivation)
    squared_values = []
    grad_conv_four, gain_four, bias_four = norm_reverse_pass(
        passed_gradient,
        fourth_normalized,
        fourth_scale,
        gain_vectors[3],
        active_flags,
        split_point,
        grand_totals,
    )
    grad_conv_four = grad_conv_four.astype(jnp.bfloat16)
    rows_grad_four = grad_conv_four.reshape(-1, grad_conv_four.shape[-1])
    grad_second_temporal = reduce_weight(
        [(rows_four, rows_grad_four)], rows_four.shape[1], rows_grad_four.shape[1]
    )
    squared_values.append(own_square(grad_second_temporal))
    grad_act_three = temporal_backward(grad_conv_four, temporal_two)
    grad_conv_three, gain_three, bias_three = norm_reverse_pass(
        grad_act_three * silu_slope(hidden_three),
        normed_three,
        scale_three,
        gain_vectors[2],
        active_flags,
        split_point,
        grand_totals,
    )
    grad_conv_three = grad_conv_three.astype(jnp.bfloat16)
    rows_three_small = grad_conv_three[:, :, :split_point].reshape(-1, grad_conv_three.shape[-1])
    rows_three_large = grad_conv_three[:, :, split_point:].reshape(-1, grad_conv_three.shape[-1])
    grad_second_spatial = reduce_weight(
        [(taps_three_small, rows_three_small), (taps_three_large, rows_three_large)],
        taps_three_small.shape[1],
        rows_three_small.shape[1],
    )
    squared_values.append(own_square(grad_second_spatial))
    channels_mid = act_two.shape[-1]
    grad_act_two = jnp.concatenate(
        [
            spatial_backward(
                rows_three_small,
                spatial_two,
                (clips, act_two.shape[1], split_point, channels_mid),
                HS,
            ),
            spatial_backward(
                rows_three_large,
                spatial_two,
                (clips, act_two.shape[1], large_cells, channels_mid),
                HL,
            ),
        ],
        axis=2,
    )
    grad_conv_two, gain_two, bias_two = norm_reverse_pass(
        grad_act_two * silu_slope(hidden_two),
        normed_two,
        scale_two,
        gain_vectors[1],
        active_flags,
        split_point,
        grand_totals,
    )
    grad_conv_two = grad_conv_two.astype(jnp.bfloat16)
    rows_grad_two = grad_conv_two.reshape(-1, grad_conv_two.shape[-1])
    grad_first_temporal = reduce_weight(
        [(rows_two, rows_grad_two)], rows_two.shape[1], rows_grad_two.shape[1]
    )
    squared_values.append(own_square(grad_first_temporal))
    grad_act_one = temporal_backward(grad_conv_two, temporal_one)
    grad_conv_one, gain_one, bias_one = norm_reverse_pass(
        grad_act_one * silu_slope(hidden_one),
        normed_one,
        scale_one,
        gain_vectors[0],
        active_flags,
        split_point,
        grand_totals,
    )
    grad_conv_one = grad_conv_one.astype(jnp.bfloat16)
    rows_one_small = grad_conv_one[:, :, :split_point].reshape(-1, grad_conv_one.shape[-1])
    rows_one_large = grad_conv_one[:, :, split_point:].reshape(-1, grad_conv_one.shape[-1])
    grad_first_spatial = reduce_weight(
        [(taps_one_small, rows_one_small), (taps_one_large, rows_one_large)],
        taps_one_small.shape[1],
        rows_one_small.shape[1],
    )
    squared_values.append(own_square(grad_first_spatial))
    input_small = passed_gradient[:, :, :split_point] + spatial_backward(
        rows_one_small, spatial_one, x_small.shape, HS
    )
    input_large = passed_gradient[:, :, split_point:] + spatial_backward(
        rows_one_large, spatial_one, x_large.shape, HL
    )
    grad_params = jnp.stack(
        [
            jnp.concatenate([gain_one, gain_two, gain_three, gain_four]),
            jnp.concatenate([bias_one, bias_two, bias_three, bias_four]),
        ]
    )
    summed = lax.psum(
        (squared_values[0], squared_values[1], squared_values[2], squared_values[3]),
        ("batch", "tm"),
    )
    weight_square = summed[0] + summed[1] + summed[2] + summed[3]
    grad_norm = jnp.sqrt(weight_square + jnp.sum(grad_params * grad_params))
    factor = THRESHOLD / jnp.maximum(grad_norm, THRESHOLD)
    one = adamw(
        first_spatial,
        grad_first_spatial,
        first_spatial_momentum,
        first_spatial_variance,
        factor,
        WEIGHT_RATE,
        WEIGHT_DECAY,
    )
    two = adamw(
        first_temporal,
        grad_first_temporal,
        first_temporal_momentum,
        first_temporal_variance,
        factor,
        WEIGHT_RATE,
        WEIGHT_DECAY,
    )
    three = adamw(
        second_spatial,
        grad_second_spatial,
        second_spatial_momentum,
        second_spatial_variance,
        factor,
        WEIGHT_RATE,
        WEIGHT_DECAY,
    )
    four = adamw(
        second_temporal,
        grad_second_temporal,
        second_temporal_momentum,
        second_temporal_variance,
        factor,
        WEIGHT_RATE,
        WEIGHT_DECAY,
    )
    norms = adamw(norm_params, grad_params, norm_momentum, norm_variance, factor, NORM_RATE, 0.0)
    return (
        block_output[:, :, :split_point],
        block_output[:, :, split_point:],
        input_small,
        input_large,
        grad_norm,
        one[0],
        one[1],
        one[2],
        two[0],
        two[1],
        two[2],
        three[0],
        three[1],
        three[2],
        four[0],
        four[1],
        four[2],
        norms[0],
        norms[1],
        norms[2],
    )


BF = jnp.bfloat16
F32 = jnp.float32
MESH_ID = pl.DeviceIdType.MESH
NT_DIMS = (((1,), (1,)), ((), ()))
NN_DIMS = (((1,), (0,)), ((), ()))
scope = lambda name: contextlib.nullcontext()
UP, DOWN, ACROSS, ALONG, TWIN = range(5)


class Place:
    def __init__(self, batches, slots):
        self.batches, self.slots = batches, slots
        self.z = lax.axis_index("batch")
        self.t = lax.axis_index("tm")
        self.core = lax.rem(self.t, 2)
        self.slab = self.t // 2
        self.slabs = slots // 2
        side = lax.rem(self.slab, 2)
        deep = self.slab // 2
        self.side_slab = deep * 2 + (1 - side)
        self.deep_slab = (1 - deep) * 2 + side
        self.far_slab = (1 - deep) * 2 + (1 - side)
        self.rel = (self.slab, self.side_slab, self.deep_slab, self.far_slab)
        self.twin = self.t + 1 - 2 * self.core

    def device(self, way):
        if way == UP:
            return (self.z + 1, self.t)
        if way == DOWN:
            return (self.z - 1, self.t)
        if way == ACROSS:
            return (self.z, self.side_slab * 2 + self.core)
        if way == ALONG:
            return (self.z, self.deep_slab * 2 + self.core)
        return (self.z, self.twin)

    def greet(self):
        barrier = pltpu.get_barrier_semaphore()
        for step in range(1, self.slots):
            pl.semaphore_signal(
                barrier, inc=1, device_id=(self.z, lax.rem(self.t + step, self.slots)),
                device_id_type=MESH_ID,
            )
        for step in range(1, self.batches):
            pl.semaphore_signal(
                barrier, inc=1, device_id=(lax.rem(self.z + step, self.batches), self.t),
                device_id_type=MESH_ID,
            )
        pl.semaphore_wait(barrier, self.slots + self.batches - 2)


def send(src, dst, send_sem, recv_sem, device):
    return pltpu.make_async_remote_copy(
        src_ref=src, dst_ref=dst, send_sem=send_sem, recv_sem=recv_sem,
        device_id=device, device_id_type=MESH_ID,
    )


class Totals:
    def __init__(self, place, rows, planes, lines, sems):
        self.p, self.rows, self.planes, self.lines = place, rows, planes, lines
        self.plane_send, self.plane_recv, self.line_send, self.line_recv = sems

    def plane_copy(self, n, step, width):
        p = self.p
        to = lax.rem(p.t + step, p.slots)
        ref = self.planes.at[n, p.t, :, pl.ds(0, width)]
        return send(ref, ref, self.plane_send.at[n, step], self.plane_recv.at[n, p.t], (p.z, to))

    def line_copy(self, n, step, width):
        p = self.p
        to = lax.rem(p.z + step, p.batches)
        ref = self.lines.at[n, p.z, :, pl.ds(0, width)]
        return send(ref, ref, self.line_send.at[n, step], self.line_recv.at[n, p.z], (to, p.t))

    def run(self, n, value, first=None, second=None):
        p = self.p
        width = value.shape[1]
        plane, line = self.planes.at[n], self.lines.at[n]
        plane[p.t, :, :width] = value
        for step in range(1, p.slots):
            self.plane_copy(n, step, width).start()
        if first is not None:
            first()
        for step in range(1, p.slots):
            origin = lax.rem(p.t + p.slots - step, p.slots)
            ref = plane.at[origin, :, pl.ds(0, width)]
            send(ref, ref, self.plane_send.at[n, step], self.plane_recv.at[n, origin],
                 (p.z, p.twin)).wait_recv()
        total = plane[0, :, :width]
        for slot in range(1, p.slots):
            total = total + plane[slot, :, :width]
        line[p.z, :, :width] = total
        for step in range(1, p.batches):
            self.line_copy(n, step, width).start()
        if second is not None:
            second()
        for step in range(1, p.batches):
            origin = lax.rem(p.z + p.batches - step, p.batches)
            ref = line.at[origin, :, pl.ds(0, width)]
            send(ref, ref, self.line_send.at[n, step], self.line_recv.at[n, origin],
                 (p.z, p.twin)).wait_recv()
        total = line[0, :, :width]
        for slot in range(1, p.batches):
            total = total + line[slot, :, :width]
        for step in range(1, p.slots):
            self.plane_copy(n, step, width).wait_send()
        for step in range(1, p.batches):
            self.line_copy(n, step, width).wait_send()
        return total


class Gather:
    def __init__(self, place, index, own, whole, block, sems):
        self.p, self.n, self.own, self.whole, self.block = place, index, own, whole, block
        self.send_sem, self.recv_sem, self.twin_sem = sems

    def copy(self, way, rel, batch, src=None):
        p = self.p
        core = p.core
        dst = self.whole.at[self.block(p.rel[rel], core, batch)]
        there = {ACROSS: {0: 1, 2: 3}, ALONG: {0: 2, 1: 3}}.get(way, {}).get(rel, rel)
        sem = self.twin_sem if way == TWIN else self.recv_sem
        return send(
            dst if src is None else src, dst, self.send_sem.at[self.n, way, rel, batch],
            sem.at[self.n, there, batch], p.device(way),
        )

    def wait(self, rel, batch, twin=False):
        p = self.p
        core = 1 - p.core if twin else p.core
        ref = self.whole.at[self.block(p.rel[rel], core, batch)]
        sem = self.twin_sem if twin else self.recv_sem
        send(ref, ref, self.send_sem.at[self.n, TWIN, rel, batch], sem.at[self.n, rel, batch],
             p.device(TWIN)).wait_recv()

    def at(self, k, fn):
        p = self.p
        if k == 0:
            fn(p.z)
            return
        pl.when(p.z - k >= 0)(lambda: fn(p.z - k))
        pl.when(p.z + k < p.batches)(lambda: fn(p.z + k))

    def start_line(self):
        p = self.p
        pl.when(p.z < p.batches - 1)(lambda: self.copy(UP, 0, p.z, self.own).start())
        pl.when(p.z > 0)(lambda: self.copy(DOWN, 0, p.z, self.own).start())
        self.copy(TWIN, 0, p.z, self.own).start()

    def start_plane(self):
        for way in (ACROSS, ALONG):
            self.copy(way, 0, self.p.z, self.own).start()

    def hop(self, k):
        p = self.p

        def below(b):
            self.wait(0, b)
            pl.when(p.z < p.batches - 1)(lambda: self.copy(UP, 0, b).start())
            self.copy(TWIN, 0, b).start()

        def above(b):
            self.wait(0, b)
            pl.when(p.z > 0)(lambda: self.copy(DOWN, 0, b).start())
            self.copy(TWIN, 0, b).start()

        pl.when(p.z - k >= 0)(lambda: below(p.z - k))
        pl.when(p.z + k < p.batches)(lambda: above(p.z + k))

    def spread(self, k, ways=(ACROSS, ALONG)):
        def one(b):
            for way in ways:
                self.copy(way, 0, b).start()

        self.at(k, one)

    def across(self, k):
        self.spread(k, (ACROSS,))

    def along(self, k):
        self.spread(k, (ALONG,))

    def from_side(self, k):
        half = self.p.batches // 2

        def one(b):
            self.wait(1, b)
            pl.when(b < half)(lambda: self.copy(ALONG, 1, b).start())
            self.copy(TWIN, 1, b).start()

        self.at(k, one)

    def from_deep(self, k):
        half = self.p.batches // 2

        def one(b):
            self.wait(2, b)
            pl.when(b >= half)(lambda: self.copy(ACROSS, 2, b).start())
            self.copy(TWIN, 2, b).start()

        self.at(k, one)

    def plane(self, k):
        self.from_side(k)
        self.from_deep(k)

    def far(self, k):
        def one(b):
            self.wait(3, b)
            self.copy(TWIN, 3, b).start()

        self.at(k, one)

    def twins(self, rel):
        def body(b, _):
            self.wait(rel, b, twin=True)
            return 0

        lax.fori_loop(0, self.p.batches, body, 0)

    def act(self, word):
        kind = word[0]
        if kind == "z":
            self.start_line()
        elif kind == "x":
            self.start_plane()
        else:
            {"h": self.hop, "s": self.spread, "a": self.across, "l": self.along, "p": self.plane, "f": self.far,
             "u": self.from_side, "v": self.from_deep}[kind](int(word[1]))

    def finish(self):
        p = self.p
        half = p.batches // 2

        def body(b, _):
            pl.when((b <= p.z) & (p.z < p.batches - 1))(lambda: self.copy(UP, 0, b, self.own).wait_send())
            pl.when((b >= p.z) & (p.z > 0))(lambda: self.copy(DOWN, 0, b, self.own).wait_send())
            for way in (ACROSS, ALONG):
                self.copy(way, 0, b, self.own).wait_send()
            for rel in range(4):
                self.copy(TWIN, rel, b, self.own).wait_send()
            pl.when(b < half)(lambda: self.copy(ALONG, 1, b, self.own).wait_send())
            pl.when(b >= half)(lambda: self.copy(ACROSS, 2, b, self.own).wait_send())
            return 0

        lax.fori_loop(0, p.batches, body, 0)


class FarLineGather(Gather):
    def line(self, rel, b, up=True, down=True):
        p = self.p
        if up:
            pl.when(p.z < p.batches - 1)(lambda: self.copy(UP, rel, b).start())
        if down:
            pl.when(p.z > 0)(lambda: self.copy(DOWN, rel, b).start())

    def side_own(self):
        z = self.p.z
        self.wait(1, z)
        self.copy(ALONG, 1, z).start()
        self.copy(TWIN, 1, z).start()

    def far_own(self):
        z = self.p.z
        self.wait(3, z)
        self.copy(TWIN, 3, z).start()
        self.line(3, z)

    def far_hop(self, k):
        p = self.p

        def below(b):
            self.wait(3, b)
            self.line(3, b, down=False)
            self.copy(TWIN, 3, b).start()

        def above(b):
            self.wait(3, b)
            self.line(3, b, up=False)
            self.copy(TWIN, 3, b).start()

        pl.when(p.z - k >= 0)(lambda: below(p.z - k))
        pl.when(p.z + k < p.batches)(lambda: above(p.z + k))

    def from_side(self, k):
        def one(b):
            self.wait(1, b)
            self.copy(TWIN, 1, b).start()

        self.at(k, one)

    def from_deep(self, k):
        def one(b):
            self.wait(2, b)
            self.copy(TWIN, 2, b).start()

        self.at(k, one)

    def act(self, word):
        if word == "c":
            self.side_own()
        elif word == "d":
            self.far_own()
        elif word[0] == "g":
            self.far_hop(int(word[1]))
        else:
            super().act(word)

    def finish(self):
        p = self.p
        self.copy(ALONG, 1, p.z, self.own).wait_send()

        def body(b, _):
            for rel in (0, 3):
                pl.when((b <= p.z) & (p.z < p.batches - 1))(
                    lambda: self.copy(UP, rel, b, self.own).wait_send())
                pl.when((b >= p.z) & (p.z > 0))(lambda: self.copy(DOWN, rel, b, self.own).wait_send())
            for way in (ACROSS, ALONG):
                self.copy(way, 0, b, self.own).wait_send()
            for rel in range(4):
                self.copy(TWIN, rel, b, self.own).wait_send()
            return 0

        lax.fori_loop(0, p.batches, body, 0)


class Halo:
    def __init__(self, place, stage, src, dst, relay, sems, cut):
        self.p, self.n, self.src, self.dst, self.buf, self.cut = place, stage, src, dst, relay, cut
        self.send_sem, self.recv_sem, self.pass_send, self.pass_recv = sems
        self.mid = place.slots // 2

    def part(self, ref, piece):
        rows = ref.shape[0]
        return ref.at[pl.ds(0, self.cut)] if piece == 0 else ref.at[pl.ds(self.cut, rows - self.cut)]

    def piece(self, side, piece, to):
        return send(self.part(self.src(side), piece), self.part(self.dst(side), piece),
                    self.send_sem.at[self.n, side, piece], self.recv_sem.at[self.n, side, piece],
                    (self.p.z, to))

    def detour(self, side):
        to = self.p.slots - 1 if side == 0 else 0
        return send(self.part(self.src(side), 1), self.buf, self.send_sem.at[self.n, side, 1],
                    self.pass_recv.at[self.n], (self.p.z, to))

    def passing(self, side):
        to = self.mid if side == 0 else self.mid - 1
        return send(self.buf, self.part(self.dst(side), 1), self.pass_send.at[self.n],
                    self.recv_sem.at[self.n, side, 1], (self.p.z, to))

    def sends(self, side):
        return self.p.t < self.p.slots - 1 if side == 0 else self.p.t > 0

    def receives(self, side):
        return self.p.t > 0 if side == 0 else self.p.t < self.p.slots - 1

    def start(self, side):
        p = self.p
        to = p.t + 1 if side == 0 else p.t - 1
        crossing = p.t == (self.mid - 1 if side == 0 else self.mid)

        @pl.when(self.sends(side))
        def _():
            pl.when(crossing)(lambda: self.detour(side).start())
            self.piece(side, 0, to).start()
            pl.when(jnp.logical_not(crossing))(lambda: self.piece(side, 1, to).start())

    def relay(self):
        p = self.p
        for side, t in ((0, p.slots - 1), (1, 0)):
            @pl.when(p.t == t)
            def _(side=side):
                send(self.buf, self.buf, self.pass_send.at[self.n], self.pass_recv.at[self.n],
                     p.device(TWIN)).wait_recv()
                self.passing(side).start()

    def wait(self, side):
        @pl.when(self.receives(side))
        def _():
            for piece in range(2):
                self.piece(side, piece, self.p.twin).wait_recv()

    def done(self):
        p = self.p
        for side in range(2):
            @pl.when(self.sends(side))
            def _(side=side):
                for piece in range(2):
                    self.piece(side, piece, p.twin).wait_send()
        for side, t in ((0, p.slots - 1), (1, 0)):
            pl.when(p.t == t)(lambda side=side: self.passing(side).wait_send())


def sigmoid(v):
    return 0.5 * jnp.tanh(0.5 * v) + 0.5


class Shape:
    def __init__(self, x_small, x_large, batches, slots):
        self.clips = x_small[0]
        self.cells = (x_small[2], x_large[2])
        self.sides = (math.isqrt(x_small[2]), math.isqrt(x_large[2]))
        self.d = x_small[3]
        self.padded = tuple(n + n % 2 for n in self.cells)
        self.rows = tuple(n * self.clips for n in self.padded)
        self.m = sum(self.rows)
        self.mid = MID
        self.k = 9 * self.d
        self.batches, self.slots = batches, slots
        self.slabs = slots // 2
        self.kw = self.k // self.slabs
        self.nb = self.mid // (2 * batches)
        self.ur = 3 * self.mid // slots
        self.uc = self.d // batches
        self.cut = -(-self.m // 32) * 16


def fits(x_small, x_large, batches, slots):
    s = Shape(x_small, x_large, batches, slots)
    return (
        s.clips == 8 and x_small[1] == 1 and slots == 8 and batches == 4
        and all(side * side == cells for side, cells in zip(s.sides, s.cells))
        and all(r % 80 == 0 for r in s.rows)
        and s.kw % 128 == 0 and s.mid % (32 * batches) == 0 and s.ur % 16 == 0 and s.uc % 128 == 0
    )


def chunks(s, size, fn, carry=None, unroll=1):
    out = []
    base = 0
    for group, rows in enumerate(s.rows):
        def body(i, c, group=group, base=base):
            return fn(group, pl.multiple_of(base + i * size, size if base % size == 0 else 16), c)

        out.append(lax.fori_loop(0, rows // size, body, carry if carry is not None else 0, unroll=unroll))
        base += rows
    return out


def sums_of(s, load, live, width):
    def body(group, r0, c):
        values = load(group, r0, 80)
        return tuple(t + jnp.sum(v.reshape(10, 8, width), axis=0) for t, v in zip(c, values))

    zero = jnp.zeros((8, width), F32)
    small, large = chunks(s, 80, body, (zero, zero))
    rows = [jnp.sum(v * live[g], axis=0, keepdims=True) for v, g in
            ((small[0], 0), (large[0], 1), (small[1], 0), (large[1], 1))]
    return jnp.concatenate(rows, axis=0)


def build_taps(s, grids, taps):
    pieces = []
    for tap in range(9):
        lo = tap * s.d
        end = lo + s.d
        while lo < end:
            hi = min(end, (lo // s.kw + 1) * s.kw)
            pieces.append((tap, lo - tap * s.d, lo // s.kw, lo % s.kw, hi - lo))
            lo = hi
    base = 0
    for group in range(2):
        side, cells = s.sides[group], s.cells[group]
        grid = grids[group]
        for tap, channel, slab, lane, width in pieces:
            i, j = tap // 3, tap % 3
            if side % 2 == 0:
                n = 2 * side * 8

                def body(r, _):
                    window = grid[pl.ds(i + 2 * r, 2), j : j + side, :, channel : channel + width]
                    taps[slab, pl.ds(pl.multiple_of(base + r * n, 16), n), lane : lane + width] = (
                        window.reshape(n, width).astype(BF)
                    )
                    return 0

                lax.fori_loop(0, side // 2, body, 0)
            else:
                window = grid[i : i + side, j : j + side, :, channel : channel + width]
                window = window.reshape(cells * 8, width)
                window = jnp.concatenate(
                    [window, jnp.zeros((s.rows[group] - cells * 8, width), F32)], axis=0
                ) if s.rows[group] > cells * 8 else window
                taps[slab, base : base + s.rows[group], lane : lane + width] = window.astype(BF)
        base += s.rows[group]


def fill_grid(s, grids, group, cell, value):
    side = s.sides[group]
    grids[group][1 + cell // side, 1 + lax.rem(cell, side)] = value


def zero_padding(s, ref, width):
    base = 0
    for group in range(2):
        base += s.rows[group]
        spare = (s.padded[group] - s.cells[group]) * s.clips
        if spare:
            size = -(-spare // 16) * 16
            keep = lax.broadcasted_iota(jnp.int32, (size, width), 0) < size - spare
            value = ref[base - size : base, :].astype(F32)
            ref[base - size : base, :] = jnp.where(keep, value, 0.0).astype(ref.dtype)


def grid_of_rows(s, grids, group, r0, value):
    side = s.sides[group]
    base = 0 if group == 0 else s.rows[0]
    first = (r0 - base) // 8
    split = value.reshape(10, 8, s.d)
    for n in range(10):
        cell = first + n
        grids[group][1 + cell // side, 1 + lax.rem(cell, side)] = split[n]


def clear_pad_cells(s, grids):
    for group in range(2):
        side = s.sides[group]
        for cell in range(s.cells[group], s.padded[group]):
            grids[group][1 + cell // side, 1 + cell % side] = jnp.zeros((8, s.d), F32)


def moments(total, inverse, width):
    mean = [total[g : g + 1, :] * inverse[g] for g in range(2)]
    scale = [
        lax.rsqrt(total[2 + g : 3 + g, :] * inverse[g] - mean[g] * mean[g] + NORM_EPS) for g in range(2)
    ]
    return mean, scale


def wide_cuts(width):
    half = -(-width // 256) * 128
    return ((0, half), (half, width - half))


def forward_kernel(s, *refs):
    (x, grad, sw1, uw1, sw2, uw2, norm, live_ref, inverse,
     gs1, gu1, gs2, gu2, taps1_o, taps2_o, xh1_o, xh2_o, xh3_o, xh4_o, z1_o, z3_o, out_o, dpre_o,
     r1_o, r2_o, r3_o, r4_o, last_o,
     tb1, tb2, own1, own2, wb, wub, taps, a, z, grid_s, grid_l, b, hs, hr, planes, lines,
     ag_send, ag_recv, ag_twin, tb_send, tb_recv, local, load, hs_send, hs_recv, pass_send, pass_recv, relay, out, dpre,
     pl_send, pl_recv, ln_send, ln_recv) = refs
    p = Place(s.batches, s.slots)
    live = [live_ref[g] for g in range(2)]
    inv = [inverse[g] for g in range(2)]
    totals = Totals(p, 4, planes, lines, (pl_send, pl_recv, ln_send, ln_recv))
    d, mid = s.d, s.mid
    bounds = (0, mid, mid + d, 2 * mid + d, 2 * mid + 2 * d)

    def gain_bias(n):
        return norm[0:1, bounds[n] : bounds[n + 1]], norm[1:2, bounds[n] : bounds[n + 1]]

    with scope("greet"):
        p.greet()

    def twin_copy(n, src, dst):
        return send(
            src.at[1 - p.core], dst.at[pl.ds(pl.multiple_of(p.core * (s.kw // 2), 16), s.kw // 2)],
            tb_send.at[n], tb_recv.at[n], p.device(TWIN),
        )

    def twin_wait(n, src, dst):
        send(
            src.at[1 - p.core], dst.at[pl.ds(pl.multiple_of((1 - p.core) * (s.kw // 2), 16), s.kw // 2)],
            tb_send.at[n], tb_recv.at[n], p.device(TWIN),
        ).wait_recv()

    for n, src, dst in ((0, sw1, tb1), (1, sw2, tb2)):
        twin_copy(n, src, dst).start()
        dst[pl.ds(pl.multiple_of(p.core * (s.kw // 2), 16), s.kw // 2)] = src[p.core]

    def s_block(slab, core, batch):
        return (slab, pl.ds(pl.multiple_of((batch * 2 + core) * s.nb, 16), s.nb))

    def u_block(slab, core, batch):
        return (pl.ds(pl.multiple_of((slab * 2 + core) * s.ur, 16), s.ur),
                pl.ds(pl.multiple_of(batch * s.uc, 128), s.uc))

    sems = (ag_send, ag_recv, ag_twin)
    gather = [
        Gather(p, 0, own1, gs1, s_block, sems),
        Gather(p, 1, uw1, gu1, u_block, sems),
        FarLineGather(p, 2, own2, gs2, s_block, sems),
        Gather(p, 3, uw2, gu2, u_block, sems),
    ]

    def keep_own(n):
        g = gather[n]
        return pltpu.make_async_copy(g.own, g.whole.at[g.block(p.slab, p.core, p.z)], local.at[n])

    def go(words):
        with scope("gather " + words):
            for word in words.split():
                gather[int(word[0])].act(word[1:])

    with scope("own"):
        twin_wait(0, sw1, tb1)
        own1[...] = tb1[...].T
        go("0z 0x")
        keep_own(0).start()
        twin_wait(1, sw2, tb2)
        own2[...] = tb2[...].T
    keep_own(1).start()
    keep_own(2).start()
    keep_own(3).start()
    for side, edge in ((0, 0), (1, p.slots - 1)):
        @pl.when(p.t == edge)
        def _(side=side):
            hr[side] = jnp.zeros(hr.shape[1:], BF)

    grids = (grid_s, grid_l)
    for grid in grids:
        def clear(i, _, grid=grid):
            grid[i] = jnp.zeros(grid.shape[1:], F32)
            return 0

        lax.fori_loop(0, grid.shape[0], clear, 0)

    def x_rows(group, r0, c):
        grid_of_rows(s, grids, group, r0, x[pl.ds(r0, 80), :].astype(F32))
        return c

    with scope("taps x"):
        chunks(s, 80, x_rows)
        clear_pad_cells(s, grids)
        build_taps(s, grids, taps)
    taps_copy = pltpu.make_async_copy(taps, taps1_o, local.at[4])
    taps_copy.start()

    def slab_load(whole, rel, half):
        lo, width = wide_cuts(mid)[half]
        rows = pl.ds(lo, width)
        return pltpu.make_async_copy(whole.at[p.rel[rel], rows], wb.at[rel, rows], load.at[rel, half])

    def conv_slab(whole, rel, first):
        for half, (lo, width) in enumerate(wide_cuts(mid)):
            slab_load(whole, rel, half).wait()
            y = lax.dot_general(taps[p.rel[rel]], wb[rel, lo : lo + width, :], NT_DIMS, preferred_element_type=F32)
            if first:
                a[:, lo : lo + width] = y
            else:
                a[:, lo : lo + width] += y

    def spatial(n, whole, order, words):
        g = gather[n]
        keep_own(n).wait()
        for i, rel in enumerate(order):
            go(words[2 * i])
            with scope("twins"):
                g.twins(rel)
            for half in range(2):
                slab_load(whole, rel, half).start()
            go(words[2 * i + 1])
            with scope("slab"):
                conv_slab(whole, rel, i == 0)

    def stats(load_rows, width):
        return sums_of(s, load_rows, live, width)

    def wide_norm(index, n, zo, xo, ro, sem, words, weight):
        def load_rows(group, r0, size):
            v = a[pl.ds(r0, size), :]
            return v, v * v

        with scope("wide stats"):
            local_sums = stats(load_rows, mid)
        go(words[0])
        with scope("total"):
            total = totals.run(index, local_sums)
        weight_load(*weight)
        go(words[1])
        mean, scale = moments(total, inv, mid)
        ro[...] = jnp.concatenate(scale, axis=0)
        gain, bias = gain_bias(n)

        def rows(group, r0, c):
            xhat = (a[pl.ds(r0, 16), :] - mean[group]) * scale[group]
            a[pl.ds(r0, 16), :] = xhat
            h = xhat * gain + bias
            z[pl.ds(r0, 16), :] = (h * sigmoid(h)).astype(BF)
            return c

        with scope("wide norm"):
            chunks(s, 16, rows)
        zero_padding(s, z, mid)
        xc = pltpu.make_async_copy(a, xo, local.at[sem])
        zc = pltpu.make_async_copy(z, zo, local.at[sem + 1])
        xc.start()
        zc.start()
        return xc, zc

    def u_load(n, whole):
        return pltpu.make_async_copy(whole, wub, load.at[4, n])

    halos = [
        Halo(p, n, lambda side: hs.at[side], lambda side: hr.at[side], relay,
             (hs_send, hs_recv, pass_send, pass_recv), s.cut)
        for n in range(2)
    ]

    def weight_load(n, index):
        with scope("u weight"):
            for rel in range(4):
                gather[index].twins(rel)
            keep_own(index).wait()
            u_load(n, gather[index].whole).start()

    def temporal(n, words):
        with scope("u conv"):
            u_load(n, gather[1].whole).wait()
            hs[0] = jnp.dot(z[...], wub[:mid, :], preferred_element_type=F32).astype(BF)
            halos[n].start(0)
            hs[1] = jnp.dot(z[...], wub[2 * mid :, :], preferred_element_type=F32).astype(BF)
            halos[n].start(1)
            b[...] = jnp.dot(z[...], wub[mid : 2 * mid, :], preferred_element_type=F32)
        go(words[0])
        with scope("relay"):
            halos[n].relay()
        go(words[1])
        with scope("halo wait"):
            halos[n].wait(0)
            halos[n].wait(1)

    def narrow_total(index):
        def load_rows(group, r0, size):
            v = b[pl.ds(r0, size), :] + hr[0, pl.ds(r0, size), :].astype(F32) + hr[1, pl.ds(r0, size), :].astype(F32)
            b[pl.ds(r0, size), :] = v
            return v, v * v

        with scope("narrow stats"):
            local_sums = stats(load_rows, d)
        with scope("total"):
            return totals.run(index, local_sums)

    go("0h1 0s1 0p0 0h2 0s2 0p1 0f0 0h3 0s3 1z")
    spatial(0, gs1, (0, 1, 2, 3), ("", "", "0p2 0f1 1h1 0p3 1h2", "1x 1s1 1h3 1s2 1s3", "0f2", "1p0", "0f3 1p1 1f0", "2z"))
    xc1, zc1 = wide_norm(0, 0, z1_o, xh1_o, r1_o, 5, ("1p2 1f1 1p3 1f2 1f3", "2x 2h1 3z"), (0, 1))
    temporal(0, ("2c", "2d 2h2"))
    total = narrow_total(1)
    go("2a1 2l1 2a2 2l2 2g1 2h3 2a3 2l3 3h1")
    mean2, scale2 = moments(total, inv, d)
    r2_o[...] = jnp.concatenate(scale2, axis=0)
    gain2, bias2 = gain_bias(1)

    def second(group, r0, c):
        xhat = (b[pl.ds(r0, 80), :] - mean2[group]) * scale2[group]
        b[pl.ds(r0, 80), :] = xhat
        h = xhat * gain2 + bias2
        grid_of_rows(s, grids, group, r0, (h * sigmoid(h)).astype(BF).astype(F32))
        return c

    with scope("norm2"):
        chunks(s, 80, second)
        clear_pad_cells(s, grids)
    xc2 = pltpu.make_async_copy(b, xh2_o, local.at[7])
    xc2.start()
    halos[0].done()
    go("2g2 3h2")
    taps_copy.wait()
    with scope("taps z2"):
        build_taps(s, grids, taps)
    taps_copy2 = pltpu.make_async_copy(taps, taps2_o, local.at[8])
    taps_copy2.start()
    xc1.wait()
    spatial(2, gs2, (0, 2, 3, 1), ("", "", "2v0 2v1 2v2 2v3", "2g3 3h3 3x 3s1 3s2 3s3", "", "2u1 2u2 2u3 3p0",
                                   "", "3p1 3f0 3p2 3f1"))
    zc1.wait()
    xc3, zc3 = wide_norm(2, 2, z3_o, xh3_o, r3_o, 9, ("3p3 3f2 3f3", ""), (1, 3))
    xc2.wait()
    temporal(1, ("", ""))
    total = narrow_total(3)
    mean4, scale4 = moments(total, inv, d)
    r4_o[...] = jnp.concatenate(scale4, axis=0)
    gain4, bias4 = gain_bias(3)

    def last(group, r0, c):
        xhat = (b[pl.ds(r0, 80), :] - mean4[group]) * scale4[group]
        b[pl.ds(r0, 80), :] = xhat
        pre = xhat * gain4 + bias4 + x[pl.ds(r0, 80), :].astype(F32)
        gate = sigmoid(pre)
        alive = jnp.broadcast_to(live[group][None], (10, 8, d)).reshape(80, d)
        out[pl.ds(r0, 80), :] = alive * (pre * gate)
        up = alive * grad[pl.ds(r0, 80), :].astype(F32) * (gate * (1.0 + pre * (1.0 - gate)))
        dpre[pl.ds(r0, 80), :] = up
        return c

    with scope("norm4"):
        chunks(s, 80, last)
        zero_padding(s, dpre, d)
    xc4 = pltpu.make_async_copy(b, xh4_o, local.at[11])
    xc4.start()
    outs = [pltpu.make_async_copy(out, out_o, local.at[12]), pltpu.make_async_copy(dpre, dpre_o, local.at[13])]
    for c in outs:
        c.start()

    def last_rows(group, r0, size):
        v = dpre[pl.ds(r0, size), :]
        return v, v * b[pl.ds(r0, size), :]

    with scope("last stats"):
        local_sums = stats(last_rows, d)
    with scope("total"):
        last_o[...] = totals.run(4, local_sums)
    halos[1].done()
    with scope("finish"):
        for g in gather:
            g.finish()
    for n, src, dst in ((0, sw1, tb1), (1, sw2, tb2)):
        twin_copy(n, src, dst).wait_send()
    for c in (taps_copy2, zc3, xc3, xc4, *outs):
        c.wait()


def forward_call(s, x, grad, sw1, uw1, sw2, uw2, norm, live, inverse):
    any_, vmem, smem = (pl.BlockSpec(memory_space=m) for m in (pl.ANY, pltpu.VMEM, pltpu.SMEM))
    S = jax.ShapeDtypeStruct
    m, d, mid = s.m, s.d, s.mid
    gs = S((s.slabs, mid, s.kw), BF)
    gu = S((3 * mid, d), BF)
    taps = S((s.slabs, m, s.kw), BF)
    wide, narrow = S((m, mid), F32), S((m, d), F32)
    zs = S((m, mid), BF)
    outs = (gs, gu, gs, gu, taps, taps, wide, narrow, wide, narrow, zs, zs, narrow, narrow,
            S((2, mid), F32), S((2, d), F32), S((2, mid), F32), S((2, d), F32), S((4, d), F32))
    specs = (any_,) * 14 + (vmem,) * 5
    dma, V = pltpu.SemaphoreType.DMA, pltpu.VMEM
    nb = s.batches
    n_sums = 5
    scratch = [
        V((s.kw, s.nb), BF), V((s.kw, s.nb), BF), V((s.nb, s.kw), BF), V((s.nb, s.kw), BF),
        V((s.slabs, mid, s.kw), BF), V((3 * mid, d), BF), V((s.slabs, m, s.kw), BF),
        V((m, mid), F32), V((m, mid), BF),
        V((s.sides[0] + 2, s.sides[0] + 2, 8, d), F32), V((s.sides[1] + 2, s.sides[1] + 2, 8, d), F32),
        V((m, d), F32), V((2, m, d), BF), V((2, m, d), BF),
        V((n_sums, s.slots, 4, mid), F32), V((n_sums, nb, 4, mid), F32),
        dma((4, 5, 4, nb)), dma((4, 4, nb)), dma((4, 4, nb)), dma((2,)), dma((2,)), dma((14,)), dma((5, 2)),
        dma((2, 2, 2)), dma((2, 2, 2)), dma((2,)), dma((2,)), V((m - s.cut, d), BF),
        V((m, d), F32), V((m, d), F32),
        dma((n_sums, s.slots)), dma((n_sums, s.slots)), dma((n_sums, nb)), dma((n_sums, nb)),
    ]
    return pl.pallas_call(
        functools.partial(forward_kernel, s),
        out_shape=outs,
        in_specs=[vmem, vmem, vmem, any_, vmem, any_, vmem, vmem, smem],
        out_specs=specs,
        scratch_shapes=scratch,
        compiler_params=pltpu.CompilerParams(
            collective_id=0, has_side_effects=True, vmem_limit_bytes=63 * 2**20
        ),
        name="forward",
    )(x, grad, sw1, uw1, sw2, uw2, norm, live, inverse)


def cell_major(s, small, large):
    parts = []
    for group, v in enumerate((small, large)):
        v = v.reshape(s.clips, s.cells[group], s.d).transpose(1, 0, 2)
        parts.append(jnp.pad(v, ((0, s.padded[group] - s.cells[group]), (0, 0), (0, 0))))
    return jnp.concatenate(parts, axis=0).reshape(s.m, s.d)


def clip_major(s, v):
    v = v.reshape(-1, s.clips, s.d)
    parts, base = [], 0
    for group in range(2):
        part = v[base : base + s.cells[group]].transpose(1, 0, 2)
        parts.append(part.reshape(s.clips, 1, s.cells[group], s.d))
        base += s.padded[group]
    return parts


def halves(s, w):
    return w.astype(BF).reshape(w.shape[0], 2, s.nb).transpose(1, 0, 2)


def add_into(dst, src, rows, step):
    def body(i, _):
        at = pl.ds(pl.multiple_of(i * step, 16), step)
        dst[at, :] = (dst[at, :].astype(F32) + src[at, :].astype(F32)).astype(BF)
        return 0

    lax.fori_loop(0, rows // step, body, 0)


class Scatter:
    def __init__(self, place, index, part, bufs, cut, rows, step, sems):
        self.p, self.n, self.part, self.cut, self.rows, self.step = place, index, part, cut, rows, step
        self.tr, self.fx, self.fa, self.rx, self.ry, self.ru, self.rd = bufs[:7]
        self.twin_s, self.twin_r, self.block_s, self.block_r = sems
        self.half = place.batches // 2

    FAR, SIDE, DEEP, RISE, FALL = range(5)

    def twin_copy(self, rel):
        p = self.p
        return send(self.part(rel, 1 - p.core), self.tr.at[rel], self.twin_s.at[self.n, rel],
                    self.twin_r.at[self.n, rel], p.device(TWIN))

    def block_copy(self, kind, b, src, dst, way):
        return send(src, dst, self.block_s.at[self.n, kind, b], self.block_r.at[self.n, kind, b],
                    self.p.device(way))

    def own(self, rel, b):
        return self.cut(self.part(rel, self.p.core), b)

    def far_copy(self, b):
        if b < self.half:
            return self.block_copy(self.FAR, b, self.own(3, b), self.cut(self.fx, b), ACROSS)
        return self.block_copy(self.FAR, b, self.own(3, b), self.cut(self.fa, b - self.half), ALONG)

    def side_copy(self, b):
        return self.block_copy(self.SIDE, b, self.own(1, b), self.cut(self.rx, b), ACROSS)

    def deep_copy(self, b):
        return self.block_copy(self.DEEP, b, self.own(2, b), self.cut(self.ry, b), ALONG)

    def rise_copy(self, b):
        return self.block_copy(self.RISE, b, self.own(0, b), self.cut(self.ru, b + 1), UP)

    def fall_copy(self, b):
        return self.block_copy(self.FALL, b, self.own(0, b), self.cut(self.ru, b), DOWN)

    def arrive(self, kind, b, ref):
        self.block_copy(kind, b, ref, ref, TWIN).wait_recv()

    def add(self, dst, src):
        add_into(dst, src, self.rows, self.step)

    def order(self):
        n = self.p.batches
        out = []
        for i in range(n // 2):
            out += [n - 1 - i, i]
        return out

    def twin(self, rel):
        self.twin_copy(rel).start()

    def join(self, rel):
        p = self.p
        self.twin_copy(rel).wait_recv()
        for b in self.order():
            self.add(self.own(rel, b), self.cut(self.tr.at[rel], b))
            if rel == 3:
                self.far_copy(b).start()
            if rel == 1 and b < self.half:
                self.side_copy(b).start()
            if rel == 2 and b >= self.half:
                self.deep_copy(b).start()

    def relay(self, b):
        if b < self.half:
            src = self.cut(self.fx, b)
            self.arrive(self.FAR, b, src)
            self.add(self.own(2, b), src)
            self.deep_copy(b).start()
        else:
            src = self.cut(self.fa, b - self.half)
            self.arrive(self.FAR, b, src)
            self.add(self.own(1, b), src)
            self.side_copy(b).start()

    def collect(self, b):
        for kind, buf in ((self.SIDE, self.rx), (self.DEEP, self.ry)):
            src = self.cut(buf, b)
            self.arrive(kind, b, src)
            self.add(self.own(0, b), src)

    def gather_own(self):
        p = self.p
        n = p.batches

        @pl.when(p.z < self.half)
        def _():
            for b in range(n - 1, -1, -1):
                self.collect(b)
                if b:
                    pl.when(p.z == 0)(lambda b=b: self.rise_copy(b).start())

        @pl.when(p.z >= self.half)
        def _():
            for b in range(n):
                self.collect(b)
                if b < n - 1:
                    pl.when(p.z == n - 1)(lambda b=b: self.fall_copy(b).start())

    def chain(self, stage):
        p = self.p

        @pl.when(p.z == stage)
        def _():
            for b in range(p.batches - 1, stage, -1):
                src = self.cut(self.ru, b + 1)
                self.arrive(self.RISE, b, src)
                self.add(self.own(0, b), src)
                self.rise_copy(b).start()

        @pl.when(p.z == p.batches - 1 - stage)
        def _():
            for b in range(p.batches - 1 - stage):
                src = self.cut(self.ru, b)
                self.arrive(self.FALL, b, src)
                self.add(self.own(0, b), src)
                self.fall_copy(b).start()

    def result(self):
        p = self.p
        up, down = self.cut(self.ru, p.z + 1), self.cut(self.ru, p.z)
        pl.when(p.z > 0)(lambda: self.arrive(self.RISE, p.z, up))
        pl.when(p.z < p.batches - 1)(lambda: self.arrive(self.FALL, p.z, down))

        @pl.when(p.z == 0)
        def _():
            up[...] = jnp.zeros(up.shape, BF)

        @pl.when(p.z == p.batches - 1)
        def _():
            down[...] = jnp.zeros(down.shape, BF)

        return self.own(0, p.z)[...].astype(F32) + up[...].astype(F32) + down[...].astype(F32)

    def sent(self, rel):
        p = self.p
        self.twin_copy(rel).wait_send()
        for b in range(p.batches):
            if rel == 3:
                self.far_copy(b).wait_send()
            elif rel == 1:
                self.side_copy(b).wait_send()
            elif rel == 2:
                self.deep_copy(b).wait_send()
            else:
                pl.when(p.z < b)(lambda b=b: self.rise_copy(b).wait_send())
                pl.when(p.z > b)(lambda b=b: self.fall_copy(b).wait_send())

    def act(self, word):
        if word == "c":
            self.gather_own()
        else:
            {"j": self.join, "r": self.relay, "k": self.chain}[word[0]](int(word[1]))


class LineScatter(Scatter):
    def rise(self, rel, b):
        return send(self.own(rel, b), self.cut(self.ru.at[rel], b + 1), self.line_s.at[self.n, 0, rel, b],
                    self.line_r.at[self.n, 0, rel, b], self.p.device(UP))

    def fall(self, rel, b):
        return send(self.own(rel, b), self.cut(self.ru.at[rel], b), self.line_s.at[self.n, 1, rel, b],
                    self.line_r.at[self.n, 1, rel, b], self.p.device(DOWN))

    def landed(self, way, rel, b):
        ref = self.cut(self.ru.at[rel], b + 1 - way)
        send(ref, ref, self.line_s.at[self.n, way, rel, b], self.line_r.at[self.n, way, rel, b],
             self.p.device(TWIN)).wait_recv()
        return ref

    def join(self, rel):
        p = self.p
        self.twin_copy(rel).wait_recv()
        add_into(self.part(rel, p.core), self.tr.at[rel], self.rows, self.step)

    def ends(self, up, down):
        p = self.p

        @pl.when(p.z == 0)
        def _():
            for rel in (3, 1, 2, 0):
                self.rise(rel, up).start()

        @pl.when(p.z == p.batches - 1)
        def _():
            for rel in (3, 1, 2, 0):
                self.fall(rel, down).start()

    def chain(self, stage):
        p = self.p

        @pl.when(p.z == stage)
        def _():
            for b in range(p.batches - 1, stage, -1):
                for rel in (3, 1, 2, 0):
                    self.add(self.own(rel, b), self.landed(0, rel, b))
                    self.rise(rel, b).start()

        @pl.when(p.z == p.batches - 1 - stage)
        def _():
            for b in range(p.batches - 1 - stage):
                for rel in (3, 1, 2, 0):
                    self.add(self.own(rel, b), self.landed(1, rel, b))
                    self.fall(rel, b).start()

    def settle(self, rel):
        p = self.p
        at = self.own(rel, p.z)
        pl.when(p.z > 0)(lambda: self.add(at, self.landed(0, rel, p.z)))
        pl.when(p.z < p.batches - 1)(lambda: self.add(at, self.landed(1, rel, p.z)))

    def cross(self, kind, rel, dst, way):
        return self.block_copy(kind, 0, self.own(rel, self.p.z), dst, way)

    def corner(self):
        self.settle(3)
        self.cross(self.FAR, 3, self.fx, ACROSS).start()
        self.settle(1)
        self.cross(self.SIDE, 1, self.rx, ACROSS).start()
        self.settle(2)

    def turn(self):
        self.arrive(self.FAR, 0, self.fx)
        self.add(self.own(2, self.p.z), self.fx)
        self.cross(self.DEEP, 2, self.ry, ALONG).start()
        self.settle(0)

    def result(self):
        self.arrive(self.SIDE, 0, self.rx)
        self.arrive(self.DEEP, 0, self.ry)
        return (self.own(0, self.p.z)[...].astype(F32) + self.rx[...].astype(F32) + self.ry[...].astype(F32))

    def sent(self):
        p = self.p
        for rel in range(4):
            self.twin_copy(rel).wait_send()
            for b in range(p.batches):
                pl.when(p.z < b)(lambda rel=rel, b=b: self.rise(rel, b).wait_send())
                pl.when(p.z > b)(lambda rel=rel, b=b: self.fall(rel, b).wait_send())
        self.cross(self.FAR, 3, self.fx, ACROSS).wait_send()
        self.cross(self.SIDE, 1, self.rx, ACROSS).wait_send()
        self.cross(self.DEEP, 2, self.ry, ALONG).wait_send()

    def act(self, word):
        if word[0] == "j":
            self.join(int(word[1]))
        elif word[0] == "k":
            self.chain(int(word[1]))
        elif word[0] == "z":
            self.ends(int(word[1]), int(word[2]))
        else:
            {"c": self.corner, "t": self.turn}[word]()


def rows_of_grid(s, grids, group, r0):
    side = s.sides[group]
    base = 0 if group == 0 else s.rows[0]
    first = (r0 - base) // 8
    cells = [grids[group][1 + (first + n) // side, 1 + lax.rem(first + n, side)] for n in range(10)]
    return jnp.concatenate(cells, axis=0)


def slope(v):
    gate = sigmoid(v)
    return gate * (1.0 + v * (1.0 - gate))


def backward_kernel(s, *refs):
    (gs1, gu1, gs2, gu2, taps1, taps2, xh1, xh2, xh3, xh4, z1, z3, dpre,
     r1, r2, r3, r4, last, norm, live_ref, inverse,
     dx, gso1, gso2, guo1, guo2, ng, square,
     ps, tr, fx, fa, rx1, ry1, rz1, rx2, ry2, rz2, pu, utr, ufx, urx, ury, urz, relay,
     nat, flip, d3, turn, planes, lines,
     load, tap_sem, tile_sem, halo_send, halo_recv, pass_send, pass_recv, line_s, line_r, twin_s, twin_r, block_s, block_r, half_s, half_r,
     pl_send, pl_recv, ln_send, ln_recv) = refs
    p = Place(s.batches, s.slots)
    live = [live_ref[g] for g in range(2)]
    inv = [inverse[g] for g in range(2)]
    totals = Totals(p, 4, planes, lines, (pl_send, pl_recv, ln_send, ln_recv))
    d, mid, m = s.d, s.mid, s.m
    bounds = (0, mid, mid + d, 2 * mid + d, 2 * mid + 2 * d)

    def gain_bias(n):
        return norm[0:1, bounds[n] : bounds[n + 1]], norm[1:2, bounds[n] : bounds[n + 1]]

    with scope("greet"):
        p.greet()
    def go(words):
        with scope("reduce " + words):
            for word in words.split():
                scatter(int(word[0])).act(word[1:])

    def cut_rows(ref, b):
        at = b * s.nb if isinstance(b, int) else pl.multiple_of(b * s.nb, 16)
        return ref.at[pl.ds(at, s.nb)]

    def cut_lanes(ref, b):
        at = b * s.uc if isinstance(b, int) else pl.multiple_of(b * s.uc, 128)
        return ref.at[:, pl.ds(at, s.uc)]

    def slot(n, rel):
        return 4 if n == 0 and rel == 0 else rel

    def part_s(n, rel, core):
        return ps.at[slot(n, rel), core]

    def part_u(rel, core):
        return pu.at[pl.ds(pl.multiple_of((p.rel[rel] * 2 + core) * s.ur, 16), s.ur)]

    sems = (twin_s, twin_r, block_s, block_r)

    def scatter(n):
        if n % 2 == 0:
            rx, ry, rz = (rx1, ry1, rz1) if n == 0 else (rx2, ry2, rz2)
            return Scatter(p, n, functools.partial(part_s, n), (tr, fx, fa, rx, ry, rz, None), cut_rows, s.nb, 48, sems)
        sc = LineScatter(p, n, part_u, (utr, ufx, None, urx, ury, urz, None), cut_lanes, s.ur, 144, sems)
        sc.line_s, sc.line_r = line_s, line_r
        return sc

    for side, edge in ((0, p.slots - 1), (2, 0)):
        @pl.when(p.t == edge)
        def _(side=side):
            d3[side] = jnp.zeros(d3.shape[1:], BF)

    def norm_back(n, total, scale, dh, xhat, store, size, width):
        gain, _ = gain_bias(n)
        ng[0:1, bounds[n] : bounds[n + 1]] = total[2:3, :] + total[3:4, :]
        ng[1:2, bounds[n] : bounds[n + 1]] = total[0:1, :] + total[1:2, :]
        lead = [gain * scale[g : g + 1, :] for g in range(2)]
        mean = [total[g : g + 1, :] * inv[g] for g in range(2)]
        cross = [total[2 + g : 3 + g, :] * inv[g] for g in range(2)]

        def rows(group, r0, c):
            at = pl.ds(r0, size)
            v = lead[group] * (dh[at, :] - mean[group] - xhat[at, :] * cross[group])
            v = v.reshape(size // 8, 8, width) * live[group][None]
            store(at, v.reshape(size, width))
            return c

        chunks(s, size, rows)

    def upstream(n, dz, xhat, fetch, size, width):
        gain, bias = gain_bias(n)

        def body(group, r0, c):
            at = pl.ds(r0, size)
            xv = xhat[at, :]
            v = fetch(group, r0) * slope(xv * gain + bias)
            dz[at, :] = v
            return (c[0] + jnp.sum(v.reshape(size // 8, 8, width), axis=0),
                    c[1] + jnp.sum((v * xv).reshape(size // 8, 8, width), axis=0))

        zero = jnp.zeros((8, width), F32)
        small, large = chunks(s, size, body, (zero, zero))
        rows = [jnp.sum(v * live[g], axis=0, keepdims=True) for v, g in
                ((small[0], 0), (large[0], 1), (small[1], 0), (large[1], 1))]
        return jnp.concatenate(rows, axis=0)

    def transpose():
        def body(j, _):
            at = pl.ds(pl.multiple_of(j * 128, 128), 128)
            flip[at, :] = nat[:, at].T
            return 0

        with scope("transpose"):
            lax.fori_loop(0, mid // 128, body, 0)

    def fetch_into(src, dst, sem):
        c = pltpu.make_async_copy(src, dst, load.at[sem])
        c.start()
        return c

    def narrow_store(at, v):
        d3[1, at, :] = v.astype(BF)

    def nat_store(at, v):
        nat[at, :] = v.astype(BF)

    def first(up, xh):
        c1, c2 = fetch_into(dpre, up, 0), fetch_into(xh4, xh, 1)
        c1.wait()
        c2.wait()
        norm_back(3, last[...], r4[...], up, xh, narrow_store, 80, d)

    fetch_into(z3, nat, 2)
    with scope("norm4 back"):
        pl.run_scoped(first, pltpu.VMEM((m, d), F32), pltpu.VMEM((m, d), F32))
    zero_padding(s, d3.at[1], d)

    def temporal(stage, index, n, whole, zs, xhs, scale, words, finish):
        halo = Halo(p, stage, lambda side: d3.at[1], lambda side: d3.at[2 - 2 * side], relay,
                    (halo_send, halo_recv, pass_send, pass_recv), s.cut)

        def run(dz, xh, wu):
            halo.start(0)
            halo.start(1)
            cz = pltpu.make_async_copy(zs, nat, load.at[2])
            if stage:
                cz.start()
            cw = fetch_into(whole, wu, 3)
            cx = fetch_into(xhs, xh, 4)
            cz.wait()
            transpose()
            cw.wait()

            def field_grad(k):
                for lo, width in wide_cuts(mid):
                    y = lax.dot_general(d3[k], wu[k * mid + lo : k * mid + lo + width, :], NT_DIMS,
                                        preferred_element_type=F32)
                    if k == 1:
                        dz[:, lo : lo + width] = y
                    else:
                        dz[:, lo : lo + width] += y

            def weight_grad(k):
                with scope("u weight grad"):
                    pu[k * mid : (k + 1) * mid, :] = jnp.dot(
                        flip[...], d3[k], preferred_element_type=F32
                    ).astype(BF)

            with scope("u grads"):
                field_grad(1)
            with scope("relay"):
                halo.relay()
            go(words[0])
            with scope("halo wait"):
                halo.wait(1)
            with scope("u grads"):
                field_grad(0)
            with scope("halo wait"):
                halo.wait(0)
            go(words[2])
            with scope("u grads"):
                field_grad(2)
            cx.wait()

            def fetch(group, r0):
                return dz[pl.ds(r0, 16), :]

            with scope("upstream"):
                local_sums = upstream(n, dz, xh, fetch, 16, mid)
            extra = finish()
            with scope("total"):
                total = totals.run(2 * stage, local_sums, lambda: weight_grad(1),
                                   lambda: (weight_grad(0), weight_grad(2)) and None)
            sc = scatter(index)
            for rel in (3, 1, 2, 0):
                sc.twin(rel)
            with scope("norm back"):
                norm_back(n, total, scale, dz, xh, nat_store, 16, mid)
            go(words[1])
            return extra

        extra = pl.run_scoped(run, pltpu.VMEM((m, mid), F32), pltpu.VMEM((m, mid), F32), pltpu.VMEM((3 * mid, d), BF))
        zero_padding(s, nat, mid)
        halo.done()
        return extra

    def finish_u(n, ref):
        sc = scatter(n)
        g = sc.result()
        ref[...] = g
        sc.sent()
        return jnp.sum(g * g, axis=0, keepdims=True)

    def finish_s(n, out):
        sc = scatter(n)
        g = sc.result()
        turn[...] = g.T
        rows = s.kw // 2

        def half(core):
            return turn.at[pl.ds(pl.multiple_of(core * rows, 16), rows)]

        keep = pltpu.make_async_copy(half(p.core), out.at[p.core], load.at[8])
        keep.start()
        copy = send(half(1 - p.core), out.at[p.core], half_s.at[n // 2], half_r.at[n // 2], p.device(TWIN))
        copy.start()
        send(half(p.core), out.at[1 - p.core], half_s.at[n // 2], half_r.at[n // 2], p.device(TWIN)).wait_recv()
        copy.wait_send()
        keep.wait()
        return jnp.sum(jnp.sum((g * g).reshape(s.nb, s.kw // 128, 128), axis=0), axis=0, keepdims=True)

    pieces = []
    for tap in range(9):
        lo, end, found = tap * d, (tap + 1) * d, []
        while lo < end:
            hi = min(end, (lo // s.kw + 1) * s.kw)
            found.append((lo // s.kw, lo % s.kw, lo - tap * d, hi - lo))
            lo = hi
        pieces.append(found)

    def spatial(index, whole, taps, grids, tap_buf, tile, words, tap_words, early, ready):
        rels = (3, 1, 2, 0)

        def tap_load(i):
            return pltpu.make_async_copy(taps.at[p.rel[rels[i]]], tap_buf.at[i % 2], tap_sem.at[i])

        def tile_loads(tap):
            return [
                pltpu.make_async_copy(
                    whole.at[slab, :, pl.ds(lane, width)], tile.at[tap % 2, :, pl.ds(at, width)],
                    tile_sem.at[tap, n],
                )
                for n, (slab, lane, at, width) in enumerate(pieces[tap])
            ]

        tap_load(0).start()
        tap_load(1).start()
        for c in tile_loads(0):
            c.start()
        go(early)
        transpose()
        for grid in grids:
            def clear(i, _, grid=grid):
                grid[i] = jnp.zeros(grid.shape[1:], F32)
                return 0

            lax.fori_loop(0, grid.shape[0], clear, 0)
        sc = scatter(index)
        for i, rel in enumerate(rels):
            tap_load(i).wait()
            ready(rel)
            with scope("dw slab"):
                for lo, width in wide_cuts(s.kw):
                    y = jnp.dot(flip[...], tap_buf[i % 2, :, lo : lo + width], preferred_element_type=F32).astype(BF)
                    for n in range(2 * s.batches):
                        b, core = n // 2, n % 2
                        ps[slot(index, rel), core, b * s.nb : (b + 1) * s.nb, lo : lo + width] = y[n * s.nb : (n + 1) * s.nb]
            sc.twin(rel)
            if i + 2 < 4:
                tap_load(i + 2).start()
            go(words[i])
        for tap in range(9):
            if tap + 1 < 9:
                for c in tile_loads(tap + 1):
                    c.start()
            for c in tile_loads(tap):
                c.wait()
            i, j = tap // 3, tap % 3
            with scope("dx tap"):
                y = jnp.dot(nat[...], tile[tap % 2], preferred_element_type=F32)
                base = 0
                for group in range(2):
                    side = s.sides[group]
                    part = y[base : base + s.cells[group] * 8].reshape(side, side, 8, d)
                    grids[group][i : i + side, j : j + side] += part
                    base += s.rows[group]
            go(tap_words[tap])
        clear_pad_cells(s, grids)

    grid_types = (
        pltpu.VMEM((s.sides[0] + 2, s.sides[0] + 2, 8, d), F32),
        pltpu.VMEM((s.sides[1] + 2, s.sides[1] + 2, 8, d), F32),
    )
    load_types = (pltpu.VMEM((2, m, s.kw), BF), pltpu.VMEM((2, mid, d), BF))
    narrow_types = (pltpu.VMEM((m, d), F32), pltpu.VMEM((m, d), F32))

    nothing = jnp.zeros((1, 128), F32)
    temporal(0, 3, 2, gu2, z3, xh3, r3[...], ("", "3j3 3j1 3j2 3j0", ""), lambda: nothing)

    def second(*grids):
        pl.run_scoped(
            lambda tap_buf, tile: spatial(
                2, gs2, taps2, grids, tap_buf, tile, ("", "2j3", "2j1 3k1", "2j2"),
                ("2j0", "", "", "", "3k2", "", "", "", ""), "3z30 3z21 3z12", lambda rel: None),
            *load_types,
        )

        def rest(b, xh):
            fetch_into(xh2, xh, 5).wait()

            def fetch(group, r0):
                return rows_of_grid(s, grids, group, r0)

            with scope("upstream"):
                local_sums = upstream(1, b, xh, fetch, 80, d)
            with scope("total"):
                total = totals.run(1, local_sums)
            with scope("norm back"):
                norm_back(1, total, r2[...], b, xh, narrow_store, 80, d)

        pl.run_scoped(rest, *narrow_types)

    pl.run_scoped(second, *grid_types)
    zero_padding(s, d3.at[1], d)

    def finish_small():
        with scope("finish u"):
            return finish_u(3, guo2)

    sums = temporal(1, 1, 0, gu1, z1, xh1, r1[...],
                    ("3c 2r0 2r1 2r3 2r2", "2c 1j3 1j1 1j2 1j0 1z30 1z21 1z12", "3t"), finish_small)

    def final(*grids):
        def ready(rel):
            if rel:
                scatter(2).sent(rel)

        pl.run_scoped(
            lambda tap_buf, tile: spatial(
                0, gs1, taps1, grids, tap_buf, tile, ("", "0j3 2k1", "0j1", "0j2 2k2"),
                ("0j0", "", "0r0 0r3", "0r1 0r2", "1k1", "", "", "", "1k2"), "", ready),
            *load_types,
        )
        with scope("finish s"):
            sums = finish_s(2, gso2)
        scatter(2).sent(0)

        def rest(b, up):
            fetch_into(dpre, up, 6).wait()

            def rows(group, r0, c):
                b[pl.ds(r0, 80), :] = rows_of_grid(s, grids, group, r0) + up[pl.ds(r0, 80), :]
                return c

            with scope("dx"):
                chunks(s, 80, rows)
            cd = fetch_into(b, dx, 7)
            go("1c 0c")
            go("1t 0k1")
            go("0k2")
            with scope("finish u"):
                part = finish_u(1, guo1)
            with scope("finish s"):
                part = part + finish_s(0, gso1)
            cd.wait()
            for rel in range(4):
                scatter(0).sent(rel)
            return part

        return sums + pl.run_scoped(rest, *narrow_types)

    sums = sums + pl.run_scoped(final, *grid_types)
    with scope("total"):
        square[...] = totals.run(3, jnp.broadcast_to(sums, (4, 128)))


def backward_call(s, saved, norm, live, inverse):
    any_, vmem, smem = (pl.BlockSpec(memory_space=m) for m in (pl.ANY, pltpu.VMEM, pltpu.SMEM))
    S, V, dma = jax.ShapeDtypeStruct, pltpu.VMEM, pltpu.SemaphoreType.DMA
    m, d, mid, nb, kw = s.m, s.d, s.mid, s.batches, s.kw
    half = nb // 2
    outs = (S((m, d), F32), S((2, kw // 2, s.nb), F32), S((2, kw // 2, s.nb), F32),
            S((s.ur, s.uc), F32), S((s.ur, s.uc), F32), S((2, 2 * (mid + d)), F32), S((4, 128), F32))
    rows = nb * s.nb
    scratch = [
        V((5, 2, rows, kw), BF), V((4, rows, kw), BF), V((half * s.nb, kw), BF), V((half * s.nb, kw), BF),
        V((rows, kw), BF), V((rows, kw), BF), V((rows + s.nb, kw), BF),
        V((rows, kw), BF), V((rows, kw), BF), V((rows + s.nb, kw), BF),
        V((3 * mid, d), BF), V((4, s.ur, d), BF), V((s.ur, s.uc), BF), V((s.ur, s.uc), BF), V((s.ur, s.uc), BF),
        V((4, s.ur, d + s.uc), BF), V((m - s.cut, d), BF),
        V((m, mid), BF), V((mid, m), BF), V((3, m, d), BF), V((kw, s.nb), F32),
        V((4, s.slots, 4, mid), F32), V((4, nb, 4, mid), F32),
        dma((9,)), dma((4,)), dma((9, 3)), dma((2, 2, 2)), dma((2, 2, 2)), dma((2,)), dma((2,)),
        dma((4, 2, 4, nb)), dma((4, 2, 4, nb)),
        dma((4, 4)), dma((4, 4)), dma((4, 5, nb)), dma((4, 5, nb)), dma((2,)), dma((2,)),
        dma((4, s.slots)), dma((4, s.slots)), dma((4, nb)), dma((4, nb)),
    ]
    return pl.pallas_call(
        functools.partial(backward_kernel, s),
        out_shape=outs,
        in_specs=[any_] * 13 + [vmem] * 7 + [smem],
        out_specs=(any_,) * 3 + (vmem,) * 4,
        scratch_shapes=scratch,
        compiler_params=pltpu.CompilerParams(
            collective_id=1, has_side_effects=True, vmem_limit_bytes=63 * 2**20
        ),
        name="backward",
    )(*saved, norm, live, inverse)


def body(batches, slots, *args):
    x_small, x_large = args[0], args[1]
    if not fits(x_small.shape, x_large.shape, batches, slots):
        return plain_body(*args)
    return fast_body(Shape(x_small.shape, x_large.shape, batches, slots), *args)


def fast_body(
    s,
    x_small,
    x_large,
    grad_small,
    grad_large,
    clip_counts,
    first_spatial,
    first_temporal,
    second_spatial,
    second_temporal,
    norm_params,
    first_spatial_momentum,
    first_temporal_momentum,
    second_spatial_momentum,
    second_temporal_momentum,
    norm_momentum,
    first_spatial_variance,
    first_temporal_variance,
    second_spatial_variance,
    second_temporal_variance,
    norm_variance,
):
    z = lax.axis_index("batch")
    slots = jnp.arange(s.clips, dtype=jnp.int32)
    counts = lax.dynamic_index_in_dim(clip_counts, z, 1, keepdims=False)
    live = (slots[None, :] < counts[:, None]).astype(F32)[:, :, None]
    totals = jnp.sum(clip_counts, axis=1).astype(F32) * (s.slots * jnp.array(s.cells, F32))
    inverse = 1.0 / totals
    x = cell_major(s, x_small, x_large)
    grad = cell_major(s, grad_small, grad_large)
    res = forward_call(
        s, x, grad, halves(s, first_spatial), first_temporal.astype(BF), halves(s, second_spatial),
        second_temporal.astype(BF), norm_params, live, inverse,
    )
    out_small, out_large = clip_major(s, res[12])
    saved = res[:12] + res[13:]
    dx, gs1, gs2, gu1, gu2, grad_params, square = backward_call(s, saved, norm_params, live, inverse)
    in_small, in_large = clip_major(s, dx)

    def whole(g):
        return g.transpose(1, 0, 2).reshape(g.shape[1], 2 * g.shape[2])

    grad_norm = jnp.sqrt(jnp.sum(square[0]) + jnp.sum(grad_params * grad_params))
    factor = THRESHOLD / jnp.maximum(grad_norm, THRESHOLD)
    one = adamw(first_spatial, whole(gs1), first_spatial_momentum, first_spatial_variance, factor,
                WEIGHT_RATE, WEIGHT_DECAY)
    two = adamw(first_temporal, gu1, first_temporal_momentum, first_temporal_variance, factor,
                WEIGHT_RATE, WEIGHT_DECAY)
    three = adamw(second_spatial, whole(gs2), second_spatial_momentum, second_spatial_variance, factor,
                  WEIGHT_RATE, WEIGHT_DECAY)
    four = adamw(second_temporal, gu2, second_temporal_momentum, second_temporal_variance, factor,
                 WEIGHT_RATE, WEIGHT_DECAY)
    norms = adamw(norm_params, grad_params, norm_momentum, norm_variance, factor, NORM_RATE, 0.0)
    return (out_small, out_large, in_small, in_large, grad_norm) + one + two + three + four + norms


def solution(mesh):
    return jax.shard_map(
        functools.partial(body, mesh.shape["batch"], mesh.shape["tm"]),
        mesh=mesh,
        in_specs=(
            P("batch", "tm", None, None),
            P("batch", "tm", None, None),
            P("batch", "tm", None, None),
            P("batch", "tm", None, None),
            P(),
            P("tm", "batch"),
            P("tm", "batch"),
            P("tm", "batch"),
            P("tm", "batch"),
            P(),
            P("tm", "batch"),
            P("tm", "batch"),
            P("tm", "batch"),
            P("tm", "batch"),
            P(),
            P("tm", "batch"),
            P("tm", "batch"),
            P("tm", "batch"),
            P("tm", "batch"),
            P(),
        ),
        out_specs=(
            P("batch", "tm", None, None),
            P("batch", "tm", None, None),
            P("batch", "tm", None, None),
            P("batch", "tm", None, None),
            P(),
            P("tm", "batch"),
            P("tm", "batch"),
            P("tm", "batch"),
            P("tm", "batch"),
            P("tm", "batch"),
            P("tm", "batch"),
            P("tm", "batch"),
            P("tm", "batch"),
            P("tm", "batch"),
            P("tm", "batch"),
            P("tm", "batch"),
            P("tm", "batch"),
            P(),
            P(),
            P(),
        ),
        check_vma=False,
    )
```
